32 devices in a mesh: seq: 8 (over z, x), chan: 4 (over y, core).
Axes of the slice: x: 2, y: 2, z: 4, core: 2. Of those that a mesh axis runs over, the one named last changes fastest.
Arguments:
- block_input: bfloat16 [8, 1024, 1024], P(None, 'seq', 'chan'), may hold values from -6 to 6
- lengths: int32 [8], replicated, may hold values from 128 to 1024, as said below
- norm1_gain: float32 [1024], P('chan'), may hold values from 0.25 to 1.75
- norm1_bias: float32 [1024], P('chan'), may hold values from -3 to 3
- a_decay: float32 [64, 1024], P(None, 'chan'), may hold values from 0.01953125 to 1
- a_freq: float32 [64, 1024], P(None, 'chan'), may hold values from 0 to 10
- b_state: float32 [2, 64, 1024], P(None, None, 'chan'), may hold values from -6 to 6
- c_state: float32 [2, 64, 1024], P(None, None, 'chan'), may hold values from -0.24 to 0.24
- step_size: float32 [1024], P('chan'), may hold values from 0.01 to 0.1
- skip_gain: float32 [1024], P('chan'), may hold values from -4 to 4
- w_value: bfloat16 [1024, 1024], P(None, 'chan'), may hold values from -0.1875 to 0.1875
- b_value: float32 [1024], P('chan'), may hold values from -3 to 3
- w_gate: bfloat16 [1024, 1024], P(None, 'chan'), may hold values from -0.1875 to 0.1875
- b_gate: float32 [1024], P('chan'), may hold values from -3 to 3
- norm2_gain: float32 [1024], P('chan'), may hold values from 0.25 to 1.75
- norm2_bias: float32 [1024], P('chan'), may hold values from -3 to 3
- w_up: bfloat16 [1024, 4096], P(None, 'chan'), may hold values from -0.1875 to 0.1875
- b_up: float32 [4096], P('chan'), may hold values from -3 to 3
- w_down: bfloat16 [4096, 1024], P('chan'), may hold values from -0.1875 to 0.1875
- b_down: float32 [1024], P('chan'), may hold values from -3 to 3
- out_grad: bfloat16 [8, 1024, 1024], P(None, 'seq', 'chan'), may hold values from -6 to 6
Outputs:
- output: bfloat16 [8, 1024, 1024], P(None, 'seq', 'chan')
- grad_input: float32 [8, 1024, 1024], P(None, 'seq', 'chan')
- grad_norm1_gain: float32 [1024], P('chan')
- grad_norm1_bias: float32 [1024], P('chan')
- grad_a_decay: float32 [64, 1024], P(None, 'chan')
- grad_a_freq: float32 [64, 1024], P(None, 'chan')
- grad_b_state: float32 [2, 64, 1024], P(None, None, 'chan')
- grad_c_state: float32 [2, 64, 1024], P(None, None, 'chan')
- grad_step_size: float32 [1024], P('chan')
- grad_skip_gain: float32 [1024], P('chan')
- grad_w_value: float32 [1024, 1024], P(None, 'chan')
- grad_b_value: float32 [1024], P('chan')
- grad_w_gate: float32 [1024, 1024], P(None, 'chan')
- grad_b_gate: float32 [1024], P('chan')
- grad_norm2_gain: float32 [1024], P('chan')
- grad_norm2_bias: float32 [1024], P('chan')
- grad_w_up: float32 [1024, 4096], P(None, 'chan')
- grad_b_up: float32 [4096], P('chan')
- grad_w_down: float32 [4096, 1024], P('chan')
- grad_b_down: float32 [1024], P('chan')
The draws below stay inside these ranges and needn't reach their ends.
Inputs may be any that keep to these rules, and one draw needn't show every extreme that they name: One sequence, chosen by the seed, has length 1024; lengths have a heavy tail toward 128.
All inputs are finite; a program needn't handle non-finite values.
Results may differ from the reference program's by a relative error of at most 0.008.
Values may be sent and summed in bfloat16 or wider, within the bound.
No kernel may reach another device: no remote copies, remote signals or barrier semaphores. Data moves between devices by JAX's collectives and lax.ppermute only.
A program may use at most 512 MiB of HBM per device.

```python
import math
import jax
import jax.numpy as jnp
from jax import lax

D = 1024
STATE = 64
FF = 4096
SEQS = 8
BLK = 128
LENGTH = 1024
SHORTEST = 128


def draw_lengths(key, part):
    key = jax.random.fold_in(key, 7)
    first_key, second_key = jax.random.split(key)
    levels = jax.random.randint(first_key, (SEQS,), 0, 33)
    extras = (LENGTH - SHORTEST) * (levels * levels * levels) // 32768
    chosen = jax.random.randint(second_key, (), 0, SEQS)
    ragged = SHORTEST + extras
    return jnp.where(jnp.arange(SEQS) == chosen, LENGTH, ragged).astype(jnp.int32)


def block_levels(rng, dims, cuts, low, top_value):
    level = 1.0
    for dim, shards_of in cuts:
        heights = jax.random.uniform(jax.random.fold_in(jax.random.fold_in(rng, 6), dim), (shards_of,), jnp.float32, low / len(cuts), top_value / len(cuts))
        level = level * jnp.repeat(jnp.exp(heights), dims[dim] // shards_of).reshape((-1,) + (1,) * (len(dims) - 1 - dim))
    return level


def bell_draw(stream_key, shape, scale, most, pieces=(), kind=jnp.bfloat16):
    entries = jax.random.normal(stream_key, shape, jnp.float32) * scale
    if len(pieces) > 0:
        entries = block_levels(stream_key, shape, pieces, -0.22, 0.18) * entries
    return jnp.clip(entries, min=-most, max=most).astype(kind)


def setup_inputs(seed: int = 0) -> dict:
    key_of = jax.random.split(jax.random.key(seed), 22)
    return {
        "block_input": bell_draw(key_of[0], (SEQS, LENGTH, D), 1.0, 6.0, ((1, 8), (2, 4))),
        "lengths": draw_lengths(jax.random.fold_in(key_of[21], 71), 0),
        "norm1_gain": jnp.clip(1.0 + 0.15 * jax.random.normal(key_of[2], (D,), jnp.float32), 0.25, 1.75),
        "norm1_bias": bell_draw(key_of[3], (D,), 0.5, 3.0, ((0, 4),), jnp.float32),
        "a_decay": jnp.clip(jnp.exp(math.log(1.0) - 3.9357395 * jax.random.uniform(key_of[4], (STATE, D), jnp.float32) ** block_levels(key_of[4], (STATE, D), ((1, 4),), -0.2, 0.2)), 0.01953125, 1.0),
        "a_freq": jnp.clip(10.0 * jax.random.uniform(key_of[5], (STATE, D), jnp.float32) ** block_levels(key_of[5], (STATE, D), ((1, 4),), -0.2, 0.2), 0.0, 10.0),
        "b_state": bell_draw(key_of[6], (2, STATE, D), 1.0, 6.0, ((2, 4),), jnp.float32),
        "c_state": bell_draw(key_of[7], (2, STATE, D), 0.04, 0.24, ((2, 4),), jnp.float32),
        "step_size": jnp.clip(jnp.exp(math.log(0.1) - 2.3025851 * jax.random.uniform(key_of[8], (D,), jnp.float32) ** block_levels(key_of[8], (D,), ((0, 4),), -0.2, 0.2)), 0.01, 0.1),
        "skip_gain": bell_draw(key_of[9], (D,), 1.0, 4.0, ((0, 4),), jnp.float32),
        "w_value": bell_draw(key_of[10], (D, D), D ** -0.5, 0.1875, ((1, 4),)),
        "b_value": bell_draw(key_of[11], (D,), 0.5, 3.0, ((0, 4),), jnp.float32),
        "w_gate": bell_draw(key_of[12], (D, D), D ** -0.5, 0.1875, ((1, 4),)),
        "b_gate": bell_draw(key_of[13], (D,), 0.5, 3.0, ((0, 4),), jnp.float32),
        "norm2_gain": jnp.clip(1.0 + 0.15 * jax.random.normal(key_of[14], (D,), jnp.float32), 0.25, 1.75),
        "norm2_bias": bell_draw(key_of[15], (D,), 0.5, 3.0, ((0, 4),), jnp.float32),
        "w_up": bell_draw(key_of[16], (D, FF), D ** -0.5, 0.1875, ((1, 4),)),
        "b_up": bell_draw(key_of[17], (FF,), 0.5, 3.0, ((0, 4),), jnp.float32),
        "w_down": bell_draw(key_of[18], (FF, D), (FF // 4) ** -0.5, 0.1875, ((0, 4),)),
        "b_down": bell_draw(key_of[19], (D,), 0.5, 3.0, ((0, 4),), jnp.float32),
        "out_grad": bell_draw(key_of[20], (SEQS, LENGTH, D), 1.0, 6.0, ((1, 8), (2, 4))),
    }


EPSILON = 1e-05

@jax.custom_vjp
def low(v):
    return lax.optimization_barrier(v.astype(jnp.bfloat16)).astype(jnp.float32)

@jax.custom_vjp
def low_back(v):
    return v

def low_keep(v):
    return (low(v), None)

def low_pass(kept, grad):
    return (grad,)

def back_keep(v):
    return (v, None)

def back_low(kept, grad):
    return (low(grad),)
low.defvjp(low_keep, low_pass)
low_back.defvjp(back_keep, back_low)

def s4_tables(decay, freq, b_state, c_state, step_size, length):
    rate = step_size * decay
    turn = step_size * freq
    half_turn = jnp.sin(0.5 * turn)
    less_re = jnp.expm1(-rate) * jnp.cos(turn) - 2.0 * half_turn * half_turn
    less_im = jnp.exp(-rate) * jnp.sin(turn)
    modulus = decay * decay + freq * freq
    ratio_re = (freq * less_im - decay * less_re) / modulus
    ratio_im = -(decay * less_im + freq * less_re) / modulus
    input_re = ratio_re * b_state[0] - ratio_im * b_state[1]
    input_im = ratio_re * b_state[1] + ratio_im * b_state[0]
    counts = jnp.arange(length + 1, dtype=jnp.float32)[:, None, None]
    damping = jnp.exp(-rate * counts)
    power_re = damping * jnp.cos(turn * counts)
    power_im = damping * jnp.sin(turn * counts)
    return (input_re, input_im, power_re, power_im, c_state[0], c_state[1])

def s4_out(signal, state_re, state_im, tables, skip_gain):
    input_re, input_im, power_re, power_im, out_re, out_im = tables
    length = signal.shape[1]
    weight_re = out_re * input_re - out_im * input_im
    weight_im = out_re * input_im + out_im * input_re
    kernel = 2.0 * lax.optimization_barrier(jnp.sum(weight_re * power_re[:length] - weight_im * power_im[:length], axis=1))
    places = jnp.arange(length, dtype=jnp.int32)
    lags = places[:, None] - places[None, :]
    toeplitz = jnp.where((lags >= 0)[:, :, None], kernel[jnp.maximum(lags, 0)], 0.0)
    local = jnp.einsum('tsh,bsh->bth', toeplitz, signal, precision=lax.Precision.HIGHEST)
    read_re = out_re * power_re[1:] - out_im * power_im[1:]
    read_im = out_re * power_im[1:] + out_im * power_re[1:]
    carried = jnp.einsum('tnh,bnh->bth', read_re, state_re, precision=lax.Precision.HIGHEST)
    carried = carried - jnp.einsum('tnh,bnh->bth', read_im, state_im, precision=lax.Precision.HIGHEST)
    return local + 2.0 * carried + skip_gain * signal

def s4_end(signal, tables):
    input_re, input_im, power_re, power_im, out_re, out_im = tables
    length = signal.shape[1]
    flip_re = power_re[:length][::-1]
    flip_im = power_im[:length][::-1]
    write_re = input_re * flip_re - input_im * flip_im
    write_im = input_re * flip_im + input_im * flip_re
    end_re = jnp.einsum('snh,bsh->bnh', write_re, signal, precision=lax.Precision.HIGHEST)
    end_im = jnp.einsum('snh,bsh->bnh', write_im, signal, precision=lax.Precision.HIGHEST)
    return (end_re, end_im, power_re[length], power_im[length])

def s4_block(signal, state_re, state_im, decay, freq, b_state, c_state, step_size, skip_gain):
    tables = s4_tables(decay, freq, b_state, c_state, step_size, signal.shape[1])
    end_re, end_im, carry_re, carry_im = s4_end(signal, tables)
    return (s4_out(signal, state_re, state_im, tables, skip_gain), end_re, end_im, carry_re, carry_im)

def mixer(signal, decay, freq, b_state, c_state, step_size, skip_gain):
    batch, total, width = signal.shape
    blocks = total // BLK
    stacked = signal.reshape(batch, blocks, BLK, width).transpose(1, 0, 2, 3)

    def advance_raw(carry, block):
        state_re, state_im = carry
        result, end_re, end_im, carry_re, carry_im = s4_block(block, state_re, state_im, decay, freq, b_state, c_state, step_size, skip_gain)
        new_re = carry_re * state_re - carry_im * state_im + end_re
        new_im = carry_re * state_im + carry_im * state_re + end_im
        return ((new_re, new_im), result)
    advance = jax.checkpoint(advance_raw)
    zeros = jnp.zeros((batch, decay.shape[0], width), jnp.float32)
    _, results = lax.scan(advance, (zeros, zeros), stacked)
    return results.transpose(1, 0, 2, 3).reshape(batch, total, width)

def layer_norm(values, gain, bias):
    center = lax.optimization_barrier(jnp.mean(values, axis=-1, keepdims=True))
    spread_var = lax.optimization_barrier(jnp.mean(values * values, axis=-1, keepdims=True)) - center * center
    return (values - center) * lax.rsqrt(spread_var + EPSILON) * gain + bias

def dense(acts, weight):
    return jnp.einsum('bld,de->ble', acts, weight, precision=lax.Precision.HIGHEST)

def reference(block_input, lengths, norm1_gain, norm1_bias, a_decay, a_freq, b_state, c_state, step_size, skip_gain, w_value, b_value, w_gate, b_gate, norm2_gain, norm2_bias, w_up, b_up, w_down, b_down, out_grad):
    places = jnp.arange(LENGTH, dtype=jnp.int32)
    mask = (places[None, :] < lengths[:, None].astype(jnp.int32)).astype(jnp.float32)[..., None]

    def forward(inputs, gain_one, bias_one, decay, freq, b_part, c_part, step_inner, skip_inner, weight_value, bias_value, weight_gate, bias_gate, gain_two, bias_two, weight_up, bias_up, weight_down, bias_down):
        signal = low(mask * layer_norm(inputs, gain_one, bias_one))
        mixed = low_back(mixer(signal, decay, freq, b_part, c_part, step_inner, skip_inner))
        activ = low(jax.nn.gelu(mixed))
        value = low_back(dense(activ, weight_value) + bias_value)
        gate = low_back(dense(activ, weight_gate) + bias_gate)
        resid = inputs + value * jax.nn.sigmoid(gate)
        normed = low(layer_norm(resid, gain_two, bias_two))
        hidden = low_back(dense(normed, weight_up) + bias_up)
        spread = low(jax.nn.gelu(hidden))
        return resid + dense(spread, weight_down) + bias_down
    floats = (block_input.astype(jnp.float32), norm1_gain.astype(jnp.float32), norm1_bias.astype(jnp.float32), a_decay.astype(jnp.float32), a_freq.astype(jnp.float32), b_state.astype(jnp.float32), c_state.astype(jnp.float32), step_size.astype(jnp.float32), skip_gain.astype(jnp.float32), w_value.astype(jnp.float32), b_value.astype(jnp.float32), w_gate.astype(jnp.float32), b_gate.astype(jnp.float32), norm2_gain.astype(jnp.float32), norm2_bias.astype(jnp.float32), w_up.astype(jnp.float32), b_up.astype(jnp.float32), w_down.astype(jnp.float32), b_down.astype(jnp.float32))
    result, pull = jax.vjp(forward, *floats)
    grads = pull(out_grad.astype(jnp.float32))
    return (result.astype(jnp.bfloat16), grads[0], grads[1], grads[2], grads[3], grads[4], grads[5], grads[6], grads[7], grads[8], grads[9], grads[10], grads[11], grads[12], grads[13], grads[14], grads[15], grads[16], grads[17], grads[18])
```

```python
import jax
import jax.numpy as jnp
from jax import lax
from jax.experimental import pallas as pl
from jax.experimental.pallas import tpu as pltpu
from jax.sharding import PartitionSpec as P

EPSILON = 1e-05
LOW = jnp.bfloat16
FULL = jnp.float32
CHANNELS = 32
UNROLL = 16
SCALE = 1.0e5
VMEM = 56 * 1024 * 1024


def swap(x, axis, distance):
    return lax.ppermute(x, axis, [(i, i ^ distance) for i in range(lax.axis_size(axis))])


def axis_bits(axis):
    size = lax.axis_size(axis)
    bits = size.bit_length() - 1
    assert size == 1 << bits
    return bits


def gather_pieces(x):
    pieces = {0: x}
    for bit in reversed(range(axis_bits("chan"))):
        for d in list(pieces):
            pieces[d ^ (1 << bit)] = swap(pieces[d], "chan", 1 << bit)
    return [pieces[d] for d in range(len(pieces))]


def reduce_pieces(parts, marks=None):
    sums = dict(enumerate(parts))
    for bit in range(axis_bits("chan")):
        if marks is not None and bit == axis_bits("chan") - 1:
            marks.append(sums[1 << bit])
        for d in sorted(sums, reverse=True):
            if d >> bit & 1:
                sums[d ^ (1 << bit)] = sums[d ^ (1 << bit)] + swap(
                    sums.pop(d).astype(LOW), "chan", 1 << bit
                ).astype(FULL)
    return sums[0]


def sum_chan(x):
    return x + sum(swap(x, "chan", d) for d in range(1, lax.axis_size("chan")))


def after(x, *others):
    return lax.optimization_barrier((x, others))[0]


def exchange_all(x):
    return lax.all_to_all(x, "seq", 0, 0, tiled=True)


def split_sum(parts, place, count):
    rows, columns = min(part.shape[0] for part, _ in parts), parts[0][0].shape[1]
    block = (rows // count, columns)
    scalars = jnp.stack([place] + [first for _, first in parts]).astype(jnp.int32)

    def kernel(scalars, *refs):
        del scalars
        ins, outs = refs[:-count], refs[-count:]
        total = sum(ref[...].astype(FULL) for ref in ins).astype(LOW)
        for e, out in enumerate(outs):

            @pl.when(pl.program_id(0) == e)
            def _(out=out):
                out[...] = total

    return pl.pallas_call(
        kernel,
        grid_spec=pltpu.PrefetchScalarGridSpec(
            num_scalar_prefetch=1,
            grid=(count,),
            in_specs=[
                pl.BlockSpec(block, lambda e, n, i=i: (n[i + 1] + (n[0] ^ e), 0)) for i in range(len(parts))
            ],
            out_specs=[pl.BlockSpec(block, lambda e, n: (0, 0))] * count,
        ),
        out_shape=[jax.ShapeDtypeStruct(block, LOW)] * count,
        compiler_params=pltpu.CompilerParams(vmem_limit_bytes=VMEM),
        cost_estimate=cost(2),
        name="split_sum",
    )(scalars, *[part for part, _ in parts])


def join(parts):
    rows, columns = parts[0].shape
    count = len(parts)

    def kernel(*refs):
        for e, ref in enumerate(refs[:-1]):

            @pl.when(pl.program_id(0) == e)
            def _(ref=ref):
                refs[-1][...] = ref[...]

    return pl.pallas_call(
        kernel,
        grid=(count,),
        in_specs=[pl.BlockSpec((rows, columns), lambda e: (0, 0))] * count,
        out_specs=pl.BlockSpec((rows, columns), lambda e: (e, 0)),
        out_shape=jax.ShapeDtypeStruct((count * rows, columns), LOW),
        compiler_params=pltpu.CompilerParams(vmem_limit_bytes=VMEM),
        cost_estimate=cost(2),
        name="join",
    )(*parts)


def sum_small(wide, narrow):
    seqs = lax.axis_size("seq")
    lanes = wide.shape[1]
    share = wide.shape[0] // seqs
    short = -(-narrow.shape[0] // (seqs * lanes))
    fill = -(-(share + 2 * short) // 16) * 16 - share - 2 * short

    def packed(wide, narrow):
        lead = wide.shape[:-2]
        high = lax.optimization_barrier(narrow.astype(LOW))
        low = (narrow - high.astype(FULL)).astype(LOW)
        return jnp.concatenate(
            [wide.astype(LOW), high, low, jnp.zeros((*lead, fill, lanes), LOW)], axis=-2
        )

    padded = jnp.pad(narrow, (0, seqs * short * lanes - narrow.shape[0])).reshape(seqs, short, lanes)
    parts = exchange_all(packed(wide.reshape(seqs, share, lanes), padded)).astype(FULL)
    total = jnp.sum(parts, axis=0)
    total = packed(total[:share], total[share : share + short] + total[share + short : share + 2 * short])
    parts = exchange_all(jnp.broadcast_to(total[None], (seqs, *total.shape))).astype(FULL)
    result = parts[:, share : share + short] + parts[:, share + short : share + 2 * short]
    return parts[:, :share].reshape(wide.shape), result.reshape(-1)[: narrow.shape[0]]


class Chain:
    def __init__(self, x, stages):
        me = lax.axis_index("seq")
        self.start = x
        self.masks, self.places = [], []
        for bits in stages:
            place = 0
            for bit in bits:
                place = 2 * place + ((me >> bit) & 1)
            self.places.append(place)
            self.masks.append(
                [
                    sum(1 << bit for i, bit in enumerate(reversed(bits)) if e >> i & 1)
                    for e in range(1 << len(bits))
                ]
            )
        self.level = 0
        size = x.shape[0] // 2
        sent = lax.dynamic_slice_in_dim(x, (1 - self.places[0]) * size, size, 0)
        self.parts = [x, swap(sent, "seq", self.masks[0][1])]

    def steps_left(self):
        return 2 * len(self.masks) - 1 - self.level

    def step(self, *deps):
        if self.steps_left() <= 0:
            return []
        count = len(self.masks)
        self.parts = list(after(tuple(self.parts), deps))
        self.level += 1
        if self.level < count:
            masks = self.masks[self.level]
            firsts = [0 * self.places[0]] * len(self.parts)
            if self.level == 1:
                firsts[0] = self.places[0] * len(masks)
            pieces = list(split_sum(list(zip(self.parts, firsts)), self.places[self.level], len(masks)))
            self.parts = pieces[:1] + [swap(p, "seq", mask) for p, mask in zip(pieces[1:], masks[1:])]
            return pieces
        if self.level == count:
            x = sum(part.astype(FULL) for part in self.parts).astype(LOW)
        else:
            x = join(self.parts)
        masks = self.masks[2 * count - 1 - self.level]
        self.parts = [x] + [swap(x, "seq", mask) for mask in masks[1:]]
        return [x]

    def place(self):
        total = 0
        for place, masks in zip(self.places, self.masks):
            total = len(masks) * total + place
        return total


def chain_stages(first, bits):
    rest = [bit for bit in range(bits) if bit != first]
    return [[first]] + [rest[i : i + 2] for i in range(0, len(rest), 2)]


def finish(chain, row_turn, half_turn, column_turn):
    assert chain.steps_left() <= 0
    rows, columns = chain.parts[0].shape
    width = columns // 4
    scalars = jnp.stack([chain.place() ^ row_turn, half_turn, column_turn]).astype(jnp.int32)
    count = 1 << (lax.axis_size("seq") - 1).bit_length()
    spec = pl.BlockSpec((rows, 2 * width), lambda half, n: (0, half))

    def kernel(scalars, own, received, out):
        size = out.shape[0] // count
        for q in range(count):
            ref, first = (own, q * size) if q < count // 2 else (received, (q - count // 2) * size)
            target = pl.ds(pl.multiple_of((scalars[0] ^ q) * size, size), size)
            for e in range(2):
                place = pl.ds(pl.multiple_of((e ^ scalars[2]) * width, width), width)
                out[target, place] = ref[first : first + size, e * width : (e + 1) * width].astype(FULL)

    return pl.pallas_call(
        kernel,
        grid_spec=pltpu.PrefetchScalarGridSpec(
            num_scalar_prefetch=1,
            grid=(2,),
            in_specs=[spec] * 2,
            out_specs=pl.BlockSpec((2 * rows, 2 * width), lambda half, n: (0, half ^ n[1])),
        ),
        out_shape=jax.ShapeDtypeStruct((2 * rows, columns), FULL),
        compiler_params=pltpu.CompilerParams(vmem_limit_bytes=VMEM),
        cost_estimate=cost(3),
        name="finish",
    )(scalars, *chain.parts)


def cost(us):
    return pl.CostEstimate(flops=0, bytes_accessed=int(us * SCALE), transcendentals=0)


def pair(re, im):
    return jnp.concatenate([re, im], axis=-1)


def factor(re, im):
    return pair(re, re), pair(-im, im)


def times(x, first, second):
    lanes = x.shape[-1]
    return x * first + pltpu.roll(x, lanes // 2, x.ndim - 1) * second


def cmul(a, b):
    return a[0] * b[0] - a[1] * b[1], a[0] * b[1] + a[1] * b[0]


def add(a, b):
    return a[0] + b[0], a[1] + b[1]


def scale(a, k):
    return a[0] * k, a[1] * k


BBAR, READ, CARRY, STRIDE, KERNEL, Z, RATIO, C, B, A_PART, STEP = 0, 2, 4, 10, 18, 19, 21, 23, 25, 27, 29
ROWS = 30


def less_one(x):
    total = 1.0 + x / 8.0
    for k in (7.0, 6.0, 5.0, 4.0, 3.0, 2.0):
        total = 1.0 + x / k * total
    return jnp.where(x > -0.25, x * total, jnp.exp(x) - 1.0)


def consts_kernel(block, decay_ref, freq_ref, b_ref, c_ref, step_ref, consts, base):
    states, width = decay_ref.shape
    lanes = 2 * states

    def wide(x):
        return jnp.concatenate([x, x], axis=0).T

    decay, freq = wide(decay_ref[...]), wide(freq_ref[...])
    b = (wide(b_ref[0]), wide(b_ref[1]))
    c = (wide(c_ref[0]), wide(c_ref[1]))
    step = jnp.broadcast_to(step_ref[...], (lanes, width)).T
    first = lax.broadcasted_iota(jnp.int32, (width, lanes), 1) < states
    rate = step * decay
    turn = step * freq
    size = jnp.exp(-rate)
    z = (size * jnp.cos(turn), size * jnp.sin(turn))
    half_turn = jnp.sin(0.5 * turn)
    less = (less_one(-rate) * jnp.cos(turn) - 2.0 * half_turn * half_turn, z[1])
    modulus = decay * decay + freq * freq
    ratio = (
        (freq * less[1] - decay * less[0]) / modulus,
        -(decay * less[1] + freq * less[0]) / modulus,
    )
    bbar = cmul(ratio, b)
    twice_c = scale(c, 2.0)

    def put_factor(k, x):
        consts[k] = x[0]
        consts[k + 1] = jnp.where(first, -x[1], x[1])

    def put_plain(k, x):
        consts[k] = x[0]
        consts[k + 1] = x[1]

    put_factor(BBAR, bbar)
    put_factor(READ, cmul(twice_c, z))
    kernel = cmul(twice_c, bbar)
    consts[KERNEL] = jnp.where(first, kernel[0], -kernel[1])
    put_plain(Z, z)
    put_plain(RATIO, ratio)
    put_plain(C, c)
    put_plain(B, b)
    consts[A_PART] = decay
    consts[A_PART + 1] = freq
    consts[STEP] = step
    power = (jnp.ones_like(size), jnp.zeros_like(size))
    for k in range(8):
        base[k] = jnp.where(first, power[0], power[1])
        power = cmul(power, z)
    k = 8
    while k < 4 * block:
        if k <= 64:
            put_factor(STRIDE + 2 * (k.bit_length() - 4), power)
        if k >= block:
            put_factor(CARRY + 2 * ((k // block).bit_length() - 1), power)
        power = cmul(power, power)
        k *= 2
    put_factor(CARRY + 4, power)


def s4_consts(a_decay, a_freq, b_state, c_state, step_size, block):
    states, width = a_decay.shape
    return pl.pallas_call(
        lambda *refs: consts_kernel(block, *refs),
        out_shape=[
            jax.ShapeDtypeStruct((ROWS, width, 2 * states), FULL),
            jax.ShapeDtypeStruct((8, width, 2 * states), FULL),
        ],
        compiler_params=pltpu.CompilerParams(vmem_limit_bytes=VMEM),
        cost_estimate=cost(6),
        name="s4_consts",
    )(a_decay, a_freq, b_state, c_state, step_size[None, :])


def half_turned(x):
    return pltpu.roll(x, x.shape[-1] // 2, x.ndim - 1)


def high_low(x):
    high = x.astype(LOW)
    return high, (x - high.astype(FULL)).astype(LOW)


def dot(a, b):
    return lax.dot_general(a, b, (((1,), (0,)), ((), ())), preferred_element_type=FULL)


def dot_t(a, b):
    return lax.dot_general(a, b, (((1,), (1,)), ((), ())), preferred_element_type=FULL)


def tables_kernel(base, consts, *refs):
    z_out, h_out = refs[-2:]
    channels, _, lanes = z_out.shape
    row8 = lax.broadcasted_iota(jnp.int32, (8, lanes), 0)
    row = lax.broadcasted_iota(jnp.int32, (lanes, lanes), 0)
    lane = lax.broadcasted_iota(jnp.int32, (lanes, lanes), 1)
    live = row + lane >= lanes - 1

    def one(c):
        first = jnp.concatenate([base[k, pl.ds(c, 1), :] for k in range(8)], axis=0)
        tiles = [(first, half_turned(first))]
        for level in range(4):
            k = STRIDE + 2 * level
            a, b = consts[k, pl.ds(c, 1), :], consts[k + 1, pl.ds(c, 1), :]
            tiles += [(t * a + u * b, u * a - t * b) for t, u in tiles]
        z = jnp.concatenate([t for t, _ in tiles], axis=0)
        high, low = high_low(z)
        z_out[c, :lanes, :] = high
        z_out[c, lanes:, :] = low
        f_high, f_low = high_low(jnp.broadcast_to(consts[KERNEL, pl.ds(c, 1), :], (8, lanes)))
        h = dot_t(jnp.concatenate([f_high, f_low], axis=0), high)
        h = h[:8] + h[8:] + dot_t(f_high, low)
        for bit in (1, 2, 4):
            h = jnp.where((7 - row8) & bit != 0, pltpu.roll(h, bit, 1), h)
        hankel = [pltpu.roll(h, lanes - 8 - k, 1) if k < lanes - 8 else h for k in range(0, lanes, 8)]
        hankel = jnp.concatenate(hankel, axis=0)
        h_out[c] = jnp.where(live, hankel, 0.0).astype(LOW)

    @pl.loop(0, channels, step=UNROLL)
    def _(c):
        for k in range(UNROLL):
            one(c + k)


def s4_tables(base, consts, part, parts, tables=(), deps=()):
    _, width, lanes = base.shape
    steps = width // CHANNELS // parts
    skip = part * steps
    anywhere = pl.BlockSpec(memory_space=pl.ANY)
    return pl.pallas_call(
        tables_kernel,
        grid=(steps,),
        in_specs=[
            pl.BlockSpec((8, CHANNELS, lanes), lambda i: (0, i + skip, 0)),
            pl.BlockSpec((ROWS, CHANNELS, lanes), lambda i: (0, i + skip, 0)),
        ]
        + [anywhere] * (len(tables) + len(deps)),
        out_specs=[
            pl.BlockSpec((CHANNELS, 2 * lanes, lanes), lambda i: (i + skip, 0, 0)),
            pl.BlockSpec((CHANNELS, lanes, lanes), lambda i: (i + skip, 0, 0)),
        ],
        out_shape=[
            jax.ShapeDtypeStruct((width, 2 * lanes, lanes), LOW),
            jax.ShapeDtypeStruct((width, lanes, lanes), LOW),
        ],
        input_output_aliases={2: 0, 3: 1} if tables else {},
        compiler_params=pltpu.CompilerParams(vmem_limit_bytes=VMEM),
        cost_estimate=cost(24 / parts),
        name="s4_tables",
    )(base, consts, *tables, *deps)


def flip_matrix(size):
    row = lax.broadcasted_iota(jnp.int32, (size, size), 0)
    lane = lax.broadcasted_iota(jnp.int32, (size, size), 1)
    return (row + lane == size - 1).astype(FULL).astype(LOW)


def rows_of_channels(consts, k):
    return jnp.stack([consts[k, c : c + 1, :] for c in range(consts.shape[1])])


def weighted_ends(x, place, z):
    high, low = high_low(x * place)
    x = x.astype(LOW)
    none = jnp.zeros_like(x)
    left = jnp.concatenate([x, high, low, none], axis=0)
    right = jnp.concatenate([x, high, none, none], axis=0)
    ends = dot(jnp.concatenate([left, right], axis=1), z)
    count = x.shape[0]
    return ends[:count], ends[count : 2 * count] + ends[2 * count : 3 * count]


def times_both(x, consts, k):
    first, second = rows_of_channels(consts, k), rows_of_channels(consts, k + 1)
    return x[0] * first + x[1] * second, x[1] * first - x[0] * second


def scan_blocks(x, consts, row, reverse):
    count = x[0].shape[1]
    for level, d in enumerate((1, 2, 4)):
        live = row < count - d if reverse else row >= d
        moved = [jnp.where(live, pltpu.roll(e, count - d if reverse else d, 1), 0.0) for e in x]
        x = add(x, times_both(moved, consts, CARRY + 2 * level))
    return x


def forward_kernel(
    signal, skip, consts, z, m, init, activ, slope, x_out, p_out, q_out, s_out, x_scr, y_scr
):
    step = pl.program_id(0)
    channels, _, lanes = z.shape
    count = signal.shape[0] // lanes
    width = signal.shape[1]

    @pl.when(step == 0)
    def _():
        flip = flip_matrix(lanes)
        for j in range(count):
            x_scr[pl.ds(j, width, stride=count), :] = dot(flip, signal[j * lanes : (j + 1) * lanes, :]).T

    rows = pl.ds(pl.multiple_of(step * channels * count, channels * count), channels * count)
    x = x_scr[rows, :].reshape(channels, count, lanes)
    place = lax.broadcasted_iota(jnp.int32, (count, lanes), 1).astype(FULL)
    row = lax.broadcasted_iota(jnp.int32, (channels, count, lanes), 1)
    plus = lax.broadcasted_iota(jnp.int32, (channels, count, lanes), 2) < lanes // 2
    ends = [weighted_ends(x[c], place, z[c]) for c in range(channels)]
    p = jnp.stack([e[0] for e in ends])
    q = jnp.stack([e[1] for e in ends])
    start = init[...][:, None, :]
    state = times_both((p, half_turned(p)), consts, BBAR)
    state = [
        jnp.where(row == 0, e, pltpu.roll(s, 1, 1)) for e, s in zip((start, half_turned(start)), state)
    ]
    state = scan_blocks(state, consts, row, False)
    read, _ = times_both(state, consts, READ)
    read = jnp.where(plus, read, -read).astype(LOW)
    y = [dot(x[c].astype(LOW), m[c]) + dot_t(read[c], z[c, :lanes, :]) for c in range(channels)]
    y_scr[rows, :] = jnp.concatenate(y, axis=0)
    x_out[...] = x
    p_out[...] = p
    q_out[...] = q
    s_out[...] = state[0]

    @pl.when(step == pl.num_programs(0) - 1)
    def _():
        for j in range(count):
            part = slice(j * lanes, (j + 1) * lanes)
            mixed = y_scr[pl.ds(j, width, stride=count), :].T + skip[...] * signal[part, :].astype(FULL)
            inner = 0.7978845608028654 * (mixed + 0.044715 * mixed * mixed * mixed)
            bent = jnp.tanh(inner)
            activ[part, :] = (0.5 * mixed * (1.0 + bent)).astype(LOW)
            slope[part, :] = 0.5 * (1.0 + bent) + 0.5 * mixed * (1.0 - bent * bent) * (
                0.7978845608028654 * (1.0 + 3 * 0.044715 * mixed * mixed)
            )


def s4_forward(signal, skip, consts, z, m, init):
    tokens, width = signal.shape
    lanes = z.shape[-1]
    count = tokens // lanes
    whole = pl.BlockSpec((tokens, width), lambda i: (0, 0))
    by_channel = pl.BlockSpec((CHANNELS, count, lanes), lambda i: (i, 0, 0))
    per_channel = jax.ShapeDtypeStruct((width, count, lanes), FULL)
    return pl.pallas_call(
        forward_kernel,
        grid=(width // CHANNELS,),
        in_specs=[
            whole,
            pl.BlockSpec((1, width), lambda i: (0, 0)),
            pl.BlockSpec((ROWS, CHANNELS, lanes), lambda i: (0, i, 0)),
            pl.BlockSpec((CHANNELS, 2 * lanes, lanes), lambda i: (i, 0, 0)),
            pl.BlockSpec((CHANNELS, lanes, lanes), lambda i: (i, 0, 0)),
            pl.BlockSpec((CHANNELS, lanes), lambda i: (i, 0)),
        ],
        out_specs=[whole, whole] + [by_channel] * 4,
        out_shape=[
            jax.ShapeDtypeStruct((tokens, width), LOW),
            jax.ShapeDtypeStruct((tokens, width), FULL),
        ]
        + [per_channel] * 4,
        scratch_shapes=[pltpu.VMEM((width * count, lanes), FULL)] * 2,
        compiler_params=pltpu.CompilerParams(vmem_limit_bytes=VMEM),
        cost_estimate=cost(18),
        name="s4_forward",
    )(signal, skip, consts, z, m, init)


def backward_kernel(
    grads, consts, z, m, init, out, g_out, u_out, v_out, h_out, g_scr, y_scr
):
    step = pl.program_id(0)
    channels, _, lanes = z.shape
    count = grads.shape[0] // lanes
    width = grads.shape[1]

    @pl.when(step == 0)
    def _():
        for j in range(count):
            g_scr[pl.ds(j, width, stride=count), :] = grads[j * lanes : (j + 1) * lanes, :].astype(FULL).T

    rows = pl.ds(pl.multiple_of(step * channels * count, channels * count), channels * count)
    g = g_scr[rows, :].reshape(channels, count, lanes)
    place = lax.broadcasted_iota(jnp.int32, (count, lanes), 1).astype(FULL)
    row = lax.broadcasted_iota(jnp.int32, (channels, count, lanes), 1)
    plus = lax.broadcasted_iota(jnp.int32, (channels, count, lanes), 2) < lanes // 2
    ends = [weighted_ends(g[c], place, z[c]) for c in range(channels)]
    u = jnp.stack([e[0] for e in ends])
    v = jnp.stack([e[1] for e in ends])
    start = init[...][:, None, :]
    later = times_both((u, half_turned(u)), consts, READ)
    later = [
        jnp.where(row == count - 1, e, pltpu.roll(s, count - 1, 1))
        for e, s in zip((start, half_turned(start)), later)
    ]
    later = scan_blocks(later, consts, row, True)
    write, _ = times_both(later, consts, BBAR)
    write = jnp.where(plus, write, -write).astype(LOW)
    y = [dot(g[c].astype(LOW), m[c]) + dot_t(write[c], z[c, :lanes, :]) for c in range(channels)]
    y_scr[rows, :] = jnp.concatenate(y, axis=0)
    g_out[...] = g
    u_out[...] = u
    v_out[...] = v
    h_out[...] = later[0]

    @pl.when(step == pl.num_programs(0) - 1)
    def _():
        flip = flip_matrix(lanes)
        for j in range(count):
            out[j * lanes : (j + 1) * lanes, :] = dot(
                flip, y_scr[pl.ds(j, width, stride=count), :].T.astype(LOW)
            )


def s4_backward(grads, consts, z, m, init):
    tokens, width = grads.shape
    lanes = z.shape[-1]
    count = tokens // lanes
    whole = pl.BlockSpec((tokens, width), lambda i: (0, 0))
    by_channel = pl.BlockSpec((CHANNELS, count, lanes), lambda i: (i, 0, 0))
    per_channel = jax.ShapeDtypeStruct((width, count, lanes), FULL)
    return pl.pallas_call(
        backward_kernel,
        grid=(width // CHANNELS,),
        in_specs=[
            whole,
            pl.BlockSpec((ROWS, CHANNELS, lanes), lambda i: (0, i, 0)),
            pl.BlockSpec((CHANNELS, 2 * lanes, lanes), lambda i: (i, 0, 0)),
            pl.BlockSpec((CHANNELS, lanes, lanes), lambda i: (i, 0, 0)),
            pl.BlockSpec((CHANNELS, lanes), lambda i: (i, 0)),
        ],
        out_specs=[whole] + [by_channel] * 4,
        out_shape=[jax.ShapeDtypeStruct((tokens, width), FULL)] + [per_channel] * 4,
        scratch_shapes=[pltpu.VMEM((width * count, lanes), FULL)] * 2,
        compiler_params=pltpu.CompilerParams(vmem_limit_bytes=VMEM),
        cost_estimate=cost(18),
        name="s4_backward",
    )(grads, consts, z, m, init)


def sums_kernel(block, x, g, p, q, s, u, v, h, z, consts, dep, out):
    del dep
    channels, count, lanes = x.shape
    states = lanes // 2
    row8 = lax.broadcasted_iota(jnp.int32, (8, lanes), 0)
    row = lax.broadcasted_iota(jnp.int32, (lanes, lanes), 0)
    lane = lax.broadcasted_iota(jnp.int32, (lanes, lanes), 1)
    place = lax.broadcasted_iota(jnp.int32, (8, lanes), 1).astype(FULL)
    live = row + lane >= lanes - 1
    first = lax.broadcasted_iota(jnp.int32, (channels, lanes), 1) < states
    w = []
    for c in range(channels):
        both = lax.dot_general(
            x[c].astype(LOW), g[c].astype(LOW), (((0,), (0,)), ((), ())), preferred_element_type=FULL
        )
        both = jnp.where(live, both, 0.0)
        tiles = [both[k : k + 8, :] for k in range(0, lanes, 8)]
        shift = 8
        while len(tiles) > 1:
            tiles = [a + pltpu.roll(b, shift, 1) for a, b in zip(tiles[::2], tiles[1::2])]
            shift *= 2
        total = pltpu.roll(tiles[0], 1, 1)
        for bit in (1, 2, 4):
            total = jnp.where(row8 & bit != 0, pltpu.roll(total, bit, 1), total)
        high, low = high_low(total)
        place_high, place_low = high_low(total * place)
        none = jnp.zeros_like(high)
        left = jnp.concatenate([high, low, place_high, place_low], axis=0)
        right = jnp.concatenate([high, none, place_high, none], axis=0)
        w.append(dot(jnp.concatenate([left, right], axis=1), z[c]))
    lag0 = jnp.sum(jnp.stack([e[:16] for e in w]), axis=1)
    lag1 = jnp.sum(jnp.stack([e[16:] for e in w]), axis=1)

    def both_halves(x):
        turned = half_turned(x)
        return jnp.where(first, x, turned), jnp.where(first, turned, x)

    def product(a, b):
        plain = jnp.sum(a * b, axis=1)
        crossed = jnp.sum(a * half_turned(b), axis=1)
        plain = jnp.where(first, plain, -plain)
        return plain + half_turned(plain), crossed + half_turned(crossed)

    states_read = product(u[...], s[...])
    slopes_read = product(u[...] + v[...], s[...])
    writes = product(h[...], p[...])
    slopes_write = product(h[...], q[...])
    carried = product(h[...], s[...])
    lag0, lag1 = both_halves(lag0), both_halves(lag1)

    def const(k):
        return consts[k]

    def const_factor(k):
        second = const(k + 1)
        return const(k), jnp.where(first, -second, second)

    bbar, read, carry = const_factor(BBAR), const_factor(READ), const_factor(CARRY)
    z_one, ratio = (const(Z), const(Z + 1)), (const(RATIO), const(RATIO + 1))
    c, b = (const(C), const(C + 1)), (const(B), const(B + 1))
    decay, freq, step = const(A_PART), const(A_PART + 1), const(STEP)
    modulus = decay * decay + freq * freq
    over_a = (-decay / modulus, -freq / modulus)
    to_c = scale(add(cmul(z_one, states_read), cmul(bbar, lag0)), 2.0)
    to_bbar = add(writes, scale(cmul(c, lag0), 2.0))
    to_log = add(
        add(cmul(read, slopes_read), cmul(bbar, slopes_write)),
        add(scale(cmul(carry, carried), float(block)), scale(cmul(cmul(c, bbar), lag1), 2.0)),
    )
    to_b = cmul(to_bbar, ratio)
    over = cmul(cmul(to_bbar, b), over_a)
    to_log = add(to_log, cmul(over, z_one))
    to_a = cmul(over, ratio)
    grad_decay = to_a[0] - step * to_log[0]
    grad_freq = to_a[1] - step * to_log[1]
    grad_step = jnp.where(first, -to_log[0] * decay, -to_log[1] * freq)
    out[0] = jnp.where(first, grad_decay, grad_freq)
    out[1] = jnp.where(first, to_b[0], -to_b[1])
    out[2] = jnp.where(first, to_c[0], -to_c[1])
    out[3] = jnp.broadcast_to(jnp.sum(grad_step, axis=1, keepdims=True), (channels, lanes))


def s4_sums(x, g, p, q, s, u, v, h, z, consts, block, dep, part, parts):
    width, count, lanes = x.shape
    steps = width // CHANNELS // parts
    skip = part * steps
    by_channel = pl.BlockSpec((CHANNELS, count, lanes), lambda i: (i + skip, 0, 0))
    return pl.pallas_call(
        lambda *refs: sums_kernel(block, *refs),
        grid=(steps,),
        in_specs=[by_channel] * 8
        + [
            pl.BlockSpec((CHANNELS, 2 * lanes, lanes), lambda i: (i + skip, 0, 0)),
            pl.BlockSpec((ROWS, CHANNELS, lanes), lambda i: (0, i + skip, 0)),
            pl.BlockSpec(memory_space=pl.ANY),
        ],
        out_specs=pl.BlockSpec((4, CHANNELS, lanes), lambda i: (0, i, 0)),
        out_shape=jax.ShapeDtypeStruct((4, width // parts, lanes), FULL),
        compiler_params=pltpu.CompilerParams(vmem_limit_bytes=VMEM),
        cost_estimate=cost(18 / parts),
        name="s4_sums",
    )(x, g, p, q, s, u, v, h, z, consts, dep)


def split(rows):
    half = rows.shape[-1] // 2
    return rows[..., :half], rows[..., half:]


def t_dot(a, b):
    return lax.dot_general(a, b, (((0,), (0,)), ((), ())), preferred_element_type=FULL)


def layer_forward(values, gain, bias, total_width, sums=None):
    if sums is None:
        sums = sum_chan(jnp.stack([jnp.sum(values, axis=-1), jnp.sum(values * values, axis=-1)]))
    center = sums[0] / total_width
    spread_var = sums[1] / total_width - center * center
    inverse = lax.rsqrt(spread_var + EPSILON)[..., None]
    normed = (values - center[..., None]) * inverse
    return normed * gain + bias, normed, inverse


def layer_backward(grad_out, normed, inverse, gain, total_width, work):
    scaled = grad_out * gain
    sums = jnp.stack([jnp.sum(scaled, axis=-1), jnp.sum(scaled * normed, axis=-1)])
    sums = after(sum_chan(sums), *work(sums))
    grad_in = inverse * (
        scaled - sums[0][..., None] / total_width - normed * sums[1][..., None] / total_width
    )
    return grad_in, jnp.sum(grad_out * normed, axis=0), jnp.sum(grad_out, axis=0)


def body(
    block_input,
    lengths,
    norm1_gain,
    norm1_bias,
    a_decay,
    a_freq,
    b_state,
    c_state,
    step_size,
    skip_gain,
    w_value,
    b_value,
    w_gate,
    b_gate,
    norm2_gain,
    norm2_bias,
    w_up,
    b_up,
    w_down,
    b_down,
    out_grad,
):
    batch, block, width = block_input.shape
    chans = lax.axis_size("chan")
    seqs = lax.axis_size("seq")
    assert seqs % batch == 0
    runs = seqs // batch
    total_width = width * chans
    assert chans == 4
    seq_me = lax.axis_index("seq")
    chan_me = lax.axis_index("chan")
    groups = None if runs == 1 else [[r * batch + j for j in range(batch)] for r in range(runs)]
    peers = None if runs == 1 else [[r * batch + j for r in range(runs)] for j in range(batch)]

    def exchange(x):
        return lax.all_to_all(x, "seq", 0, 0, axis_index_groups=groups, tiled=True)

    def rows_of(w):
        return [
            lax.dynamic_slice_in_dim(w, (chan_me ^ d) * width, width, 0) for d in range(chans)
        ]

    inputs_low = exchange(block_input).reshape(batch * block, width)

    consts, base = s4_consts(a_decay, a_freq, b_state, c_state, step_size, block)
    tables = s4_tables(base, consts, 0, 2)
    inputs_low = after(inputs_low, tables[0])
    inputs = inputs_low.astype(FULL)
    moments = jnp.stack([jnp.sum(inputs, axis=-1), jnp.sum(inputs * inputs, axis=-1)])
    grad_low = exchange(after(out_grad, moments)).reshape(batch * block, width)
    z, m = s4_tables(base, consts, 1, 2, tables, (moments,))
    moments = after(sum_chan(moments), m)
    states = a_decay.shape[0]

    def const_factor(k):
        return consts[k, :, :states], consts[k + 1, :, states:]

    begin = (seq_me // batch) * batch * block
    places = begin + jnp.arange(batch * block, dtype=jnp.int32)
    mask = (places < lengths[seq_me % batch]).astype(FULL)[:, None]
    norm_one, normed_one, inverse_one = layer_forward(inputs, norm1_gain, norm1_bias, total_width, moments)
    signal = (mask * norm_one).astype(LOW)
    skip = skip_gain[None, :]
    init = jnp.zeros((width, 2 * states), FULL)
    if runs > 1:
        _, _, _, p, _, s = s4_forward(signal, skip, consts, z, m, init)
        carry = const_factor(CARRY)
        end = add(cmul(carry, split(s[:, -1])), cmul(const_factor(BBAR), split(p[:, -1])))
        ends = lax.all_gather(pair(*end), "seq", axis_index_groups=peers)
        hop = carry
        for _ in range(3):
            hop = cmul(hop, hop)
        for r in range(runs - 1):
            moved = add(cmul(hop, split(init)), split(ends[r]))
            init = jnp.where(r < seq_me // batch, pair(*moved), init)
    activ, slope, xs, ps, qs, ss = s4_forward(signal, skip, consts, z, m, init)

    wv, wg = rows_of(w_value), rows_of(w_gate)
    w_gated = [jnp.concatenate([a, b], axis=1) for a, b in zip(wv, wg)]
    w_ups = rows_of(w_up)
    w_downs = [
        lax.dynamic_slice_in_dim(w_down, (chan_me ^ d) * width, width, 1) for d in range(chans)
    ]
    grads = gather_pieces(grad_low)
    activs = gather_pieces(after(activ, grads[2]))
    both = sum(dot(a, w) for a, w in zip(activs, w_gated))
    value = both[:, :width] + b_value
    gate = both[:, width:] + b_gate
    opened = jax.nn.sigmoid(gate)
    resid = inputs + value * opened
    norm_two, normed_two, inverse_two = layer_forward(resid, norm2_gain, norm2_bias, total_width)
    norms = gather_pieces(norm_two.astype(LOW))
    hidden = sum(dot(a, w) for a, w in zip(norms, w_ups)) + b_up
    spread, gelu_pull = jax.vjp(jax.nn.gelu, hidden)
    spread = spread.astype(LOW)
    downs = [dot(spread, w) for w in w_downs]
    output = (resid + reduce_pieces(downs) + b_down).astype(LOW)
    output = exchange(output.reshape(batch, block, width))

    grad_out = grad_low.astype(FULL)
    grad_spread = sum(dot_t(a, w) for a, w in zip(grads, w_downs))
    grad_hidden = gelu_pull(grad_spread)[0].astype(LOW)
    marks = []
    grad_norm_two = reduce_pieces([dot_t(grad_hidden, w) for w in w_ups], marks)
    bits = axis_bits("seq")
    orders = chain_stages(0, bits), chain_stages(1, bits)
    spread_late, hidden_late = after(spread, marks[0]), after(grad_hidden, marks[0])
    downs = [Chain(t_dot(spread_late, jnp.concatenate(grads, axis=1)).astype(LOW), orders[0])]
    ups = [Chain(t_dot(jnp.concatenate(norms, axis=1), hidden_late).astype(LOW), orders[1])]
    grad_norm_two = after(grad_norm_two, *[chain.start for chain in downs + ups])

    def steps(chains, *deps):
        return [made for chain in chains for made in chain.step(*deps)]

    grad_resid, grad_norm2_gain, grad_norm2_bias = layer_backward(
        grad_norm_two, normed_two, inverse_two, norm2_gain, total_width, lambda dep: []
    )
    grad_resid = grad_out + grad_resid
    grad_value = (grad_resid * opened).astype(LOW)
    grad_gate = (grad_resid * value * opened * (1.0 - opened)).astype(LOW)
    grad_both = jnp.concatenate([grad_value, grad_gate], axis=1)
    grad_activ = reduce_pieces([dot_t(grad_both, w) for w in w_gated], marks)
    gateds = [
        Chain(t_dot(jnp.concatenate(activs, axis=1), after(grad_both, marks[1])).astype(LOW), orders[0])
    ]
    grad_activ = after(grad_activ, gateds[0].start, *steps(downs, marks[1]))
    grad_mixed = (grad_activ * slope).astype(LOW)
    init = jnp.zeros((width, 2 * states), FULL)
    if runs > 1:
        _, _, u, _, h = s4_backward(grad_mixed, consts, z, m, init)
        end = add(cmul(carry, split(h[:, 0])), cmul(const_factor(READ), split(u[:, 0])))
        ends = lax.all_gather(pair(*end), "seq", axis_index_groups=peers)
        for r in reversed(range(1, runs)):
            moved = add(cmul(hop, split(init)), split(ends[r]))
            init = jnp.where(r > seq_me // batch, pair(*moved), init)
    grad_signal, gs, us, vs, hs = s4_backward(grad_mixed, consts, z, m, init)
    grad_signal = grad_signal + skip * grad_mixed.astype(FULL)
    s4_parts = (xs, gs, ps, qs, ss, us, vs, hs, z, consts, block)
    sums = []

    def sums_part(*deps):
        sums.append(s4_sums(*s4_parts, after(hs, *deps), len(sums), 4))
        return sums[-1]

    grad_input, grad_norm1_gain, grad_norm1_bias = layer_backward(
        grad_signal * mask,
        normed_one,
        inverse_one,
        norm1_gain,
        total_width,
        lambda dep: [sums_part(dep)],
    )
    grad_input_low = (grad_resid + grad_input).astype(LOW)
    grad_input = exchange(grad_input_low.reshape(batch, block, width))
    part = sums_part(grad_input_low, output, *steps(downs, sums[0]))
    part = sums_part(*steps(ups + gateds, part))
    part = sums_part(*steps(downs + gateds, part))
    work = steps(ups + gateds, part)
    grad_input = after(grad_input, part).astype(FULL)
    sums = jnp.concatenate(sums, axis=1)
    narrow = jnp.concatenate(
        [
            grad_norm1_gain,
            grad_norm1_bias,
            jnp.sum(grad_mixed.astype(FULL) * signal.astype(FULL), axis=0),
            jnp.sum(grad_value.astype(FULL), axis=0),
            jnp.sum(grad_gate.astype(FULL), axis=0),
            grad_norm2_gain,
            grad_norm2_bias,
            jnp.sum(grad_out, axis=0),
            sums[3, :, 0],
            jnp.sum(grad_hidden.astype(FULL), axis=0),
        ]
    )
    wide, narrow = sum_small(sums[:3].reshape(3 * width, 2 * states), narrow)
    wide = wide.reshape(3, width, 2 * states).transpose(0, 2, 1)
    chains = downs + ups + gateds
    while any(chain.steps_left() > 0 for chain in chains):
        work = steps(chains, *work)
    vectors = [narrow[k * width : (k + 1) * width] for k in range(9)]
    vectors.insert(2, vectors.pop(8))

    zero = 0 * chan_me
    down = finish(downs[0], zero, chan_me >> 1, chan_me & 1)
    up = finish(ups[0], chan_me * (seqs // chans), zero, zero)
    gated = finish(gateds[0], chan_me * (seqs // chans), zero, zero)
    return (
        output,
        grad_input,
        vectors[0],
        vectors[1],
        wide[0, :states],
        wide[0, states:],
        wide[1].reshape(2, states, width),
        wide[2].reshape(2, states, width),
        vectors[2],
        vectors[3],
        gated[:, :width],
        vectors[4],
        gated[:, width:],
        vectors[5],
        vectors[6],
        vectors[7],
        up,
        narrow[9 * width :],
        down,
        vectors[8],
    )


def solution(mesh):
    in_specs = (
        P(None, "seq", "chan"),
        P(),
        P("chan"),
        P("chan"),
        P(None, "chan"),
        P(None, "chan"),
        P(None, None, "chan"),
        P(None, None, "chan"),
        P("chan"),
        P("chan"),
        P(None, "chan"),
        P("chan"),
        P(None, "chan"),
        P("chan"),
        P("chan"),
        P("chan"),
        P(None, "chan"),
        P("chan"),
        P("chan", None),
        P("chan"),
        P(None, "seq", "chan"),
    )
    out_specs = (
        P(None, "seq", "chan"),
        P(None, "seq", "chan"),
        P("chan"),
        P("chan"),
        P(None, "chan"),
        P(None, "chan"),
        P(None, None, "chan"),
        P(None, None, "chan"),
        P("chan"),
        P("chan"),
        P(None, "chan"),
        P("chan"),
        P(None, "chan"),
        P("chan"),
        P("chan"),
        P("chan"),
        P(None, "chan"),
        P("chan"),
        P("chan", None),
        P("chan"),
    )
    return jax.shard_map(body, mesh=mesh, in_specs=in_specs, out_specs=out_specs, check_vma=False)
```

```python
import jax
import jax.numpy as jnp
from jax import lax
from jax.experimental import pallas as pl
from jax.experimental.pallas import tpu as pltpu
from jax.sharding import PartitionSpec as P

EPSILON = 1e-05
LOW = jnp.bfloat16
FULL = jnp.float32
CHANNELS = 32
UNROLL = 16
SCALE = 1.0e5
VMEM = 56 * 1024 * 1024


def swap(x, axis, distance):
    return lax.ppermute(x, axis, [(i, i ^ distance) for i in range(lax.axis_size(axis))])


def axis_bits(axis):
    size = lax.axis_size(axis)
    bits = size.bit_length() - 1
    assert size == 1 << bits
    return bits


def gather_pieces(x):
    pieces = {0: x}
    for bit in reversed(range(axis_bits("chan"))):
        for d in list(pieces):
            pieces[d ^ (1 << bit)] = swap(pieces[d], "chan", 1 << bit)
    return [pieces[d] for d in range(len(pieces))]


def reduce_pieces(parts, marks=None):
    sums = dict(enumerate(parts))
    for bit in range(axis_bits("chan")):
        if marks is not None and bit == axis_bits("chan") - 1:
            marks += [sums[1 << bit], sums[0]]
        for d in sorted(sums, reverse=True):
            if d >> bit & 1:
                received = swap(sums.pop(d).astype(LOW), "chan", 1 << bit)
                if marks is not None and d == 1 << (axis_bits("chan") - 1):
                    marks.append(received)
                sums[d ^ (1 << bit)] = sums[d ^ (1 << bit)] + received.astype(FULL)
    return sums[0]


def sum_chan(x):
    return x + sum(swap(x, "chan", d) for d in range(1, lax.axis_size("chan")))


def after(x, *others):
    return lax.optimization_barrier((x, others))[0]


def exchange_all(x):
    return lax.all_to_all(x, "seq", 0, 0, tiled=True)


def small_kernel(share, parts, *refs):
    out = refs[-1]
    total = sum(parts[k].astype(FULL) for k in range(parts.shape[0]))
    narrow = total[share : share + 8] + total[share + 8 : share + 16]
    high = narrow.astype(LOW).astype(FULL)
    rows = [total[:share], high, narrow - high]
    fill = total.shape[0] - share - 16
    if fill:
        rows.append(jnp.zeros((fill, total.shape[1]), FULL))
    total = jnp.concatenate(rows, axis=0).astype(LOW)
    for k in range(parts.shape[0]):
        out[k] = total


def pack_kernel(share, sums, narrow, *refs):
    packed = refs[-1]
    seqs, rows, lanes = packed.shape
    groups, width, _ = sums.shape
    flat = sums[: groups - 1].reshape((groups - 1) * width, lanes)
    for k in range(seqs):
        part = narrow[k]
        high = part.astype(LOW).astype(FULL)
        pieces = [flat[k * share : (k + 1) * share], high, part - high]
        if rows > share + 16:
            pieces.append(jnp.zeros((rows - share - 16, lanes), FULL))
        packed[k] = jnp.concatenate(pieces, axis=0).astype(LOW)


def sum_small(sums, narrow, deps, late_deps):
    seqs = lax.axis_size("seq")
    groups, width, lanes = sums.shape
    share = (groups - 1) * width // seqs
    short = -(-narrow.shape[0] // (seqs * lanes))
    assert short <= 8
    rows = -(-(share + 16) // 16) * 16
    narrow_rows = jnp.pad(narrow, (0, seqs * short * lanes - narrow.shape[0])).reshape(seqs, short, lanes)
    narrow_rows = jnp.pad(narrow_rows, ((0, 0), (0, 8 - short), (0, 0)))
    here, anywhere = pl.BlockSpec(memory_space=pltpu.VMEM), pl.BlockSpec(memory_space=pl.ANY)
    packed = pl.pallas_call(
        lambda *refs: pack_kernel(share, *refs),
        in_specs=[here] * 2 + [anywhere] * len(deps),
        out_specs=here,
        out_shape=jax.ShapeDtypeStruct((seqs, rows, lanes), LOW),
        compiler_params=pltpu.CompilerParams(vmem_limit_bytes=VMEM),
        cost_estimate=cost(1),
        name="pack_small",
    )(sums, narrow_rows, *deps)
    total = pl.pallas_call(
        lambda *refs: small_kernel(share, *refs),
        in_specs=[here] + [anywhere] * len(late_deps),
        out_specs=here,
        out_shape=jax.ShapeDtypeStruct(packed.shape, LOW),
        compiler_params=pltpu.CompilerParams(vmem_limit_bytes=VMEM),
        cost_estimate=cost(1),
        name="sum_small",
    )(exchange_all(packed), *late_deps)
    parts = exchange_all(total).astype(FULL)
    result = parts[:, share : share + short] + parts[:, share + 8 : share + 8 + short]
    wide = parts[:, :share].reshape(groups - 1, width, lanes)
    return wide, result.reshape(-1)[: narrow.shape[0]], packed


QUAD = 4


def deal(x):
    seqs = lax.axis_size("seq")
    groups = [list(range(i, i + QUAD)) for i in range(0, seqs, QUAD)]
    return lax.all_to_all(x.reshape(QUAD, -1, x.shape[1]), "seq", 0, 0, axis_index_groups=groups, tiled=True)


class Chain:
    def __init__(self, parts, halves):
        self.masks = [1 << bit for bit in range(axis_bits("seq")) if 1 << bit >= QUAD]
        self.parts = parts
        self.halves = halves
        self.tasks = ["deal" if halves else "whole", "sum"]

    def accept(self, task, outs):
        if task == "deal":
            self.parts = [outs[0], swap(outs[1], "seq", self.masks[0])]
        elif task == "whole":
            self.parts = [outs[0], swap(outs[0], "seq", self.masks[0])]
        else:
            total = outs[0]
            for mask in self.masks[1:]:
                total = (total.astype(FULL) + swap(total, "seq", mask).astype(FULL)).astype(LOW)
            self.parts = [total]
            if self.halves:
                self.parts.append(swap(total, "seq", self.masks[0]))


def gather(part):
    return [part] + [swap(part, "seq", mask) for mask in range(1, QUAD)]


def join_sum(left, own, received, deps):
    rows, columns = left.shape

    def kernel(left, own, received, *refs):
        out = refs[-1]
        out[:, :columns] = left[...]
        out[:, columns:] = (own[...].astype(FULL) + received[...].astype(FULL)).astype(LOW)

    here, anywhere = pl.BlockSpec(memory_space=pltpu.VMEM), pl.BlockSpec(memory_space=pl.ANY)
    return pl.pallas_call(
        kernel,
        in_specs=[here] * 3 + [anywhere] * len(deps),
        out_specs=here,
        out_shape=jax.ShapeDtypeStruct((rows, columns + own.shape[1]), LOW),
        compiler_params=pltpu.CompilerParams(vmem_limit_bytes=VMEM),
        cost_estimate=cost(2),
        name="join_sum",
    )(left, own, received, *deps)


def advance(chains, *deps):
    tasks = [chain.tasks.pop(0) for chain in chains]
    parts = [chain.parts for chain in chains]
    shapes = []
    for task, part in zip(tasks, parts):
        rows, columns = part[0].shape[-2:]
        made = {"deal": [rows // 2 * len(part)] * 2, "whole": [rows * len(part)], "sum": [rows]}[task]
        shapes.append([jax.ShapeDtypeStruct((size, columns), LOW) for size in made])
    counts = [len(part) for part in parts]
    me = lax.axis_index("seq")
    high = (me // QUAD % 2).astype(jnp.int32)[None]

    def kernel(high, *refs):
        ins = list(refs[: sum(counts)])
        outs = list(refs[len(refs) - sum(len(shape) for shape in shapes) :])
        for task, count in zip(tasks, counts):
            refs = [ins.pop(0) for _ in range(count)]
            if task == "deal":
                half = refs[0].shape[1] // 2
                for block in (high[0], 1 - high[0]):
                    place = pl.ds(pl.multiple_of(block * half, half), half)
                    out = outs.pop(0)
                    for i, ref in enumerate(refs):
                        out[i * half : (i + 1) * half, :] = sum(
                            ref[k, place, :].astype(FULL) for k in range(QUAD)
                        ).astype(LOW)
            elif task == "whole":
                out = outs.pop(0)
                rows = refs[0].shape[1]
                for i, ref in enumerate(refs):
                    out[i * rows : (i + 1) * rows, :] = sum(ref[k].astype(FULL) for k in range(QUAD)).astype(LOW)
            else:
                outs.pop(0)[...] = (refs[0][...].astype(FULL) + refs[1][...].astype(FULL)).astype(LOW)

    here, anywhere = pl.BlockSpec(memory_space=pltpu.VMEM), pl.BlockSpec(memory_space=pl.ANY)
    results = list(
        pl.pallas_call(
            kernel,
            in_specs=[pl.BlockSpec(memory_space=pltpu.SMEM)] + [here] * sum(counts) + [anywhere] * len(deps),
            out_specs=[here] * sum(len(shape) for shape in shapes),
            out_shape=[one for shape in shapes for one in shape],
            compiler_params=pltpu.CompilerParams(vmem_limit_bytes=VMEM),
            cost_estimate=cost(2),
            name="advance",
        )(high, *[array for part in parts for array in part], *deps)
    )
    rest = list(results)
    for task, chain, shape in zip(tasks, chains, shapes):
        chain.accept(task, [rest.pop(0) for _ in shape])
    return results


def finish(groups, slot, slots, columns, first, row_turn, half_turn, column_turn, outputs=1):
    rows = groups[0][0].shape[0] // slots
    width = columns // 4
    skip = first // (2 * width)
    me = lax.axis_index("seq")
    high = me // QUAD % 2
    scalars = jnp.stack([(me & (QUAD - 1)) ^ row_turn, half_turn, column_turn, high]).astype(jnp.int32)
    count = len(groups)

    def kernel(scalars, *refs):
        ins, outs = refs[: count * QUAD], refs[-outputs:]

        def put(out):
            for k in range(count):
                for q in range(QUAD):
                    block = (scalars[0] ^ q) * count
                    if count == 2:
                        block = block + (scalars[3] ^ k)
                    target = pl.ds(pl.multiple_of(block * rows, rows), rows)
                    ref = ins[k * QUAD + q]
                    for e in range(2):
                        place = pl.ds(pl.multiple_of((e ^ scalars[2]) * width, width), width)
                        out[target, place] = ref[:, e * width : (e + 1) * width].astype(FULL)

        if outputs == 1:
            put(outs[0])
        else:
            for k in range(2):
                pl.when(pl.program_id(0) == k)(lambda k=k: put(outs[k]))

    return pl.pallas_call(
        kernel,
        grid_spec=pltpu.PrefetchScalarGridSpec(
            num_scalar_prefetch=1,
            grid=(2,),
            in_specs=[pl.BlockSpec((rows, 2 * width), lambda half, n: (slot, half + skip))] * (count * QUAD),
            out_specs=[
                pl.BlockSpec(
                    (count * QUAD * rows, 2 * width),
                    (lambda half, n: (0, half ^ n[1])) if outputs == 1 else (lambda half, n: (0, 0)),
                )
            ]
            * outputs,
        ),
        out_shape=[jax.ShapeDtypeStruct((count * QUAD * rows, columns // outputs), FULL)] * outputs,
        compiler_params=pltpu.CompilerParams(vmem_limit_bytes=VMEM),
        cost_estimate=cost(3),
        name="finish",
    )(scalars, *[part for group in groups for part in group])


def cost(us):
    return pl.CostEstimate(flops=0, bytes_accessed=int(us * SCALE), transcendentals=0)


def pair(re, im):
    return jnp.concatenate([re, im], axis=-1)


def factor(re, im):
    return pair(re, re), pair(-im, im)


def times(x, first, second):
    lanes = x.shape[-1]
    return x * first + pltpu.roll(x, lanes // 2, x.ndim - 1) * second


def cmul(a, b):
    return a[0] * b[0] - a[1] * b[1], a[0] * b[1] + a[1] * b[0]


def add(a, b):
    return a[0] + b[0], a[1] + b[1]


def scale(a, k):
    return a[0] * k, a[1] * k


BBAR, READ, CARRY, STRIDE, KERNEL, Z, RATIO, C, B, A_PART, STEP = 0, 2, 4, 10, 18, 19, 21, 23, 25, 27, 29
ROWS = 30


def less_one(x):
    total = 1.0 + x / 8.0
    for k in (7.0, 6.0, 5.0, 4.0, 3.0, 2.0):
        total = 1.0 + x / k * total
    return jnp.where(x > -0.25, x * total, jnp.exp(x) - 1.0)


def consts_kernel(block, decay_ref, freq_ref, b_ref, c_ref, step_ref, consts, base):
    states, width = decay_ref.shape
    lanes = 2 * states

    def wide(x):
        return jnp.concatenate([x, x], axis=0).T

    decay, freq = wide(decay_ref[...]), wide(freq_ref[...])
    b = (wide(b_ref[0]), wide(b_ref[1]))
    c = (wide(c_ref[0]), wide(c_ref[1]))
    step = jnp.broadcast_to(step_ref[...], (lanes, width)).T
    first = lax.broadcasted_iota(jnp.int32, (width, lanes), 1) < states
    rate = step * decay
    turn = step * freq
    size = jnp.exp(-rate)
    z = (size * jnp.cos(turn), size * jnp.sin(turn))
    half_turn = jnp.sin(0.5 * turn)
    less = (less_one(-rate) * jnp.cos(turn) - 2.0 * half_turn * half_turn, z[1])
    modulus = decay * decay + freq * freq
    ratio = (
        (freq * less[1] - decay * less[0]) / modulus,
        -(decay * less[1] + freq * less[0]) / modulus,
    )
    bbar = cmul(ratio, b)
    twice_c = scale(c, 2.0)

    def put_factor(k, x):
        consts[k] = x[0]
        consts[k + 1] = jnp.where(first, -x[1], x[1])

    def put_plain(k, x):
        consts[k] = x[0]
        consts[k + 1] = x[1]

    put_factor(BBAR, bbar)
    put_factor(READ, cmul(twice_c, z))
    kernel = cmul(twice_c, bbar)
    consts[KERNEL] = jnp.where(first, kernel[0], -kernel[1])
    put_plain(Z, z)
    put_plain(RATIO, ratio)
    put_plain(C, c)
    put_plain(B, b)
    consts[A_PART] = decay
    consts[A_PART + 1] = freq
    consts[STEP] = step
    power = (jnp.ones_like(size), jnp.zeros_like(size))
    for k in range(8):
        base[k] = jnp.where(first, power[0], power[1])
        power = cmul(power, z)
    k = 8
    while k < 4 * block:
        if k <= 64:
            put_factor(STRIDE + 2 * (k.bit_length() - 4), power)
        if k >= block:
            put_factor(CARRY + 2 * ((k // block).bit_length() - 1), power)
        power = cmul(power, power)
        k *= 2
    put_factor(CARRY + 4, power)


def s4_consts(a_decay, a_freq, b_state, c_state, step_size, block):
    states, width = a_decay.shape
    return pl.pallas_call(
        lambda *refs: consts_kernel(block, *refs),
        out_shape=[
            jax.ShapeDtypeStruct((ROWS, width, 2 * states), FULL),
            jax.ShapeDtypeStruct((8, width, 2 * states), FULL),
        ],
        compiler_params=pltpu.CompilerParams(vmem_limit_bytes=VMEM),
        cost_estimate=cost(6),
        name="s4_consts",
    )(a_decay, a_freq, b_state, c_state, step_size[None, :])


def half_turned(x):
    return pltpu.roll(x, x.shape[-1] // 2, x.ndim - 1)


def high_low(x):
    high = x.astype(LOW)
    return high, (x - high.astype(FULL)).astype(LOW)


def dot(a, b):
    return lax.dot_general(a, b, (((1,), (0,)), ((), ())), preferred_element_type=FULL)


def dot_t(a, b):
    return lax.dot_general(a, b, (((1,), (1,)), ((), ())), preferred_element_type=FULL)


def tables_kernel(base, consts, *refs):
    z_out, h_out = refs[-2:]
    channels, _, lanes = z_out.shape
    row8 = lax.broadcasted_iota(jnp.int32, (8, lanes), 0)
    row = lax.broadcasted_iota(jnp.int32, (lanes, lanes), 0)
    lane = lax.broadcasted_iota(jnp.int32, (lanes, lanes), 1)
    live = row + lane >= lanes - 1

    def one(c):
        first = jnp.concatenate([base[k, pl.ds(c, 1), :] for k in range(8)], axis=0)
        tiles = [(first, half_turned(first))]
        for level in range(4):
            k = STRIDE + 2 * level
            a, b = consts[k, pl.ds(c, 1), :], consts[k + 1, pl.ds(c, 1), :]
            tiles += [(t * a + u * b, u * a - t * b) for t, u in tiles]
        z = jnp.concatenate([t for t, _ in tiles], axis=0)
        high, low = high_low(z)
        z_out[c, :lanes, :] = high
        z_out[c, lanes:, :] = low
        f_high, f_low = high_low(jnp.broadcast_to(consts[KERNEL, pl.ds(c, 1), :], (8, lanes)))
        h = dot_t(jnp.concatenate([f_high, f_low], axis=0), high)
        h = h[:8] + h[8:] + dot_t(f_high, low)
        for bit in (1, 2, 4):
            h = jnp.where((7 - row8) & bit != 0, pltpu.roll(h, bit, 1), h)
        hankel = [pltpu.roll(h, lanes - 8 - k, 1) if k < lanes - 8 else h for k in range(0, lanes, 8)]
        hankel = jnp.concatenate(hankel, axis=0)
        h_out[c] = jnp.where(live, hankel, 0.0).astype(LOW)

    @pl.loop(0, channels, step=UNROLL)
    def _(c):
        for k in range(UNROLL):
            one(c + k)


def s4_tables(base, consts, part, parts, tables=(), deps=()):
    _, width, lanes = base.shape
    steps = width // CHANNELS // parts
    skip = part * steps
    anywhere = pl.BlockSpec(memory_space=pl.ANY)
    return pl.pallas_call(
        tables_kernel,
        grid=(steps,),
        in_specs=[
            pl.BlockSpec((8, CHANNELS, lanes), lambda i: (0, i + skip, 0)),
            pl.BlockSpec((ROWS, CHANNELS, lanes), lambda i: (0, i + skip, 0)),
        ]
        + [anywhere] * (len(tables) + len(deps)),
        out_specs=[
            pl.BlockSpec((CHANNELS, 2 * lanes, lanes), lambda i: (i + skip, 0, 0)),
            pl.BlockSpec((CHANNELS, lanes, lanes), lambda i: (i + skip, 0, 0)),
        ],
        out_shape=[
            jax.ShapeDtypeStruct((width, 2 * lanes, lanes), LOW),
            jax.ShapeDtypeStruct((width, lanes, lanes), LOW),
        ],
        input_output_aliases={2: 0, 3: 1} if tables else {},
        compiler_params=pltpu.CompilerParams(vmem_limit_bytes=VMEM),
        cost_estimate=cost(24 / parts),
        name="s4_tables",
    )(base, consts, *tables, *deps)


def flip_matrix(size):
    row = lax.broadcasted_iota(jnp.int32, (size, size), 0)
    lane = lax.broadcasted_iota(jnp.int32, (size, size), 1)
    return (row + lane == size - 1).astype(FULL).astype(LOW)


def rows_of_channels(consts, k):
    return jnp.stack([consts[k, c : c + 1, :] for c in range(consts.shape[1])])


def weighted_ends(x, place, z):
    high, low = high_low(x * place)
    x = x.astype(LOW)
    none = jnp.zeros_like(x)
    left = jnp.concatenate([x, high, low, none], axis=0)
    right = jnp.concatenate([x, high, none, none], axis=0)
    ends = dot(jnp.concatenate([left, right], axis=1), z)
    count = x.shape[0]
    return ends[:count], ends[count : 2 * count] + ends[2 * count : 3 * count]


def times_both(x, consts, k):
    first, second = rows_of_channels(consts, k), rows_of_channels(consts, k + 1)
    return x[0] * first + x[1] * second, x[1] * first - x[0] * second


def scan_blocks(x, consts, row, reverse):
    count = x[0].shape[1]
    for level, d in enumerate((1, 2, 4)):
        live = row < count - d if reverse else row >= d
        moved = [jnp.where(live, pltpu.roll(e, count - d if reverse else d, 1), 0.0) for e in x]
        x = add(x, times_both(moved, consts, CARRY + 2 * level))
    return x


def forward_kernel(
    signal, skip, consts, z, m, init, activ, slope, x_out, p_out, q_out, s_out, x_scr, y_scr
):
    step = pl.program_id(0)
    channels, _, lanes = z.shape
    count = signal.shape[0] // lanes
    width = signal.shape[1]

    @pl.when(step == 0)
    def _():
        flip = flip_matrix(lanes)
        for j in range(count):
            x_scr[pl.ds(j, width, stride=count), :] = dot(flip, signal[j * lanes : (j + 1) * lanes, :]).T

    rows = pl.ds(pl.multiple_of(step * channels * count, channels * count), channels * count)
    x = x_scr[rows, :].reshape(channels, count, lanes)
    place = lax.broadcasted_iota(jnp.int32, (count, lanes), 1).astype(FULL)
    row = lax.broadcasted_iota(jnp.int32, (channels, count, lanes), 1)
    plus = lax.broadcasted_iota(jnp.int32, (channels, count, lanes), 2) < lanes // 2
    ends = [weighted_ends(x[c], place, z[c]) for c in range(channels)]
    p = jnp.stack([e[0] for e in ends])
    q = jnp.stack([e[1] for e in ends])
    start = init[...][:, None, :]
    state = times_both((p, half_turned(p)), consts, BBAR)
    state = [
        jnp.where(row == 0, e, pltpu.roll(s, 1, 1)) for e, s in zip((start, half_turned(start)), state)
    ]
    state = scan_blocks(state, consts, row, False)
    read, _ = times_both(state, consts, READ)
    read = jnp.where(plus, read, -read).astype(LOW)
    y = [dot(x[c].astype(LOW), m[c]) + dot_t(read[c], z[c, :lanes, :]) for c in range(channels)]
    y_scr[rows, :] = jnp.concatenate(y, axis=0)
    x_out[...] = x
    p_out[...] = p
    q_out[...] = q
    s_out[...] = state[0]

    @pl.when(step == pl.num_programs(0) - 1)
    def _():
        for j in range(count):
            part = slice(j * lanes, (j + 1) * lanes)
            mixed = y_scr[pl.ds(j, width, stride=count), :].T + skip[...] * signal[part, :].astype(FULL)
            inner = 0.7978845608028654 * (mixed + 0.044715 * mixed * mixed * mixed)
            bent = jnp.tanh(inner)
            activ[part, :] = (0.5 * mixed * (1.0 + bent)).astype(LOW)
            slope[part, :] = 0.5 * (1.0 + bent) + 0.5 * mixed * (1.0 - bent * bent) * (
                0.7978845608028654 * (1.0 + 3 * 0.044715 * mixed * mixed)
            )


def s4_forward(signal, skip, consts, z, m, init):
    tokens, width = signal.shape
    lanes = z.shape[-1]
    count = tokens // lanes
    whole = pl.BlockSpec((tokens, width), lambda i: (0, 0))
    by_channel = pl.BlockSpec((CHANNELS, count, lanes), lambda i: (i, 0, 0))
    per_channel = jax.ShapeDtypeStruct((width, count, lanes), FULL)
    return pl.pallas_call(
        forward_kernel,
        grid=(width // CHANNELS,),
        in_specs=[
            whole,
            pl.BlockSpec((1, width), lambda i: (0, 0)),
            pl.BlockSpec((ROWS, CHANNELS, lanes), lambda i: (0, i, 0)),
            pl.BlockSpec((CHANNELS, 2 * lanes, lanes), lambda i: (i, 0, 0)),
            pl.BlockSpec((CHANNELS, lanes, lanes), lambda i: (i, 0, 0)),
            pl.BlockSpec((CHANNELS, lanes), lambda i: (i, 0)),
        ],
        out_specs=[whole, whole] + [by_channel] * 4,
        out_shape=[
            jax.ShapeDtypeStruct((tokens, width), LOW),
            jax.ShapeDtypeStruct((tokens, width), FULL),
        ]
        + [per_channel] * 4,
        scratch_shapes=[pltpu.VMEM((width * count, lanes), FULL)] * 2,
        compiler_params=pltpu.CompilerParams(vmem_limit_bytes=VMEM),
        cost_estimate=cost(18),
        name="s4_forward",
    )(signal, skip, consts, z, m, init)


def backward_kernel(grads, consts, z, m, init, *refs):
    out, g_out, u_out, v_out, h_out, g_scr, y_scr = refs[-7:]
    step = pl.program_id(0)
    channels, _, lanes = z.shape
    count = grads.shape[0] // lanes
    width = grads.shape[1]

    @pl.when(step == 0)
    def _():
        for j in range(count):
            g_scr[pl.ds(j, width, stride=count), :] = grads[j * lanes : (j + 1) * lanes, :].astype(FULL).T

    rows = pl.ds(pl.multiple_of(step * channels * count, channels * count), channels * count)
    g = g_scr[rows, :].reshape(channels, count, lanes)
    place = lax.broadcasted_iota(jnp.int32, (count, lanes), 1).astype(FULL)
    row = lax.broadcasted_iota(jnp.int32, (channels, count, lanes), 1)
    plus = lax.broadcasted_iota(jnp.int32, (channels, count, lanes), 2) < lanes // 2
    ends = [weighted_ends(g[c], place, z[c]) for c in range(channels)]
    u = jnp.stack([e[0] for e in ends])
    v = jnp.stack([e[1] for e in ends])
    start = init[...][:, None, :]
    later = times_both((u, half_turned(u)), consts, READ)
    later = [
        jnp.where(row == count - 1, e, pltpu.roll(s, count - 1, 1))
        for e, s in zip((start, half_turned(start)), later)
    ]
    later = scan_blocks(later, consts, row, True)
    write, _ = times_both(later, consts, BBAR)
    write = jnp.where(plus, write, -write).astype(LOW)
    y = [dot(g[c].astype(LOW), m[c]) + dot_t(write[c], z[c, :lanes, :]) for c in range(channels)]
    y_scr[rows, :] = jnp.concatenate(y, axis=0)
    g_out[...] = g
    u_out[...] = u
    v_out[...] = v
    h_out[...] = later[0]

    @pl.when(step == pl.num_programs(0) - 1)
    def _():
        flip = flip_matrix(lanes)
        for j in range(count):
            out[j * lanes : (j + 1) * lanes, :] = dot(
                flip, y_scr[pl.ds(j, width, stride=count), :].T.astype(LOW)
            )


def s4_backward(grads, consts, z, m, init, deps=()):
    tokens, width = grads.shape
    lanes = z.shape[-1]
    count = tokens // lanes
    whole = pl.BlockSpec((tokens, width), lambda i: (0, 0))
    by_channel = pl.BlockSpec((CHANNELS, count, lanes), lambda i: (i, 0, 0))
    per_channel = jax.ShapeDtypeStruct((width, count, lanes), FULL)
    return pl.pallas_call(
        backward_kernel,
        grid=(width // CHANNELS,),
        in_specs=[
            whole,
            pl.BlockSpec((ROWS, CHANNELS, lanes), lambda i: (0, i, 0)),
            pl.BlockSpec((CHANNELS, 2 * lanes, lanes), lambda i: (i, 0, 0)),
            pl.BlockSpec((CHANNELS, lanes, lanes), lambda i: (i, 0, 0)),
            pl.BlockSpec((CHANNELS, lanes), lambda i: (i, 0)),
        ]
        + [pl.BlockSpec(memory_space=pl.ANY)] * len(deps),
        out_specs=[whole] + [by_channel] * 4,
        out_shape=[jax.ShapeDtypeStruct((tokens, width), FULL)] + [per_channel] * 4,
        scratch_shapes=[pltpu.VMEM((width * count, lanes), FULL)] * 2,
        compiler_params=pltpu.CompilerParams(vmem_limit_bytes=VMEM),
        cost_estimate=cost(18),
        name="s4_backward",
    )(grads, consts, z, m, init, *deps)


def sums_kernel(block, x, g, p, q, s, u, v, h, z, consts, *refs):
    out = refs[-1]
    channels, count, lanes = x.shape
    states = lanes // 2
    row8 = lax.broadcasted_iota(jnp.int32, (8, lanes), 0)
    row = lax.broadcasted_iota(jnp.int32, (lanes, lanes), 0)
    lane = lax.broadcasted_iota(jnp.int32, (lanes, lanes), 1)
    place = lax.broadcasted_iota(jnp.int32, (8, lanes), 1).astype(FULL)
    live = row + lane >= lanes - 1
    first = lax.broadcasted_iota(jnp.int32, (channels, lanes), 1) < states
    w = []
    for c in range(channels):
        both = lax.dot_general(
            x[c].astype(LOW), g[c].astype(LOW), (((0,), (0,)), ((), ())), preferred_element_type=FULL
        )
        both = jnp.where(live, both, 0.0)
        tiles = [both[k : k + 8, :] for k in range(0, lanes, 8)]
        shift = 8
        while len(tiles) > 1:
            tiles = [a + pltpu.roll(b, shift, 1) for a, b in zip(tiles[::2], tiles[1::2])]
            shift *= 2
        total = pltpu.roll(tiles[0], 1, 1)
        for bit in (1, 2, 4):
            total = jnp.where(row8 & bit != 0, pltpu.roll(total, bit, 1), total)
        high, low = high_low(total)
        place_high, place_low = high_low(total * place)
        none = jnp.zeros_like(high)
        left = jnp.concatenate([high, low, place_high, place_low], axis=0)
        right = jnp.concatenate([high, none, place_high, none], axis=0)
        w.append(dot(jnp.concatenate([left, right], axis=1), z[c]))
    lag0 = jnp.sum(jnp.stack([e[:16] for e in w]), axis=1)
    lag1 = jnp.sum(jnp.stack([e[16:] for e in w]), axis=1)

    def both_halves(x):
        turned = half_turned(x)
        return jnp.where(first, x, turned), jnp.where(first, turned, x)

    def product(a, b):
        plain = jnp.sum(a * b, axis=1)
        crossed = jnp.sum(a * half_turned(b), axis=1)
        plain = jnp.where(first, plain, -plain)
        return plain + half_turned(plain), crossed + half_turned(crossed)

    states_read = product(u[...], s[...])
    slopes_read = product(u[...] + v[...], s[...])
    writes = product(h[...], p[...])
    slopes_write = product(h[...], q[...])
    carried = product(h[...], s[...])
    lag0, lag1 = both_halves(lag0), both_halves(lag1)

    def const(k):
        return consts[k]

    def const_factor(k):
        second = const(k + 1)
        return const(k), jnp.where(first, -second, second)

    bbar, read, carry = const_factor(BBAR), const_factor(READ), const_factor(CARRY)
    z_one, ratio = (const(Z), const(Z + 1)), (const(RATIO), const(RATIO + 1))
    c, b = (const(C), const(C + 1)), (const(B), const(B + 1))
    decay, freq, step = const(A_PART), const(A_PART + 1), const(STEP)
    modulus = decay * decay + freq * freq
    over_a = (-decay / modulus, -freq / modulus)
    to_c = scale(add(cmul(z_one, states_read), cmul(bbar, lag0)), 2.0)
    to_bbar = add(writes, scale(cmul(c, lag0), 2.0))
    to_log = add(
        add(cmul(read, slopes_read), cmul(bbar, slopes_write)),
        add(scale(cmul(carry, carried), float(block)), scale(cmul(cmul(c, bbar), lag1), 2.0)),
    )
    to_b = cmul(to_bbar, ratio)
    over = cmul(cmul(to_bbar, b), over_a)
    to_log = add(to_log, cmul(over, z_one))
    to_a = cmul(over, ratio)
    grad_decay = to_a[0] - step * to_log[0]
    grad_freq = to_a[1] - step * to_log[1]
    grad_step = jnp.where(first, -to_log[0] * decay, -to_log[1] * freq)
    out[0] = jnp.where(first, grad_decay, grad_freq)
    out[1] = jnp.where(first, to_b[0], -to_b[1])
    out[2] = jnp.where(first, to_c[0], -to_c[1])
    out[3] = jnp.broadcast_to(jnp.sum(grad_step, axis=1, keepdims=True), (channels, lanes))


def s4_sums(x, g, p, q, s, u, v, h, z, consts, block, deps, skip, steps):
    width, count, lanes = x.shape
    by_channel = pl.BlockSpec((CHANNELS, count, lanes), lambda i: (i + skip, 0, 0))
    return pl.pallas_call(
        lambda *refs: sums_kernel(block, *refs),
        grid=(steps,),
        in_specs=[by_channel] * 8
        + [
            pl.BlockSpec((CHANNELS, 2 * lanes, lanes), lambda i: (i + skip, 0, 0)),
            pl.BlockSpec((ROWS, CHANNELS, lanes), lambda i: (0, i + skip, 0)),
        ]
        + [pl.BlockSpec(memory_space=pl.ANY)] * len(deps),
        out_specs=pl.BlockSpec((4, CHANNELS, lanes), lambda i: (0, i, 0)),
        out_shape=jax.ShapeDtypeStruct((4, steps * CHANNELS, lanes), FULL),
        compiler_params=pltpu.CompilerParams(vmem_limit_bytes=VMEM),
        cost_estimate=cost(18 * steps * CHANNELS / width),
        name="s4_sums",
    )(x, g, p, q, s, u, v, h, z, consts, *deps)


def split(rows):
    half = rows.shape[-1] // 2
    return rows[..., :half], rows[..., half:]


def t_dot(a, b):
    return lax.dot_general(a, b, (((0,), (0,)), ((), ())), preferred_element_type=FULL)


def layer_forward(values, gain, bias, total_width, sums=None):
    if sums is None:
        sums = sum_chan(jnp.stack([jnp.sum(values, axis=-1), jnp.sum(values * values, axis=-1)]))
    center = sums[0] / total_width
    spread_var = sums[1] / total_width - center * center
    inverse = lax.rsqrt(spread_var + EPSILON)[..., None]
    normed = (values - center[..., None]) * inverse
    return normed * gain + bias, normed, inverse


def layer_backward(grad_out, normed, inverse, gain, total_width, work):
    scaled = grad_out * gain
    sums = jnp.stack([jnp.sum(scaled, axis=-1), jnp.sum(scaled * normed, axis=-1)])
    sums = after(sum_chan(sums), *work(sums))
    grad_in = inverse * (
        scaled - sums[0][..., None] / total_width - normed * sums[1][..., None] / total_width
    )
    return grad_in, jnp.sum(grad_out * normed, axis=0), jnp.sum(grad_out, axis=0)


def body(
    block_input,
    lengths,
    norm1_gain,
    norm1_bias,
    a_decay,
    a_freq,
    b_state,
    c_state,
    step_size,
    skip_gain,
    w_value,
    b_value,
    w_gate,
    b_gate,
    norm2_gain,
    norm2_bias,
    w_up,
    b_up,
    w_down,
    b_down,
    out_grad,
):
    batch, block, width = block_input.shape
    chans = lax.axis_size("chan")
    seqs = lax.axis_size("seq")
    assert seqs % batch == 0
    runs = seqs // batch
    total_width = width * chans
    assert chans == 4
    seq_me = lax.axis_index("seq")
    chan_me = lax.axis_index("chan")
    groups = None if runs == 1 else [[r * batch + j for j in range(batch)] for r in range(runs)]
    peers = None if runs == 1 else [[r * batch + j for r in range(runs)] for j in range(batch)]

    def exchange(x):
        return lax.all_to_all(x, "seq", 0, 0, axis_index_groups=groups, tiled=True)

    def rows_of(w):
        return [
            lax.dynamic_slice_in_dim(w, (chan_me ^ d) * width, width, 0) for d in range(chans)
        ]

    moved = exchange(jnp.concatenate([block_input, out_grad], axis=-1)).reshape(batch * block, 2 * width)

    consts, base = s4_consts(a_decay, a_freq, b_state, c_state, step_size, block)
    z, m = s4_tables(base, consts, 0, 1)
    moved = after(moved, z)
    inputs = moved[:, :width].astype(FULL)
    grad_low = moved[:, width:]
    moments = sum_chan(jnp.stack([jnp.sum(inputs, axis=-1), jnp.sum(inputs * inputs, axis=-1)]))
    states = a_decay.shape[0]

    def const_factor(k):
        return consts[k, :, :states], consts[k + 1, :, states:]

    begin = (seq_me // batch) * batch * block
    places = begin + jnp.arange(batch * block, dtype=jnp.int32)
    mask = (places < lengths[seq_me % batch]).astype(FULL)[:, None]
    norm_one, normed_one, inverse_one = layer_forward(inputs, norm1_gain, norm1_bias, total_width, moments)
    signal = (mask * norm_one).astype(LOW)
    skip = skip_gain[None, :]
    init = jnp.zeros((width, 2 * states), FULL)
    if runs > 1:
        _, _, _, p, _, s = s4_forward(signal, skip, consts, z, m, init)
        carry = const_factor(CARRY)
        end = add(cmul(carry, split(s[:, -1])), cmul(const_factor(BBAR), split(p[:, -1])))
        ends = lax.all_gather(pair(*end), "seq", axis_index_groups=peers)
        hop = carry
        for _ in range(3):
            hop = cmul(hop, hop)
        for r in range(runs - 1):
            moved = add(cmul(hop, split(init)), split(ends[r]))
            init = jnp.where(r < seq_me // batch, pair(*moved), init)
    activ, slope, xs, ps, qs, ss = s4_forward(signal, skip, consts, z, m, init)

    wv, wg = rows_of(w_value), rows_of(w_gate)
    w_gated = [jnp.concatenate([a, b], axis=1) for a, b in zip(wv, wg)]
    w_ups = rows_of(w_up)
    w_downs = [
        lax.dynamic_slice_in_dim(w_down, (chan_me ^ d) * width, width, 1) for d in range(chans)
    ]
    grads = gather_pieces(grad_low)
    activs = gather_pieces(after(activ, grads[2]))
    both = sum(dot(a, w) for a, w in zip(activs, w_gated))
    value = both[:, :width] + b_value
    gate = both[:, width:] + b_gate
    opened = jax.nn.sigmoid(gate)
    resid = inputs + value * opened
    norm_two, normed_two, inverse_two = layer_forward(resid, norm2_gain, norm2_bias, total_width)
    norms = gather_pieces(norm_two.astype(LOW))
    hidden = sum(dot(a, w) for a, w in zip(norms, w_ups)) + b_up
    spread, gelu_pull = jax.vjp(jax.nn.gelu, hidden)
    spread = spread.astype(LOW)

    grad_out = grad_low.astype(FULL)
    grad_spread = sum(dot_t(a, w) for a, w in zip(grads, w_downs))
    grad_hidden = gelu_pull(grad_spread)[0].astype(LOW)
    grad_w_down = t_dot(after(spread, grad_hidden), jnp.concatenate(grads, axis=1)).astype(LOW)
    downs_dealt = deal(grad_w_down)
    marks = []
    hidden_late = after(grad_hidden, grad_w_down)
    grad_norm_two = reduce_pieces([dot_t(hidden_late, w) for w in w_ups], marks)
    grad_w_up = t_dot(jnp.concatenate(norms, axis=1), after(grad_hidden, *marks[:2])).astype(LOW)
    grad_norm_two = after(grad_norm_two, grad_w_up)
    chains = []

    def start_ups(dep):
        chains.append(Chain([downs_dealt, deal(after(grad_w_up, dep))], True))
        return []

    grad_resid, grad_norm2_gain, grad_norm2_bias = layer_backward(
        grad_norm_two, normed_two, inverse_two, norm2_gain, total_width, start_ups
    )
    wide_chain = chains[0]
    grad_resid = grad_out + grad_resid
    grad_value = (grad_resid * opened).astype(LOW)
    grad_gate = (grad_resid * value * opened * (1.0 - opened)).astype(LOW)
    grad_both = jnp.concatenate([grad_value, grad_gate], axis=1)
    marks = []
    grad_activ = reduce_pieces([dot_t(grad_both, w) for w in w_gated], marks)
    grad_w_gated = t_dot(jnp.concatenate(activs, axis=1), after(grad_both, *marks[:2])).astype(LOW)
    gated_chain = Chain([deal(after(grad_w_gated, grad_activ))], False)
    grad_activ = after(grad_activ, grad_w_gated)
    grad_mixed = (grad_activ * slope).astype(LOW)
    made = advance([wide_chain], grad_mixed)
    init = jnp.zeros((width, 2 * states), FULL)
    if runs > 1:
        _, _, u, _, h = s4_backward(grad_mixed, consts, z, m, init)
        end = add(cmul(carry, split(h[:, 0])), cmul(const_factor(READ), split(u[:, 0])))
        ends = lax.all_gather(pair(*end), "seq", axis_index_groups=peers)
        for r in reversed(range(1, runs)):
            moved = add(cmul(hop, split(init)), split(ends[r]))
            init = jnp.where(r > seq_me // batch, pair(*moved), init)
    grad_signal, gs, us, vs, hs = s4_backward(grad_mixed, consts, z, m, init, made)
    grad_signal = after(grad_signal, *advance([wide_chain, gated_chain], grad_signal))
    grad_signal = grad_signal + skip * grad_mixed.astype(FULL)
    s4_parts = (xs, gs, ps, qs, ss, us, vs, hs, z, consts, block)
    grad_input, grad_norm1_gain, grad_norm1_bias = layer_backward(
        grad_signal * mask, normed_one, inverse_one, norm1_gain, total_width, lambda dep: []
    )
    grad_input = (grad_resid + grad_input).astype(LOW)
    wide_own = gather(wide_chain.parts[0])
    sums = s4_sums(*s4_parts, [grad_input], 0, width // CHANNELS)
    grad_input_moved = exchange(grad_input.reshape(batch, block, width))
    made = join_sum(wide_chain.parts[1], *gated_chain.parts, [sums, *wide_own[1:]])
    last = gather(made)
    grad_input = grad_input_moved.astype(FULL)
    narrow = jnp.concatenate(
        [
            grad_norm1_gain,
            grad_norm1_bias,
            jnp.sum(grad_mixed.astype(FULL) * signal.astype(FULL), axis=0),
            jnp.sum(grad_value.astype(FULL), axis=0),
            jnp.sum(grad_gate.astype(FULL), axis=0),
            grad_norm2_gain,
            grad_norm2_bias,
            jnp.sum(grad_out, axis=0),
            sums[3, :, 0],
            jnp.sum(grad_hidden.astype(FULL), axis=0),
        ]
    )
    wide, narrow, packed = sum_small(sums, narrow, [made, grad_input_moved], last[1:])
    wide = wide.transpose(0, 2, 1)
    spread_late = after(spread, made)
    output = reduce_pieces([dot(spread_late, w) for w in w_downs])
    output = exchange((resid + output + b_down).astype(LOW).reshape(batch, block, width))
    vectors = [narrow[k * width : (k + 1) * width] for k in range(9)]
    vectors.insert(2, vectors.pop(8))

    zero = 0 * chan_me
    (down,) = finish([wide_own, last], 0, 2, total_width, 0, zero, chan_me >> 1, chan_me & 1)
    (up,) = finish([wide_own, last], 1, 2, grad_w_up.shape[1], 0, chan_me, zero, zero)
    grad_w_value, grad_w_gate = finish([last], 0, 1, 2 * width, total_width, chan_me, zero, zero, 2)
    return (
        output,
        grad_input,
        vectors[0],
        vectors[1],
        wide[0, :states],
        wide[0, states:],
        wide[1].reshape(2, states, width),
        wide[2].reshape(2, states, width),
        vectors[2],
        vectors[3],
        grad_w_value,
        vectors[4],
        grad_w_gate,
        vectors[5],
        vectors[6],
        vectors[7],
        up,
        narrow[9 * width :],
        down,
        vectors[8],
    )


def solution(mesh):
    in_specs = (
        P(None, "seq", "chan"),
        P(),
        P("chan"),
        P("chan"),
        P(None, "chan"),
        P(None, "chan"),
        P(None, None, "chan"),
        P(None, None, "chan"),
        P("chan"),
        P("chan"),
        P(None, "chan"),
        P("chan"),
        P(None, "chan"),
        P("chan"),
        P("chan"),
        P("chan"),
        P(None, "chan"),
        P("chan"),
        P("chan", None),
        P("chan"),
        P(None, "seq", "chan"),
    )
    out_specs = (
        P(None, "seq", "chan"),
        P(None, "seq", "chan"),
        P("chan"),
        P("chan"),
        P(None, "chan"),
        P(None, "chan"),
        P(None, None, "chan"),
        P(None, None, "chan"),
        P("chan"),
        P("chan"),
        P(None, "chan"),
        P("chan"),
        P(None, "chan"),
        P("chan"),
        P("chan"),
        P("chan"),
        P(None, "chan"),
        P("chan"),
        P("chan", None),
        P("chan"),
    )
    return jax.shard_map(body, mesh=mesh, in_specs=in_specs, out_specs=out_specs, check_vma=False)
```

```python
import jax
import jax.numpy as jnp
from jax import lax
from jax.experimental import pallas as pl
from jax.experimental.pallas import tpu as pltpu
from jax.sharding import PartitionSpec as P

EPSILON = 1e-05
LOW = jnp.bfloat16
FULL = jnp.float32
CHANNELS = 32
UNROLL = 16
SCALE = 1.0e5
VMEM = 56 * 1024 * 1024


def swap(x, axis, distance):
    return lax.ppermute(x, axis, [(i, i ^ distance) for i in range(lax.axis_size(axis))])


def axis_bits(axis):
    size = lax.axis_size(axis)
    bits = size.bit_length() - 1
    assert size == 1 << bits
    return bits


def gather_pieces(x):
    pieces = {0: x}
    for bit in reversed(range(axis_bits("chan"))):
        for d in list(pieces):
            pieces[d ^ (1 << bit)] = swap(pieces[d], "chan", 1 << bit)
    return [pieces[d] for d in range(len(pieces))]


def reduce_pieces(parts, marks=None):
    sums = dict(enumerate(parts))
    for bit in range(axis_bits("chan")):
        if marks is not None and bit == axis_bits("chan") - 1:
            marks += [sums[1 << bit], sums[0]]
        for d in sorted(sums, reverse=True):
            if d >> bit & 1:
                received = swap(sums.pop(d).astype(LOW), "chan", 1 << bit)
                if marks is not None and d == 1 << (axis_bits("chan") - 1):
                    marks.append(received)
                sums[d ^ (1 << bit)] = sums[d ^ (1 << bit)] + received.astype(FULL)
    return sums[0]


def sum_chan(x):
    return x + sum(swap(x, "chan", d) for d in range(1, lax.axis_size("chan")))


def after(x, *others):
    return lax.optimization_barrier((x, others))[0]


def exchange_all(x):
    return lax.all_to_all(x, "seq", 0, 0, tiled=True)


def small_shares(sums, size):
    seqs = lax.axis_size("seq")
    groups, width, lanes = sums.shape
    short = -(-size // (seqs * lanes))
    assert short <= 8
    share = (groups - 1) * width // seqs
    return share, short, -(-(share + 16) // 16) * 16


def pack_small(sums, narrow):
    seqs = lax.axis_size("seq")
    groups, width, lanes = sums.shape
    size = narrow.shape[0]
    share, short, rows = small_shares(sums, size)
    narrow_rows = jnp.pad(narrow, (0, seqs * short * lanes - size)).reshape(seqs, short, lanes)
    narrow_rows = jnp.pad(narrow_rows, ((0, 0), (0, 8 - short), (0, 0)))

    def pack(sums, narrow, packed):
        flat = sums[: groups - 1].reshape((groups - 1) * width, lanes)
        for k in range(seqs):
            part = narrow[k]
            high = part.astype(LOW).astype(FULL)
            pieces = [flat[k * share : (k + 1) * share], high, part - high]
            if rows > share + 16:
                pieces.append(jnp.zeros((rows - share - 16, lanes), FULL))
            packed[k] = jnp.concatenate(pieces, axis=0).astype(LOW)

    shape = jax.ShapeDtypeStruct((seqs, rows, lanes), LOW)
    return call_here(pack, [sums, narrow_rows], [], [shape], "pack_small")[0]


def sum_small(dealt, sums, size, deps):
    seqs, rows, lanes = dealt.shape
    groups, width, _ = sums.shape
    share, short, _ = small_shares(sums, size)

    def add(dealt, out):
        total = sum(dealt[k].astype(FULL) for k in range(seqs))
        narrow = total[share : share + 8] + total[share + 8 : share + 16]
        high = narrow.astype(LOW).astype(FULL)
        pieces = [total[:share], high, narrow - high] + ([total[share + 16 :]] if rows > share + 16 else [])
        total = jnp.concatenate(pieces, axis=0).astype(LOW)
        for k in range(seqs):
            out[k] = total

    parts = exchange_all(call_here(add, [dealt], deps, [jax.ShapeDtypeStruct(dealt.shape, LOW)], "sum_small")[0])
    states = lanes // 2

    def unpack(parts, decay, freq, b, c, narrow):
        flat = jnp.concatenate([parts[k, :share, :].astype(FULL) for k in range(seqs)], axis=0)
        a, b_both, c_both = (flat[g * width : (g + 1) * width].T for g in range(3))
        decay[...], freq[...] = a[:states], a[states:]
        b[0], b[1] = b_both[:states], b_both[states:]
        c[0], c[1] = c_both[:states], c_both[states:]
        for k in range(seqs):
            part = parts[k].astype(FULL)
            narrow[k] = part[share : share + 8] + part[share + 8 : share + 16]

    one, two = (states, width), (2, states, width)
    *wide, narrow = call_here(
        unpack,
        [parts],
        [],
        [jax.ShapeDtypeStruct(shape, FULL) for shape in (one, one, two, two, (seqs, 8, lanes))],
        "unpack_small",
    )
    return parts, wide, narrow[:, :short].reshape(-1)[:size]


def beside(left, right, deps):
    rows, columns = left.shape

    def kernel(left, right, out):
        out[:, :columns] = left[...]
        out[:, columns:] = right[...]

    shape = jax.ShapeDtypeStruct((rows, columns + right.shape[1]), left.dtype)
    return call_here(kernel, [left, right], deps, [shape], "beside")[0]


def call_here(kernel, ins, deps, outs, name):
    here, anywhere = pl.BlockSpec(memory_space=pltpu.VMEM), pl.BlockSpec(memory_space=pl.ANY)
    return pl.pallas_call(
        lambda *refs: kernel(*refs[: len(ins)], *refs[len(ins) + len(deps) :]),
        in_specs=[here] * len(ins) + [anywhere] * len(deps),
        out_specs=[here] * len(outs),
        out_shape=outs,
        compiler_params=pltpu.CompilerParams(vmem_limit_bytes=VMEM),
        cost_estimate=cost(2),
        name=name,
    )(*ins, *deps)


QUAD = 4


def deal(x):
    seqs = lax.axis_size("seq")
    groups = [list(range(i, i + QUAD)) for i in range(0, seqs, QUAD)]
    return lax.all_to_all(x.reshape(QUAD, -1, x.shape[1]), "seq", 0, 0, axis_index_groups=groups, tiled=True)


class Chain:
    def __init__(self, parts, halves):
        self.masks = [1 << bit for bit in range(axis_bits("seq")) if 1 << bit >= QUAD]
        self.parts = parts
        self.halves = halves
        self.tasks = ["deal" if halves else "whole", "sum"]

    def accept(self, task, outs):
        if task == "deal":
            self.parts = [outs[0], swap(outs[1], "seq", self.masks[0])]
        elif task == "whole":
            self.parts = [outs[0], swap(outs[0], "seq", self.masks[0])]
        else:
            total = outs[0]
            for mask in self.masks[1:]:
                total = (total.astype(FULL) + swap(total, "seq", mask).astype(FULL)).astype(LOW)
            self.parts = [total]
            if self.halves:
                self.parts.append(swap(total, "seq", self.masks[0]))


def gather(part):
    return [part] + [swap(part, "seq", mask) for mask in range(1, QUAD)]


def gather_relayed(part):
    first, second = swap(part, "seq", 1), swap(part, "seq", 2)
    half = part.shape[0] // 2
    third = jnp.concatenate([swap(second[:half], "seq", 1), swap(first[half:], "seq", 2)])
    return [part, first, second, third]


def join_sum(left, own, received, deps):
    rows, columns = left.shape

    def kernel(left, own, received, *refs):
        out = refs[-1]
        out[:, :columns] = left[...]
        out[:, columns:] = (own[...].astype(FULL) + received[...].astype(FULL)).astype(LOW)

    here, anywhere = pl.BlockSpec(memory_space=pltpu.VMEM), pl.BlockSpec(memory_space=pl.ANY)
    return pl.pallas_call(
        kernel,
        in_specs=[here] * 3 + [anywhere] * len(deps),
        out_specs=here,
        out_shape=jax.ShapeDtypeStruct((rows, columns + own.shape[1]), LOW),
        compiler_params=pltpu.CompilerParams(vmem_limit_bytes=VMEM),
        cost_estimate=cost(2),
        name="join_sum",
    )(left, own, received, *deps)


def advance(chains, *deps):
    tasks = [chain.tasks.pop(0) for chain in chains]
    parts = [chain.parts for chain in chains]
    shapes = []
    for task, part in zip(tasks, parts):
        rows, columns = part[0].shape[-2:]
        made = {"deal": [rows // 2 * len(part)] * 2, "whole": [rows * len(part)], "sum": [rows]}[task]
        shapes.append([jax.ShapeDtypeStruct((size, columns), LOW) for size in made])
    counts = [len(part) for part in parts]
    me = lax.axis_index("seq")
    high = (me // QUAD % 2).astype(jnp.int32)[None]

    def kernel(high, *refs):
        ins = list(refs[: sum(counts)])
        outs = list(refs[len(refs) - sum(len(shape) for shape in shapes) :])
        for task, count in zip(tasks, counts):
            refs = [ins.pop(0) for _ in range(count)]
            if task == "deal":
                half = refs[0].shape[1] // 2
                for block in (high[0], 1 - high[0]):
                    place = pl.ds(pl.multiple_of(block * half, half), half)
                    out = outs.pop(0)
                    for i, ref in enumerate(refs):
                        out[i * half : (i + 1) * half, :] = sum(
                            ref[k, place, :].astype(FULL) for k in range(QUAD)
                        ).astype(LOW)
            elif task == "whole":
                out = outs.pop(0)
                rows = refs[0].shape[1]
                for i, ref in enumerate(refs):
                    out[i * rows : (i + 1) * rows, :] = sum(ref[k].astype(FULL) for k in range(QUAD)).astype(LOW)
            else:
                outs.pop(0)[...] = (refs[0][...].astype(FULL) + refs[1][...].astype(FULL)).astype(LOW)

    here, anywhere = pl.BlockSpec(memory_space=pltpu.VMEM), pl.BlockSpec(memory_space=pl.ANY)
    results = list(
        pl.pallas_call(
            kernel,
            in_specs=[pl.BlockSpec(memory_space=pltpu.SMEM)] + [here] * sum(counts) + [anywhere] * len(deps),
            out_specs=[here] * sum(len(shape) for shape in shapes),
            out_shape=[one for shape in shapes for one in shape],
            compiler_params=pltpu.CompilerParams(vmem_limit_bytes=VMEM),
            cost_estimate=cost(2),
            name="advance",
        )(high, *[array for part in parts for array in part], *deps)
    )
    rest = list(results)
    for task, chain, shape in zip(tasks, chains, shapes):
        chain.accept(task, [rest.pop(0) for _ in shape])
    return results


def finish(groups, slot, slots, columns, first, row_turn, half_turn, column_turn, outputs=1):
    rows = groups[0][0].shape[0] // slots
    width = columns // 4
    skip = first // (2 * width)
    me = lax.axis_index("seq")
    high = me // QUAD % 2
    scalars = jnp.stack([(me & (QUAD - 1)) ^ row_turn, half_turn, column_turn, high]).astype(jnp.int32)
    count = len(groups)

    def kernel(scalars, *refs):
        ins, outs = refs[: count * QUAD], refs[-outputs:]

        def put(out):
            for k in range(count):
                for q in range(QUAD):
                    block = (scalars[0] ^ q) * count
                    if count == 2:
                        block = block + (scalars[3] ^ k)
                    target = pl.ds(pl.multiple_of(block * rows, rows), rows)
                    ref = ins[k * QUAD + q]
                    for e in range(2):
                        place = pl.ds(pl.multiple_of((e ^ scalars[2]) * width, width), width)
                        out[target, place] = ref[:, e * width : (e + 1) * width].astype(FULL)

        if outputs == 1:
            put(outs[0])
        else:
            for k in range(2):
                pl.when(pl.program_id(0) == k)(lambda k=k: put(outs[k]))

    return pl.pallas_call(
        kernel,
        grid_spec=pltpu.PrefetchScalarGridSpec(
            num_scalar_prefetch=1,
            grid=(2,),
            in_specs=[pl.BlockSpec((rows, 2 * width), lambda half, n: (slot, half + skip))] * (count * QUAD),
            out_specs=[
                pl.BlockSpec(
                    (count * QUAD * rows, 2 * width),
                    (lambda half, n: (0, half ^ n[1])) if outputs == 1 else (lambda half, n: (0, 0)),
                )
            ]
            * outputs,
        ),
        out_shape=[jax.ShapeDtypeStruct((count * QUAD * rows, columns // outputs), FULL)] * outputs,
        compiler_params=pltpu.CompilerParams(vmem_limit_bytes=VMEM),
        cost_estimate=cost(3),
        name="finish",
    )(scalars, *[part for group in groups for part in group])


def cost(us):
    return pl.CostEstimate(flops=0, bytes_accessed=int(us * SCALE), transcendentals=0)


def pair(re, im):
    return jnp.concatenate([re, im], axis=-1)


def factor(re, im):
    return pair(re, re), pair(-im, im)


def times(x, first, second):
    lanes = x.shape[-1]
    return x * first + pltpu.roll(x, lanes // 2, x.ndim - 1) * second


def cmul(a, b):
    return a[0] * b[0] - a[1] * b[1], a[0] * b[1] + a[1] * b[0]


def add(a, b):
    return a[0] + b[0], a[1] + b[1]


def scale(a, k):
    return a[0] * k, a[1] * k


BBAR, READ, CARRY, STRIDE, KERNEL, Z, RATIO, C, B, A_PART, STEP = 0, 2, 4, 10, 18, 19, 21, 23, 25, 27, 29
ROWS = 30


def less_one(x):
    total = 1.0 + x / 8.0
    for k in (7.0, 6.0, 5.0, 4.0, 3.0, 2.0):
        total = 1.0 + x / k * total
    return jnp.where(x > -0.25, x * total, jnp.exp(x) - 1.0)


def consts_kernel(block, decay_ref, freq_ref, b_ref, c_ref, step_ref, consts, base):
    states, width = decay_ref.shape
    lanes = 2 * states

    def wide(x):
        return jnp.concatenate([x, x], axis=0).T

    decay, freq = wide(decay_ref[...]), wide(freq_ref[...])
    b = (wide(b_ref[0]), wide(b_ref[1]))
    c = (wide(c_ref[0]), wide(c_ref[1]))
    step = jnp.broadcast_to(step_ref[...], (lanes, width)).T
    first = lax.broadcasted_iota(jnp.int32, (width, lanes), 1) < states
    rate = step * decay
    turn = step * freq
    size = jnp.exp(-rate)
    z = (size * jnp.cos(turn), size * jnp.sin(turn))
    half_turn = jnp.sin(0.5 * turn)
    less = (less_one(-rate) * jnp.cos(turn) - 2.0 * half_turn * half_turn, z[1])
    modulus = decay * decay + freq * freq
    ratio = (
        (freq * less[1] - decay * less[0]) / modulus,
        -(decay * less[1] + freq * less[0]) / modulus,
    )
    bbar = cmul(ratio, b)
    twice_c = scale(c, 2.0)

    def put_factor(k, x):
        consts[k] = x[0]
        consts[k + 1] = jnp.where(first, -x[1], x[1])

    def put_plain(k, x):
        consts[k] = x[0]
        consts[k + 1] = x[1]

    put_factor(BBAR, bbar)
    put_factor(READ, cmul(twice_c, z))
    kernel = cmul(twice_c, bbar)
    consts[KERNEL] = jnp.where(first, kernel[0], -kernel[1])
    put_plain(Z, z)
    put_plain(RATIO, ratio)
    put_plain(C, c)
    put_plain(B, b)
    consts[A_PART] = decay
    consts[A_PART + 1] = freq
    consts[STEP] = step
    power = (jnp.ones_like(size), jnp.zeros_like(size))
    for k in range(8):
        base[k] = jnp.where(first, power[0], power[1])
        power = cmul(power, z)
    k = 8
    while k < 4 * block:
        if k <= 64:
            put_factor(STRIDE + 2 * (k.bit_length() - 4), power)
        if k >= block:
            put_factor(CARRY + 2 * ((k // block).bit_length() - 1), power)
        power = cmul(power, power)
        k *= 2
    put_factor(CARRY + 4, power)


def s4_consts(a_decay, a_freq, b_state, c_state, step_size, block):
    states, width = a_decay.shape
    return pl.pallas_call(
        lambda *refs: consts_kernel(block, *refs),
        out_shape=[
            jax.ShapeDtypeStruct((ROWS, width, 2 * states), FULL),
            jax.ShapeDtypeStruct((8, width, 2 * states), FULL),
        ],
        compiler_params=pltpu.CompilerParams(vmem_limit_bytes=VMEM),
        cost_estimate=cost(6),
        name="s4_consts",
    )(a_decay, a_freq, b_state, c_state, step_size[None, :])


def half_turned(x):
    return pltpu.roll(x, x.shape[-1] // 2, x.ndim - 1)


def high_low(x):
    high = x.astype(LOW)
    return high, (x - high.astype(FULL)).astype(LOW)


def dot(a, b):
    return lax.dot_general(a, b, (((1,), (0,)), ((), ())), preferred_element_type=FULL)


def dot_t(a, b):
    return lax.dot_general(a, b, (((1,), (1,)), ((), ())), preferred_element_type=FULL)


def tables_kernel(base, consts, *refs):
    z_out, h_out = refs[-2:]
    channels, _, lanes = z_out.shape
    row8 = lax.broadcasted_iota(jnp.int32, (8, lanes), 0)
    row = lax.broadcasted_iota(jnp.int32, (lanes, lanes), 0)
    lane = lax.broadcasted_iota(jnp.int32, (lanes, lanes), 1)
    live = row + lane >= lanes - 1

    def one(c):
        first = jnp.concatenate([base[k, pl.ds(c, 1), :] for k in range(8)], axis=0)
        tiles = [(first, half_turned(first))]
        for level in range(4):
            k = STRIDE + 2 * level
            a, b = consts[k, pl.ds(c, 1), :], consts[k + 1, pl.ds(c, 1), :]
            tiles += [(t * a + u * b, u * a - t * b) for t, u in tiles]
        z = jnp.concatenate([t for t, _ in tiles], axis=0)
        high, low = high_low(z)
        z_out[c, :lanes, :] = high
        z_out[c, lanes:, :] = low
        f_high, f_low = high_low(jnp.broadcast_to(consts[KERNEL, pl.ds(c, 1), :], (8, lanes)))
        h = dot_t(jnp.concatenate([f_high, f_low], axis=0), high)
        h = h[:8] + h[8:] + dot_t(f_high, low)
        for bit in (1, 2, 4):
            h = jnp.where((7 - row8) & bit != 0, pltpu.roll(h, bit, 1), h)
        hankel = [pltpu.roll(h, lanes - 8 - k, 1) if k < lanes - 8 else h for k in range(0, lanes, 8)]
        hankel = jnp.concatenate(hankel, axis=0)
        h_out[c] = jnp.where(live, hankel, 0.0).astype(LOW)

    @pl.loop(0, channels, step=UNROLL)
    def _(c):
        for k in range(UNROLL):
            one(c + k)


def s4_tables(base, consts, part, parts, tables=(), deps=()):
    _, width, lanes = base.shape
    steps = width // CHANNELS // parts
    skip = part * steps
    anywhere = pl.BlockSpec(memory_space=pl.ANY)
    return pl.pallas_call(
        tables_kernel,
        grid=(steps,),
        in_specs=[
            pl.BlockSpec((8, CHANNELS, lanes), lambda i: (0, i + skip, 0)),
            pl.BlockSpec((ROWS, CHANNELS, lanes), lambda i: (0, i + skip, 0)),
        ]
        + [anywhere] * (len(tables) + len(deps)),
        out_specs=[
            pl.BlockSpec((CHANNELS, 2 * lanes, lanes), lambda i: (i + skip, 0, 0)),
            pl.BlockSpec((CHANNELS, lanes, lanes), lambda i: (i + skip, 0, 0)),
        ],
        out_shape=[
            jax.ShapeDtypeStruct((width, 2 * lanes, lanes), LOW),
            jax.ShapeDtypeStruct((width, lanes, lanes), LOW),
        ],
        input_output_aliases={2: 0, 3: 1} if tables else {},
        compiler_params=pltpu.CompilerParams(vmem_limit_bytes=VMEM),
        cost_estimate=cost(24 / parts),
        name="s4_tables",
    )(base, consts, *tables, *deps)


def flip_matrix(size):
    row = lax.broadcasted_iota(jnp.int32, (size, size), 0)
    lane = lax.broadcasted_iota(jnp.int32, (size, size), 1)
    return (row + lane == size - 1).astype(FULL).astype(LOW)


def rows_of_channels(consts, k):
    return jnp.stack([consts[k, c : c + 1, :] for c in range(consts.shape[1])])


def weighted_ends(x, place, z):
    high, low = high_low(x * place)
    x = x.astype(LOW)
    none = jnp.zeros_like(x)
    left = jnp.concatenate([x, high, low, none], axis=0)
    right = jnp.concatenate([x, high, none, none], axis=0)
    ends = dot(jnp.concatenate([left, right], axis=1), z)
    count = x.shape[0]
    return ends[:count], ends[count : 2 * count] + ends[2 * count : 3 * count]


def times_both(x, consts, k):
    first, second = rows_of_channels(consts, k), rows_of_channels(consts, k + 1)
    return x[0] * first + x[1] * second, x[1] * first - x[0] * second


def scan_blocks(x, consts, row, reverse):
    count = x[0].shape[1]
    for level, d in enumerate((1, 2, 4)):
        live = row < count - d if reverse else row >= d
        moved = [jnp.where(live, pltpu.roll(e, count - d if reverse else d, 1), 0.0) for e in x]
        x = add(x, times_both(moved, consts, CARRY + 2 * level))
    return x


def forward_kernel(
    signal, skip, consts, z, m, init, activ, slope, x_out, p_out, q_out, s_out, x_scr, y_scr
):
    step = pl.program_id(0)
    channels, _, lanes = z.shape
    count = signal.shape[0] // lanes
    width = signal.shape[1]

    @pl.when(step == 0)
    def _():
        flip = flip_matrix(lanes)
        for j in range(count):
            x_scr[pl.ds(j, width, stride=count), :] = dot(flip, signal[j * lanes : (j + 1) * lanes, :]).T

    rows = pl.ds(pl.multiple_of(step * channels * count, channels * count), channels * count)
    x = x_scr[rows, :].reshape(channels, count, lanes)
    place = lax.broadcasted_iota(jnp.int32, (count, lanes), 1).astype(FULL)
    row = lax.broadcasted_iota(jnp.int32, (channels, count, lanes), 1)
    plus = lax.broadcasted_iota(jnp.int32, (channels, count, lanes), 2) < lanes // 2
    ends = [weighted_ends(x[c], place, z[c]) for c in range(channels)]
    p = jnp.stack([e[0] for e in ends])
    q = jnp.stack([e[1] for e in ends])
    start = init[...][:, None, :]
    state = times_both((p, half_turned(p)), consts, BBAR)
    state = [
        jnp.where(row == 0, e, pltpu.roll(s, 1, 1)) for e, s in zip((start, half_turned(start)), state)
    ]
    state = scan_blocks(state, consts, row, False)
    read, _ = times_both(state, consts, READ)
    read = jnp.where(plus, read, -read).astype(LOW)
    y = [dot(x[c].astype(LOW), m[c]) + dot_t(read[c], z[c, :lanes, :]) for c in range(channels)]
    y_scr[rows, :] = jnp.concatenate(y, axis=0)
    x_out[...] = x
    p_out[...] = p
    q_out[...] = q
    s_out[...] = state[0]

    @pl.when(step == pl.num_programs(0) - 1)
    def _():
        for j in range(count):
            part = slice(j * lanes, (j + 1) * lanes)
            mixed = y_scr[pl.ds(j, width, stride=count), :].T + skip[...] * signal[part, :].astype(FULL)
            inner = 0.7978845608028654 * (mixed + 0.044715 * mixed * mixed * mixed)
            bent = jnp.tanh(inner)
            activ[part, :] = (0.5 * mixed * (1.0 + bent)).astype(LOW)
            slope[part, :] = 0.5 * (1.0 + bent) + 0.5 * mixed * (1.0 - bent * bent) * (
                0.7978845608028654 * (1.0 + 3 * 0.044715 * mixed * mixed)
            )


def s4_forward(signal, skip, consts, z, m, init):
    tokens, width = signal.shape
    lanes = z.shape[-1]
    count = tokens // lanes
    whole = pl.BlockSpec((tokens, width), lambda i: (0, 0))
    by_channel = pl.BlockSpec((CHANNELS, count, lanes), lambda i: (i, 0, 0))
    per_channel = jax.ShapeDtypeStruct((width, count, lanes), FULL)
    return pl.pallas_call(
        forward_kernel,
        grid=(width // CHANNELS,),
        in_specs=[
            whole,
            pl.BlockSpec((1, width), lambda i: (0, 0)),
            pl.BlockSpec((ROWS, CHANNELS, lanes), lambda i: (0, i, 0)),
            pl.BlockSpec((CHANNELS, 2 * lanes, lanes), lambda i: (i, 0, 0)),
            pl.BlockSpec((CHANNELS, lanes, lanes), lambda i: (i, 0, 0)),
            pl.BlockSpec((CHANNELS, lanes), lambda i: (i, 0)),
        ],
        out_specs=[whole, whole] + [by_channel] * 4,
        out_shape=[
            jax.ShapeDtypeStruct((tokens, width), LOW),
            jax.ShapeDtypeStruct((tokens, width), FULL),
        ]
        + [per_channel] * 4,
        scratch_shapes=[pltpu.VMEM((width * count, lanes), FULL)] * 2,
        compiler_params=pltpu.CompilerParams(vmem_limit_bytes=VMEM),
        cost_estimate=cost(18),
        name="s4_forward",
    )(signal, skip, consts, z, m, init)


def backward_kernel(grads, consts, z, m, init, *refs):
    out, g_out, u_out, v_out, h_out, g_scr, y_scr = refs[-7:]
    step = pl.program_id(0)
    channels, _, lanes = z.shape
    count = grads.shape[0] // lanes
    width = grads.shape[1]

    @pl.when(step == 0)
    def _():
        for j in range(count):
            g_scr[pl.ds(j, width, stride=count), :] = grads[j * lanes : (j + 1) * lanes, :].astype(FULL).T

    rows = pl.ds(pl.multiple_of(step * channels * count, channels * count), channels * count)
    g = g_scr[rows, :].reshape(channels, count, lanes)
    place = lax.broadcasted_iota(jnp.int32, (count, lanes), 1).astype(FULL)
    row = lax.broadcasted_iota(jnp.int32, (channels, count, lanes), 1)
    plus = lax.broadcasted_iota(jnp.int32, (channels, count, lanes), 2) < lanes // 2
    ends = [weighted_ends(g[c], place, z[c]) for c in range(channels)]
    u = jnp.stack([e[0] for e in ends])
    v = jnp.stack([e[1] for e in ends])
    start = init[...][:, None, :]
    later = times_both((u, half_turned(u)), consts, READ)
    later = [
        jnp.where(row == count - 1, e, pltpu.roll(s, count - 1, 1))
        for e, s in zip((start, half_turned(start)), later)
    ]
    later = scan_blocks(later, consts, row, True)
    write, _ = times_both(later, consts, BBAR)
    write = jnp.where(plus, write, -write).astype(LOW)
    y = [dot(g[c].astype(LOW), m[c]) + dot_t(write[c], z[c, :lanes, :]) for c in range(channels)]
    y_scr[rows, :] = jnp.concatenate(y, axis=0)
    g_out[...] = g
    u_out[...] = u
    v_out[...] = v
    h_out[...] = later[0]

    @pl.when(step == pl.num_programs(0) - 1)
    def _():
        flip = flip_matrix(lanes)
        for j in range(count):
            out[j * lanes : (j + 1) * lanes, :] = dot(
                flip, y_scr[pl.ds(j, width, stride=count), :].T.astype(LOW)
            )


def s4_backward(grads, consts, z, m, init, deps=()):
    tokens, width = grads.shape
    lanes = z.shape[-1]
    count = tokens // lanes
    whole = pl.BlockSpec((tokens, width), lambda i: (0, 0))
    by_channel = pl.BlockSpec((CHANNELS, count, lanes), lambda i: (i, 0, 0))
    per_channel = jax.ShapeDtypeStruct((width, count, lanes), FULL)
    return pl.pallas_call(
        backward_kernel,
        grid=(width // CHANNELS,),
        in_specs=[
            whole,
            pl.BlockSpec((ROWS, CHANNELS, lanes), lambda i: (0, i, 0)),
            pl.BlockSpec((CHANNELS, 2 * lanes, lanes), lambda i: (i, 0, 0)),
            pl.BlockSpec((CHANNELS, lanes, lanes), lambda i: (i, 0, 0)),
            pl.BlockSpec((CHANNELS, lanes), lambda i: (i, 0)),
        ]
        + [pl.BlockSpec(memory_space=pl.ANY)] * len(deps),
        out_specs=[whole] + [by_channel] * 4,
        out_shape=[jax.ShapeDtypeStruct((tokens, width), FULL)] + [per_channel] * 4,
        scratch_shapes=[pltpu.VMEM((width * count, lanes), FULL)] * 2,
        compiler_params=pltpu.CompilerParams(vmem_limit_bytes=VMEM),
        cost_estimate=cost(18),
        name="s4_backward",
    )(grads, consts, z, m, init, *deps)


def sums_kernel(block, x, g, p, q, s, u, v, h, z, consts, *refs):
    out = refs[-1]
    channels, count, lanes = x.shape
    states = lanes // 2
    row8 = lax.broadcasted_iota(jnp.int32, (8, lanes), 0)
    row = lax.broadcasted_iota(jnp.int32, (lanes, lanes), 0)
    lane = lax.broadcasted_iota(jnp.int32, (lanes, lanes), 1)
    place = lax.broadcasted_iota(jnp.int32, (8, lanes), 1).astype(FULL)
    live = row + lane >= lanes - 1
    first = lax.broadcasted_iota(jnp.int32, (channels, lanes), 1) < states
    w = []
    for c in range(channels):
        both = lax.dot_general(
            x[c].astype(LOW), g[c].astype(LOW), (((0,), (0,)), ((), ())), preferred_element_type=FULL
        )
        both = jnp.where(live, both, 0.0)
        tiles = [both[k : k + 8, :] for k in range(0, lanes, 8)]
        shift = 8
        while len(tiles) > 1:
            tiles = [a + pltpu.roll(b, shift, 1) for a, b in zip(tiles[::2], tiles[1::2])]
            shift *= 2
        total = pltpu.roll(tiles[0], 1, 1)
        for bit in (1, 2, 4):
            total = jnp.where(row8 & bit != 0, pltpu.roll(total, bit, 1), total)
        high, low = high_low(total)
        place_high, place_low = high_low(total * place)
        none = jnp.zeros_like(high)
        left = jnp.concatenate([high, low, place_high, place_low], axis=0)
        right = jnp.concatenate([high, none, place_high, none], axis=0)
        w.append(dot(jnp.concatenate([left, right], axis=1), z[c]))
    lag0 = jnp.sum(jnp.stack([e[:16] for e in w]), axis=1)
    lag1 = jnp.sum(jnp.stack([e[16:] for e in w]), axis=1)

    def both_halves(x):
        turned = half_turned(x)
        return jnp.where(first, x, turned), jnp.where(first, turned, x)

    def product(a, b):
        plain = jnp.sum(a * b, axis=1)
        crossed = jnp.sum(a * half_turned(b), axis=1)
        plain = jnp.where(first, plain, -plain)
        return plain + half_turned(plain), crossed + half_turned(crossed)

    states_read = product(u[...], s[...])
    slopes_read = product(u[...] + v[...], s[...])
    writes = product(h[...], p[...])
    slopes_write = product(h[...], q[...])
    carried = product(h[...], s[...])
    lag0, lag1 = both_halves(lag0), both_halves(lag1)

    def const(k):
        return consts[k]

    def const_factor(k):
        second = const(k + 1)
        return const(k), jnp.where(first, -second, second)

    bbar, read, carry = const_factor(BBAR), const_factor(READ), const_factor(CARRY)
    z_one, ratio = (const(Z), const(Z + 1)), (const(RATIO), const(RATIO + 1))
    c, b = (const(C), const(C + 1)), (const(B), const(B + 1))
    decay, freq, step = const(A_PART), const(A_PART + 1), const(STEP)
    modulus = decay * decay + freq * freq
    over_a = (-decay / modulus, -freq / modulus)
    to_c = scale(add(cmul(z_one, states_read), cmul(bbar, lag0)), 2.0)
    to_bbar = add(writes, scale(cmul(c, lag0), 2.0))
    to_log = add(
        add(cmul(read, slopes_read), cmul(bbar, slopes_write)),
        add(scale(cmul(carry, carried), float(block)), scale(cmul(cmul(c, bbar), lag1), 2.0)),
    )
    to_b = cmul(to_bbar, ratio)
    over = cmul(cmul(to_bbar, b), over_a)
    to_log = add(to_log, cmul(over, z_one))
    to_a = cmul(over, ratio)
    grad_decay = to_a[0] - step * to_log[0]
    grad_freq = to_a[1] - step * to_log[1]
    grad_step = jnp.where(first, -to_log[0] * decay, -to_log[1] * freq)
    out[0] = jnp.where(first, grad_decay, grad_freq)
    out[1] = jnp.where(first, to_b[0], -to_b[1])
    out[2] = jnp.where(first, to_c[0], -to_c[1])
    out[3] = jnp.broadcast_to(jnp.sum(grad_step, axis=1, keepdims=True), (channels, lanes))


def s4_sums(x, g, p, q, s, u, v, h, z, consts, block, deps, skip, steps):
    width, count, lanes = x.shape
    by_channel = pl.BlockSpec((CHANNELS, count, lanes), lambda i: (i + skip, 0, 0))
    return pl.pallas_call(
        lambda *refs: sums_kernel(block, *refs),
        grid=(steps,),
        in_specs=[by_channel] * 8
        + [
            pl.BlockSpec((CHANNELS, 2 * lanes, lanes), lambda i: (i + skip, 0, 0)),
            pl.BlockSpec((ROWS, CHANNELS, lanes), lambda i: (0, i + skip, 0)),
        ]
        + [pl.BlockSpec(memory_space=pl.ANY)] * len(deps),
        out_specs=pl.BlockSpec((4, CHANNELS, lanes), lambda i: (0, i, 0)),
        out_shape=jax.ShapeDtypeStruct((4, steps * CHANNELS, lanes), FULL),
        compiler_params=pltpu.CompilerParams(vmem_limit_bytes=VMEM),
        cost_estimate=cost(18 * steps * CHANNELS / width),
        name="s4_sums",
    )(x, g, p, q, s, u, v, h, z, consts, *deps)


def split(rows):
    half = rows.shape[-1] // 2
    return rows[..., :half], rows[..., half:]


def t_dot(a, b):
    return lax.dot_general(a, b, (((0,), (0,)), ((), ())), preferred_element_type=FULL)


def layer_forward(values, gain, bias, total_width, sums=None):
    if sums is None:
        sums = sum_chan(jnp.stack([jnp.sum(values, axis=-1), jnp.sum(values * values, axis=-1)]))
    center = sums[0] / total_width
    spread_var = sums[1] / total_width - center * center
    inverse = lax.rsqrt(spread_var + EPSILON)[..., None]
    normed = (values - center[..., None]) * inverse
    return normed * gain + bias, normed, inverse


def layer_backward(grad_out, normed, inverse, gain, total_width, work):
    scaled = grad_out * gain
    sums = jnp.stack([jnp.sum(scaled, axis=-1), jnp.sum(scaled * normed, axis=-1)])
    sums = after(sum_chan(sums), *work(sums))
    grad_in = inverse * (
        scaled - sums[0][..., None] / total_width - normed * sums[1][..., None] / total_width
    )
    return grad_in, jnp.sum(grad_out * normed, axis=0), jnp.sum(grad_out, axis=0)


def body(
    block_input,
    lengths,
    norm1_gain,
    norm1_bias,
    a_decay,
    a_freq,
    b_state,
    c_state,
    step_size,
    skip_gain,
    w_value,
    b_value,
    w_gate,
    b_gate,
    norm2_gain,
    norm2_bias,
    w_up,
    b_up,
    w_down,
    b_down,
    out_grad,
):
    batch, block, width = block_input.shape
    chans = lax.axis_size("chan")
    seqs = lax.axis_size("seq")
    assert seqs % batch == 0
    runs = seqs // batch
    total_width = width * chans
    assert chans == 4
    seq_me = lax.axis_index("seq")
    chan_me = lax.axis_index("chan")
    groups = None if runs == 1 else [[r * batch + j for j in range(batch)] for r in range(runs)]
    peers = None if runs == 1 else [[r * batch + j for r in range(runs)] for j in range(batch)]

    def exchange(x):
        return lax.all_to_all(x, "seq", 0, 0, axis_index_groups=groups, tiled=True)

    def rows_of(w):
        return [
            lax.dynamic_slice_in_dim(w, (chan_me ^ d) * width, width, 0) for d in range(chans)
        ]

    moved = exchange(jnp.concatenate([block_input, out_grad], axis=-1)).reshape(batch * block, 2 * width)

    consts, base = s4_consts(a_decay, a_freq, b_state, c_state, step_size, block)
    z, m = s4_tables(base, consts, 0, 1)
    moved = after(moved, z)
    inputs = moved[:, :width].astype(FULL)
    grad_low = moved[:, width:]
    moments = sum_chan(jnp.stack([jnp.sum(inputs, axis=-1), jnp.sum(inputs * inputs, axis=-1)]))
    states = a_decay.shape[0]

    def const_factor(k):
        return consts[k, :, :states], consts[k + 1, :, states:]

    begin = (seq_me // batch) * batch * block
    places = begin + jnp.arange(batch * block, dtype=jnp.int32)
    mask = (places < lengths[seq_me % batch]).astype(FULL)[:, None]
    norm_one, normed_one, inverse_one = layer_forward(inputs, norm1_gain, norm1_bias, total_width, moments)
    signal = (mask * norm_one).astype(LOW)
    skip = skip_gain[None, :]
    init = jnp.zeros((width, 2 * states), FULL)
    if runs > 1:
        _, _, _, p, _, s = s4_forward(signal, skip, consts, z, m, init)
        carry = const_factor(CARRY)
        end = add(cmul(carry, split(s[:, -1])), cmul(const_factor(BBAR), split(p[:, -1])))
        ends = lax.all_gather(pair(*end), "seq", axis_index_groups=peers)
        hop = carry
        for _ in range(3):
            hop = cmul(hop, hop)
        for r in range(runs - 1):
            moved = add(cmul(hop, split(init)), split(ends[r]))
            init = jnp.where(r < seq_me // batch, pair(*moved), init)
    activ, slope, xs, ps, qs, ss = s4_forward(signal, skip, consts, z, m, init)

    wv, wg = rows_of(w_value), rows_of(w_gate)
    w_gated = [jnp.concatenate([a, b], axis=1) for a, b in zip(wv, wg)]
    w_ups = rows_of(w_up)
    w_downs = [
        lax.dynamic_slice_in_dim(w_down, (chan_me ^ d) * width, width, 1) for d in range(chans)
    ]
    grads = gather_pieces(grad_low)
    activs = gather_pieces(after(activ, grads[2]))
    both = sum(dot(a, w) for a, w in zip(activs, w_gated))
    value = both[:, :width] + b_value
    gate = both[:, width:] + b_gate
    opened = jax.nn.sigmoid(gate)
    resid = inputs + value * opened
    norm_two, normed_two, inverse_two = layer_forward(resid, norm2_gain, norm2_bias, total_width)
    norms = gather_pieces(norm_two.astype(LOW))
    hidden = sum(dot(a, w) for a, w in zip(norms, w_ups)) + b_up
    spread, gelu_pull = jax.vjp(jax.nn.gelu, hidden)
    spread = spread.astype(LOW)

    grad_out = grad_low.astype(FULL)
    grad_spread = sum(dot_t(a, w) for a, w in zip(grads, w_downs))
    grad_hidden = gelu_pull(grad_spread)[0].astype(LOW)
    grad_w_down = t_dot(after(spread, grad_hidden), jnp.concatenate(grads, axis=1)).astype(LOW)
    downs_dealt = deal(grad_w_down)
    marks = []
    hidden_late = after(grad_hidden, grad_w_down)
    grad_norm_two = reduce_pieces([dot_t(hidden_late, w) for w in w_ups], marks)
    grad_w_up = t_dot(jnp.concatenate(norms, axis=1), after(grad_hidden, *marks[:2])).astype(LOW)
    grad_norm_two = after(grad_norm_two, grad_w_up)
    chains = []

    def start_ups(dep):
        chains.append(Chain([downs_dealt, deal(after(grad_w_up, dep))], True))
        return []

    grad_resid, grad_norm2_gain, grad_norm2_bias = layer_backward(
        grad_norm_two, normed_two, inverse_two, norm2_gain, total_width, start_ups
    )
    wide_chain = chains[0]
    grad_resid = grad_out + grad_resid
    grad_value = (grad_resid * opened).astype(LOW)
    grad_gate = (grad_resid * value * opened * (1.0 - opened)).astype(LOW)
    grad_both = jnp.concatenate([grad_value, grad_gate], axis=1)
    marks = []
    grad_activ = reduce_pieces([dot_t(grad_both, w) for w in w_gated], marks)
    grad_w_gated = t_dot(jnp.concatenate(activs, axis=1), after(grad_both, *marks[:2])).astype(LOW)
    gated_chain = Chain([deal(after(grad_w_gated, grad_activ))], False)
    grad_activ = after(grad_activ, grad_w_gated)
    grad_mixed = (grad_activ * slope).astype(LOW)
    made = advance([wide_chain], grad_mixed)
    init = jnp.zeros((width, 2 * states), FULL)
    if runs > 1:
        _, _, u, _, h = s4_backward(grad_mixed, consts, z, m, init)
        end = add(cmul(carry, split(h[:, 0])), cmul(const_factor(READ), split(u[:, 0])))
        ends = lax.all_gather(pair(*end), "seq", axis_index_groups=peers)
        for r in reversed(range(1, runs)):
            moved = add(cmul(hop, split(init)), split(ends[r]))
            init = jnp.where(r > seq_me // batch, pair(*moved), init)
    grad_signal, gs, us, vs, hs = s4_backward(grad_mixed, consts, z, m, init, made)
    grad_signal = after(grad_signal, *advance([wide_chain, gated_chain], grad_signal))
    grad_signal = grad_signal + skip * grad_mixed.astype(FULL)
    s4_parts = (xs, gs, ps, qs, ss, us, vs, hs, z, consts, block)
    grad_input, grad_norm1_gain, grad_norm1_bias = layer_backward(
        grad_signal * mask, normed_one, inverse_one, norm1_gain, total_width, lambda dep: []
    )
    grad_input = (grad_resid + grad_input).astype(LOW)
    wide_own = gather(wide_chain.parts[0])
    sums = s4_sums(*s4_parts, [grad_input], 0, width // CHANNELS)
    narrow = jnp.concatenate(
        [
            grad_norm1_gain,
            grad_norm1_bias,
            jnp.sum(grad_mixed.astype(FULL) * signal.astype(FULL), axis=0),
            jnp.sum(grad_value.astype(FULL), axis=0),
            jnp.sum(grad_gate.astype(FULL), axis=0),
            grad_norm2_gain,
            grad_norm2_bias,
            jnp.sum(grad_out, axis=0),
            sums[3, :, 0],
            jnp.sum(grad_hidden.astype(FULL), axis=0),
        ]
    )
    packed = pack_small(sums, narrow)
    dealt = exchange_all(packed)
    made = join_sum(wide_chain.parts[1], *gated_chain.parts, [packed, *wide_own[1:]])
    last = gather_relayed(made)
    spread_late = after(spread, made)
    output = reduce_pieces([dot(spread_late, w) for w in w_downs])
    output = (resid + output + b_down).astype(LOW)
    parts, wide, narrow = sum_small(dealt, sums, narrow.shape[0], last[1:3])
    moved = beside(grad_input, output, [parts, *last[1:]])
    moved = exchange(moved.reshape(batch, block, 2 * width))
    grad_input, output = moved[:, :, :width].astype(FULL), moved[:, :, width:]
    vectors = [narrow[k * width : (k + 1) * width] for k in range(9)]
    vectors.insert(2, vectors.pop(8))

    zero = 0 * chan_me
    (down,) = finish([wide_own, last], 0, 2, total_width, 0, zero, chan_me >> 1, chan_me & 1)
    (up,) = finish([wide_own, last], 1, 2, grad_w_up.shape[1], 0, chan_me, zero, zero)
    grad_w_value, grad_w_gate = finish([last], 0, 1, 2 * width, total_width, chan_me, zero, zero, 2)
    return (
        output,
        grad_input,
        vectors[0],
        vectors[1],
        *wide,
        vectors[2],
        vectors[3],
        grad_w_value,
        vectors[4],
        grad_w_gate,
        vectors[5],
        vectors[6],
        vectors[7],
        up,
        narrow[9 * width :],
        down,
        vectors[8],
    )


def solution(mesh):
    in_specs = (
        P(None, "seq", "chan"),
        P(),
        P("chan"),
        P("chan"),
        P(None, "chan"),
        P(None, "chan"),
        P(None, None, "chan"),
        P(None, None, "chan"),
        P("chan"),
        P("chan"),
        P(None, "chan"),
        P("chan"),
        P(None, "chan"),
        P("chan"),
        P("chan"),
        P("chan"),
        P(None, "chan"),
        P("chan"),
        P("chan", None),
        P("chan"),
        P(None, "seq", "chan"),
    )
    out_specs = (
        P(None, "seq", "chan"),
        P(None, "seq", "chan"),
        P("chan"),
        P("chan"),
        P(None, "chan"),
        P(None, "chan"),
        P(None, None, "chan"),
        P(None, None, "chan"),
        P("chan"),
        P("chan"),
        P(None, "chan"),
        P("chan"),
        P(None, "chan"),
        P("chan"),
        P("chan"),
        P("chan"),
        P(None, "chan"),
        P("chan"),
        P("chan", None),
        P("chan"),
    )
    return jax.shard_map(body, mesh=mesh, in_specs=in_specs, out_specs=out_specs, check_vma=False)
```

```python
import jax
import jax.numpy as jnp
from jax import lax
from jax.experimental import pallas as pl
from jax.experimental.pallas import tpu as pltpu
from jax.sharding import PartitionSpec as P

EPSILON = 1e-05
LOW = jnp.bfloat16
FULL = jnp.float32
CHANNELS = 32
UNROLL = 16
SCALE = 1.0e5
VMEM = 56 * 1024 * 1024


def swap(x, axis, distance):
    return lax.ppermute(x, axis, [(i, i ^ distance) for i in range(lax.axis_size(axis))])


def axis_bits(axis):
    size = lax.axis_size(axis)
    bits = size.bit_length() - 1
    assert size == 1 << bits
    return bits


def gather_pieces(x):
    pieces = {0: x}
    for bit in reversed(range(axis_bits("chan"))):
        for d in list(pieces):
            pieces[d ^ (1 << bit)] = swap(pieces[d], "chan", 1 << bit)
    return [pieces[d] for d in range(len(pieces))]


def reduce_pieces(parts, marks=None):
    sums = dict(enumerate(parts))
    for bit in range(axis_bits("chan")):
        if marks is not None and bit == axis_bits("chan") - 1:
            marks += [sums[1 << bit], sums[0]]
        for d in sorted(sums, reverse=True):
            if d >> bit & 1:
                received = swap(sums.pop(d).astype(LOW), "chan", 1 << bit)
                if marks is not None and d == 1 << (axis_bits("chan") - 1):
                    marks.append(received)
                sums[d ^ (1 << bit)] = sums[d ^ (1 << bit)] + received.astype(FULL)
    return sums[0]


def sum_chan(x):
    return x + sum(swap(x, "chan", d) for d in range(1, lax.axis_size("chan")))


def after(x, *others):
    return lax.optimization_barrier((x, others))[0]


def exchange_all(x):
    return lax.all_to_all(x, "seq", 0, 0, tiled=True)


def small_shares(sums, size):
    seqs = lax.axis_size("seq")
    groups, width, lanes = sums.shape
    short = -(-size // (seqs * lanes))
    assert short <= 8
    share = (groups - 1) * width // seqs
    return share, short, -(-(share + 16) // 16) * 16


def pack_small(sums, narrow):
    seqs = lax.axis_size("seq")
    groups, width, lanes = sums.shape
    size = narrow.shape[0]
    share, short, rows = small_shares(sums, size)
    narrow_rows = jnp.pad(narrow, (0, seqs * short * lanes - size)).reshape(seqs, short, lanes)
    narrow_rows = jnp.pad(narrow_rows, ((0, 0), (0, 8 - short), (0, 0)))

    def pack(sums, narrow, packed):
        flat = sums[: groups - 1].reshape((groups - 1) * width, lanes)
        for k in range(seqs):
            part = narrow[k]
            high = part.astype(LOW).astype(FULL)
            pieces = [flat[k * share : (k + 1) * share], high, part - high]
            if rows > share + 16:
                pieces.append(jnp.zeros((rows - share - 16, lanes), FULL))
            packed[k] = jnp.concatenate(pieces, axis=0).astype(LOW)

    shape = jax.ShapeDtypeStruct((seqs, rows, lanes), LOW)
    return call_here(pack, [sums, narrow_rows], [], [shape], "pack_small")[0]


def sum_small(dealt, sums, size, deps):
    seqs, rows, lanes = dealt.shape
    groups, width, _ = sums.shape
    share, short, _ = small_shares(sums, size)

    def add(dealt, out):
        total = sum(dealt[k].astype(FULL) for k in range(seqs))
        narrow = total[share : share + 8] + total[share + 8 : share + 16]
        high = narrow.astype(LOW).astype(FULL)
        pieces = [total[:share], high, narrow - high] + ([total[share + 16 :]] if rows > share + 16 else [])
        total = jnp.concatenate(pieces, axis=0).astype(LOW)
        for k in range(seqs):
            out[k] = total

    parts = exchange_all(call_here(add, [dealt], deps, [jax.ShapeDtypeStruct(dealt.shape, LOW)], "sum_small")[0])
    states = lanes // 2

    def unpack(parts, decay, freq, b, c, narrow):
        flat = jnp.concatenate([parts[k, :share, :].astype(FULL) for k in range(seqs)], axis=0)
        a, b_both, c_both = (flat[g * width : (g + 1) * width].T for g in range(3))
        decay[...], freq[...] = a[:states], a[states:]
        b[0], b[1] = b_both[:states], b_both[states:]
        c[0], c[1] = c_both[:states], c_both[states:]
        for k in range(seqs):
            part = parts[k].astype(FULL)
            narrow[k] = part[share : share + 8] + part[share + 8 : share + 16]

    one, two = (states, width), (2, states, width)
    *wide, narrow = call_here(
        unpack,
        [parts],
        [],
        [jax.ShapeDtypeStruct(shape, FULL) for shape in (one, one, two, two, (seqs, 8, lanes))],
        "unpack_small",
    )
    return parts, wide, narrow[:, :short].reshape(-1)[:size]


def beside(left, right, deps):
    rows, columns = left.shape

    def kernel(left, right, out):
        out[:, :columns] = left[...]
        out[:, columns:] = right[...]

    shape = jax.ShapeDtypeStruct((rows, columns + right.shape[1]), left.dtype)
    return call_here(kernel, [left, right], deps, [shape], "beside")[0]


def call_here(kernel, ins, deps, outs, name):
    here, anywhere = pl.BlockSpec(memory_space=pltpu.VMEM), pl.BlockSpec(memory_space=pl.ANY)
    return pl.pallas_call(
        lambda *refs: kernel(*refs[: len(ins)], *refs[len(ins) + len(deps) :]),
        in_specs=[here] * len(ins) + [anywhere] * len(deps),
        out_specs=[here] * len(outs),
        out_shape=outs,
        compiler_params=pltpu.CompilerParams(vmem_limit_bytes=VMEM),
        cost_estimate=cost(2),
        name=name,
    )(*ins, *deps)


QUAD = 4


def deal(x):
    seqs = lax.axis_size("seq")
    groups = [list(range(i, i + QUAD)) for i in range(0, seqs, QUAD)]
    return lax.all_to_all(x.reshape(QUAD, -1, x.shape[1]), "seq", 0, 0, axis_index_groups=groups, tiled=True)


class Chain:
    def __init__(self, parts, halves):
        self.masks = [1 << bit for bit in range(axis_bits("seq")) if 1 << bit >= QUAD]
        self.parts = parts
        self.halves = halves
        self.tasks = ["deal" if halves else "whole", "sum"]

    def accept(self, task, outs):
        if task == "deal":
            self.parts = [outs[0], swap(outs[1], "seq", self.masks[0])]
            return
        total = outs[0]
        for mask in self.masks[1:]:
            total = (total.astype(FULL) + swap(total, "seq", mask).astype(FULL)).astype(LOW)
        self.parts = [total]
        if task == "whole" or self.halves:
            self.parts.append(swap(total, "seq", self.masks[0]))


def gather(part):
    return [part] + [swap(part, "seq", mask) for mask in range(1, QUAD)]


def gather_relayed(part):
    first, second = swap(part, "seq", 1), swap(part, "seq", 2)
    half = part.shape[0] // 2
    third = jnp.concatenate([swap(second[:half], "seq", 1), swap(first[half:], "seq", 2)])
    return [part, first, second, third]


def join_sum(left, own, received, deps):
    rows, columns = left.shape

    def kernel(left, own, received, *refs):
        out = refs[-1]
        out[:, :columns] = left[...]
        out[:, columns:] = (own[...].astype(FULL) + received[...].astype(FULL)).astype(LOW)

    here, anywhere = pl.BlockSpec(memory_space=pltpu.VMEM), pl.BlockSpec(memory_space=pl.ANY)
    return pl.pallas_call(
        kernel,
        in_specs=[here] * 3 + [anywhere] * len(deps),
        out_specs=here,
        out_shape=jax.ShapeDtypeStruct((rows, columns + own.shape[1]), LOW),
        compiler_params=pltpu.CompilerParams(vmem_limit_bytes=VMEM),
        cost_estimate=cost(2),
        name="join_sum",
    )(left, own, received, *deps)


def advance(chains, *deps):
    tasks = [chain.tasks.pop(0) for chain in chains]
    parts = [chain.parts for chain in chains]
    shapes = []
    for task, part in zip(tasks, parts):
        rows, columns = part[0].shape[-2:]
        made = {"deal": [rows // 2 * len(part)] * 2, "whole": [rows * len(part)], "sum": [rows]}[task]
        shapes.append([jax.ShapeDtypeStruct((size, columns), LOW) for size in made])
    counts = [len(part) for part in parts]
    me = lax.axis_index("seq")
    high = (me // QUAD % 2).astype(jnp.int32)[None]

    def kernel(high, *refs):
        ins = list(refs[: sum(counts)])
        outs = list(refs[len(refs) - sum(len(shape) for shape in shapes) :])
        for task, count in zip(tasks, counts):
            refs = [ins.pop(0) for _ in range(count)]
            if task == "deal":
                half = refs[0].shape[1] // 2
                for block in (high[0], 1 - high[0]):
                    place = pl.ds(pl.multiple_of(block * half, half), half)
                    out = outs.pop(0)
                    for i, ref in enumerate(refs):
                        out[i * half : (i + 1) * half, :] = sum(
                            ref[k, place, :].astype(FULL) for k in range(QUAD)
                        ).astype(LOW)
            elif task == "whole":
                out = outs.pop(0)
                rows = refs[0].shape[1]
                for i, ref in enumerate(refs):
                    out[i * rows : (i + 1) * rows, :] = sum(ref[k].astype(FULL) for k in range(QUAD)).astype(LOW)
            else:
                outs.pop(0)[...] = (refs[0][...].astype(FULL) + refs[1][...].astype(FULL)).astype(LOW)

    here, anywhere = pl.BlockSpec(memory_space=pltpu.VMEM), pl.BlockSpec(memory_space=pl.ANY)
    results = list(
        pl.pallas_call(
            kernel,
            in_specs=[pl.BlockSpec(memory_space=pltpu.SMEM)] + [here] * sum(counts) + [anywhere] * len(deps),
            out_specs=[here] * sum(len(shape) for shape in shapes),
            out_shape=[one for shape in shapes for one in shape],
            compiler_params=pltpu.CompilerParams(vmem_limit_bytes=VMEM),
            cost_estimate=cost(2),
            name="advance",
        )(high, *[array for part in parts for array in part], *deps)
    )
    rest = list(results)
    for task, chain, shape in zip(tasks, chains, shapes):
        chain.accept(task, [rest.pop(0) for _ in shape])
    return results


def finish(groups, slot, slots, columns, first, row_turn, half_turn, column_turn, outputs=1):
    rows = groups[0][0].shape[0] // slots
    width = columns // 4
    skip = first // (2 * width)
    me = lax.axis_index("seq")
    high = me // QUAD % 2
    scalars = jnp.stack([(me & (QUAD - 1)) ^ row_turn, half_turn, column_turn, high]).astype(jnp.int32)
    count = len(groups)

    def kernel(scalars, *refs):
        ins, outs = refs[: count * QUAD], refs[-outputs:]

        def put(out):
            for k in range(count):
                for q in range(QUAD):
                    block = (scalars[0] ^ q) * count
                    if count == 2:
                        block = block + (scalars[3] ^ k)
                    target = pl.ds(pl.multiple_of(block * rows, rows), rows)
                    ref = ins[k * QUAD + q]
                    for e in range(2):
                        place = pl.ds(pl.multiple_of((e ^ scalars[2]) * width, width), width)
                        out[target, place] = ref[:, e * width : (e + 1) * width].astype(FULL)

        if outputs == 1:
            put(outs[0])
        else:
            for k in range(2):
                pl.when(pl.program_id(0) == k)(lambda k=k: put(outs[k]))

    return pl.pallas_call(
        kernel,
        grid_spec=pltpu.PrefetchScalarGridSpec(
            num_scalar_prefetch=1,
            grid=(2,),
            in_specs=[pl.BlockSpec((rows, 2 * width), lambda half, n: (slot, half + skip))] * (count * QUAD),
            out_specs=[
                pl.BlockSpec(
                    (count * QUAD * rows, 2 * width),
                    (lambda half, n: (0, half ^ n[1])) if outputs == 1 else (lambda half, n: (0, 0)),
                )
            ]
            * outputs,
        ),
        out_shape=[jax.ShapeDtypeStruct((count * QUAD * rows, columns // outputs), FULL)] * outputs,
        compiler_params=pltpu.CompilerParams(vmem_limit_bytes=VMEM),
        cost_estimate=cost(3),
        name="finish",
    )(scalars, *[part for group in groups for part in group])


def cost(us):
    return pl.CostEstimate(flops=0, bytes_accessed=int(us * SCALE), transcendentals=0)


def pair(re, im):
    return jnp.concatenate([re, im], axis=-1)


def factor(re, im):
    return pair(re, re), pair(-im, im)


def times(x, first, second):
    lanes = x.shape[-1]
    return x * first + pltpu.roll(x, lanes // 2, x.ndim - 1) * second


def cmul(a, b):
    return a[0] * b[0] - a[1] * b[1], a[0] * b[1] + a[1] * b[0]


def add(a, b):
    return a[0] + b[0], a[1] + b[1]


def scale(a, k):
    return a[0] * k, a[1] * k


BBAR, READ, CARRY, STRIDE, KERNEL, Z, RATIO, C, B, A_PART, STEP = 0, 2, 4, 10, 18, 19, 21, 23, 25, 27, 29
ROWS = 30


def less_one(x):
    total = 1.0 + x / 8.0
    for k in (7.0, 6.0, 5.0, 4.0, 3.0, 2.0):
        total = 1.0 + x / k * total
    return jnp.where(x > -0.25, x * total, jnp.exp(x) - 1.0)


def consts_kernel(block, decay_ref, freq_ref, b_ref, c_ref, step_ref, consts, base):
    states, width = decay_ref.shape
    lanes = 2 * states

    def wide(x):
        return jnp.concatenate([x, x], axis=0).T

    decay, freq = wide(decay_ref[...]), wide(freq_ref[...])
    b = (wide(b_ref[0]), wide(b_ref[1]))
    c = (wide(c_ref[0]), wide(c_ref[1]))
    step = jnp.broadcast_to(step_ref[...], (lanes, width)).T
    first = lax.broadcasted_iota(jnp.int32, (width, lanes), 1) < states
    rate = step * decay
    turn = step * freq
    size = jnp.exp(-rate)
    z = (size * jnp.cos(turn), size * jnp.sin(turn))
    half_turn = jnp.sin(0.5 * turn)
    less = (less_one(-rate) * jnp.cos(turn) - 2.0 * half_turn * half_turn, z[1])
    modulus = decay * decay + freq * freq
    ratio = (
        (freq * less[1] - decay * less[0]) / modulus,
        -(decay * less[1] + freq * less[0]) / modulus,
    )
    bbar = cmul(ratio, b)
    twice_c = scale(c, 2.0)

    def put_factor(k, x):
        consts[k] = x[0]
        consts[k + 1] = jnp.where(first, -x[1], x[1])

    def put_plain(k, x):
        consts[k] = x[0]
        consts[k + 1] = x[1]

    put_factor(BBAR, bbar)
    put_factor(READ, cmul(twice_c, z))
    kernel = cmul(twice_c, bbar)
    consts[KERNEL] = jnp.where(first, kernel[0], -kernel[1])
    put_plain(Z, z)
    put_plain(RATIO, ratio)
    put_plain(C, c)
    put_plain(B, b)
    consts[A_PART] = decay
    consts[A_PART + 1] = freq
    consts[STEP] = step
    power = (jnp.ones_like(size), jnp.zeros_like(size))
    for k in range(8):
        base[k] = jnp.where(first, power[0], power[1])
        power = cmul(power, z)
    k = 8
    while k < 4 * block:
        if k <= 64:
            put_factor(STRIDE + 2 * (k.bit_length() - 4), power)
        if k >= block:
            put_factor(CARRY + 2 * ((k // block).bit_length() - 1), power)
        power = cmul(power, power)
        k *= 2
    put_factor(CARRY + 4, power)


def s4_consts(a_decay, a_freq, b_state, c_state, step_size, block):
    states, width = a_decay.shape
    return pl.pallas_call(
        lambda *refs: consts_kernel(block, *refs),
        out_shape=[
            jax.ShapeDtypeStruct((ROWS, width, 2 * states), FULL),
            jax.ShapeDtypeStruct((8, width, 2 * states), FULL),
        ],
        compiler_params=pltpu.CompilerParams(vmem_limit_bytes=VMEM),
        cost_estimate=cost(6),
        name="s4_consts",
    )(a_decay, a_freq, b_state, c_state, step_size[None, :])


def half_turned(x):
    return pltpu.roll(x, x.shape[-1] // 2, x.ndim - 1)


def high_low(x):
    high = x.astype(LOW)
    return high, (x - high.astype(FULL)).astype(LOW)


def dot(a, b):
    return lax.dot_general(a, b, (((1,), (0,)), ((), ())), preferred_element_type=FULL)


def dot_t(a, b):
    return lax.dot_general(a, b, (((1,), (1,)), ((), ())), preferred_element_type=FULL)


def tables_kernel(base, consts, *refs):
    z_out, h_out = refs[-2:]
    channels, _, lanes = z_out.shape
    row8 = lax.broadcasted_iota(jnp.int32, (8, lanes), 0)
    row = lax.broadcasted_iota(jnp.int32, (lanes, lanes), 0)
    lane = lax.broadcasted_iota(jnp.int32, (lanes, lanes), 1)
    live = row + lane >= lanes - 1

    def one(c):
        first = jnp.concatenate([base[k, pl.ds(c, 1), :] for k in range(8)], axis=0)
        tiles = [(first, half_turned(first))]
        for level in range(4):
            k = STRIDE + 2 * level
            a, b = consts[k, pl.ds(c, 1), :], consts[k + 1, pl.ds(c, 1), :]
            tiles += [(t * a + u * b, u * a - t * b) for t, u in tiles]
        z = jnp.concatenate([t for t, _ in tiles], axis=0)
        high, low = high_low(z)
        z_out[c, :lanes, :] = high
        z_out[c, lanes:, :] = low
        f_high, f_low = high_low(jnp.broadcast_to(consts[KERNEL, pl.ds(c, 1), :], (8, lanes)))
        h = dot_t(jnp.concatenate([f_high, f_low], axis=0), high)
        h = h[:8] + h[8:] + dot_t(f_high, low)
        for bit in (1, 2, 4):
            h = jnp.where((7 - row8) & bit != 0, pltpu.roll(h, bit, 1), h)
        hankel = [pltpu.roll(h, lanes - 8 - k, 1) if k < lanes - 8 else h for k in range(0, lanes, 8)]
        hankel = jnp.concatenate(hankel, axis=0)
        h_out[c] = jnp.where(live, hankel, 0.0).astype(LOW)

    @pl.loop(0, channels, step=UNROLL)
    def _(c):
        for k in range(UNROLL):
            one(c + k)


def s4_tables(base, consts, part, parts, tables=(), deps=()):
    _, width, lanes = base.shape
    steps = width // CHANNELS // parts
    skip = part * steps
    anywhere = pl.BlockSpec(memory_space=pl.ANY)
    return pl.pallas_call(
        tables_kernel,
        grid=(steps,),
        in_specs=[
            pl.BlockSpec((8, CHANNELS, lanes), lambda i: (0, i + skip, 0)),
            pl.BlockSpec((ROWS, CHANNELS, lanes), lambda i: (0, i + skip, 0)),
        ]
        + [anywhere] * (len(tables) + len(deps)),
        out_specs=[
            pl.BlockSpec((CHANNELS, 2 * lanes, lanes), lambda i: (i + skip, 0, 0)),
            pl.BlockSpec((CHANNELS, lanes, lanes), lambda i: (i + skip, 0, 0)),
        ],
        out_shape=[
            jax.ShapeDtypeStruct((width, 2 * lanes, lanes), LOW),
            jax.ShapeDtypeStruct((width, lanes, lanes), LOW),
        ],
        input_output_aliases={2: 0, 3: 1} if tables else {},
        compiler_params=pltpu.CompilerParams(vmem_limit_bytes=VMEM),
        cost_estimate=cost(24 / parts),
        name="s4_tables",
    )(base, consts, *tables, *deps)


def flip_matrix(size):
    row = lax.broadcasted_iota(jnp.int32, (size, size), 0)
    lane = lax.broadcasted_iota(jnp.int32, (size, size), 1)
    return (row + lane == size - 1).astype(FULL).astype(LOW)


def rows_of_channels(consts, k):
    return jnp.stack([consts[k, c : c + 1, :] for c in range(consts.shape[1])])


def weighted_ends(x, place, z):
    high, low = high_low(x * place)
    x = x.astype(LOW)
    none = jnp.zeros_like(x)
    left = jnp.concatenate([x, high, low, none], axis=0)
    right = jnp.concatenate([x, high, none, none], axis=0)
    ends = dot(jnp.concatenate([left, right], axis=1), z)
    count = x.shape[0]
    return ends[:count], ends[count : 2 * count] + ends[2 * count : 3 * count]


def times_both(x, consts, k):
    first, second = rows_of_channels(consts, k), rows_of_channels(consts, k + 1)
    return x[0] * first + x[1] * second, x[1] * first - x[0] * second


def scan_blocks(x, consts, row, reverse):
    count = x[0].shape[1]
    for level, d in enumerate((1, 2, 4)):
        live = row < count - d if reverse else row >= d
        moved = [jnp.where(live, pltpu.roll(e, count - d if reverse else d, 1), 0.0) for e in x]
        x = add(x, times_both(moved, consts, CARRY + 2 * level))
    return x


def forward_kernel(
    signal, skip, consts, z, m, init, activ, slope, x_out, p_out, q_out, s_out, x_scr, y_scr
):
    step = pl.program_id(0)
    channels, _, lanes = z.shape
    count = signal.shape[0] // lanes
    width = signal.shape[1]

    @pl.when(step == 0)
    def _():
        flip = flip_matrix(lanes)
        for j in range(count):
            x_scr[pl.ds(j, width, stride=count), :] = dot(flip, signal[j * lanes : (j + 1) * lanes, :]).T

    rows = pl.ds(pl.multiple_of(step * channels * count, channels * count), channels * count)
    x = x_scr[rows, :].reshape(channels, count, lanes)
    place = lax.broadcasted_iota(jnp.int32, (count, lanes), 1).astype(FULL)
    row = lax.broadcasted_iota(jnp.int32, (channels, count, lanes), 1)
    plus = lax.broadcasted_iota(jnp.int32, (channels, count, lanes), 2) < lanes // 2
    ends = [weighted_ends(x[c], place, z[c]) for c in range(channels)]
    p = jnp.stack([e[0] for e in ends])
    q = jnp.stack([e[1] for e in ends])
    start = init[...][:, None, :]
    state = times_both((p, half_turned(p)), consts, BBAR)
    state = [
        jnp.where(row == 0, e, pltpu.roll(s, 1, 1)) for e, s in zip((start, half_turned(start)), state)
    ]
    state = scan_blocks(state, consts, row, False)
    read, _ = times_both(state, consts, READ)
    read = jnp.where(plus, read, -read).astype(LOW)
    y = [dot(x[c].astype(LOW), m[c]) + dot_t(read[c], z[c, :lanes, :]) for c in range(channels)]
    y_scr[rows, :] = jnp.concatenate(y, axis=0)
    x_out[...] = x
    p_out[...] = p
    q_out[...] = q
    s_out[...] = state[0]

    @pl.when(step == pl.num_programs(0) - 1)
    def _():
        for j in range(count):
            part = slice(j * lanes, (j + 1) * lanes)
            mixed = y_scr[pl.ds(j, width, stride=count), :].T + skip[...] * signal[part, :].astype(FULL)
            inner = 0.7978845608028654 * (mixed + 0.044715 * mixed * mixed * mixed)
            bent = jnp.tanh(inner)
            activ[part, :] = (0.5 * mixed * (1.0 + bent)).astype(LOW)
            slope[part, :] = 0.5 * (1.0 + bent) + 0.5 * mixed * (1.0 - bent * bent) * (
                0.7978845608028654 * (1.0 + 3 * 0.044715 * mixed * mixed)
            )


def s4_forward(signal, skip, consts, z, m, init):
    tokens, width = signal.shape
    lanes = z.shape[-1]
    count = tokens // lanes
    whole = pl.BlockSpec((tokens, width), lambda i: (0, 0))
    by_channel = pl.BlockSpec((CHANNELS, count, lanes), lambda i: (i, 0, 0))
    per_channel = jax.ShapeDtypeStruct((width, count, lanes), FULL)
    return pl.pallas_call(
        forward_kernel,
        grid=(width // CHANNELS,),
        in_specs=[
            whole,
            pl.BlockSpec((1, width), lambda i: (0, 0)),
            pl.BlockSpec((ROWS, CHANNELS, lanes), lambda i: (0, i, 0)),
            pl.BlockSpec((CHANNELS, 2 * lanes, lanes), lambda i: (i, 0, 0)),
            pl.BlockSpec((CHANNELS, lanes, lanes), lambda i: (i, 0, 0)),
            pl.BlockSpec((CHANNELS, lanes), lambda i: (i, 0)),
        ],
        out_specs=[whole, whole] + [by_channel] * 4,
        out_shape=[
            jax.ShapeDtypeStruct((tokens, width), LOW),
            jax.ShapeDtypeStruct((tokens, width), FULL),
        ]
        + [per_channel] * 4,
        scratch_shapes=[pltpu.VMEM((width * count, lanes), FULL)] * 2,
        compiler_params=pltpu.CompilerParams(vmem_limit_bytes=VMEM),
        cost_estimate=cost(18),
        name="s4_forward",
    )(signal, skip, consts, z, m, init)


def backward_kernel(grads, consts, z, m, init, *refs):
    out, g_out, u_out, v_out, h_out, g_scr, y_scr = refs[-7:]
    step = pl.program_id(0)
    channels, _, lanes = z.shape
    count = grads.shape[0] // lanes
    width = grads.shape[1]

    @pl.when(step == 0)
    def _():
        for j in range(count):
            g_scr[pl.ds(j, width, stride=count), :] = grads[j * lanes : (j + 1) * lanes, :].astype(FULL).T

    rows = pl.ds(pl.multiple_of(step * channels * count, channels * count), channels * count)
    g = g_scr[rows, :].reshape(channels, count, lanes)
    place = lax.broadcasted_iota(jnp.int32, (count, lanes), 1).astype(FULL)
    row = lax.broadcasted_iota(jnp.int32, (channels, count, lanes), 1)
    plus = lax.broadcasted_iota(jnp.int32, (channels, count, lanes), 2) < lanes // 2
    ends = [weighted_ends(g[c], place, z[c]) for c in range(channels)]
    u = jnp.stack([e[0] for e in ends])
    v = jnp.stack([e[1] for e in ends])
    start = init[...][:, None, :]
    later = times_both((u, half_turned(u)), consts, READ)
    later = [
        jnp.where(row == count - 1, e, pltpu.roll(s, count - 1, 1))
        for e, s in zip((start, half_turned(start)), later)
    ]
    later = scan_blocks(later, consts, row, True)
    write, _ = times_both(later, consts, BBAR)
    write = jnp.where(plus, write, -write).astype(LOW)
    y = [dot(g[c].astype(LOW), m[c]) + dot_t(write[c], z[c, :lanes, :]) for c in range(channels)]
    y_scr[rows, :] = jnp.concatenate(y, axis=0)
    g_out[...] = g
    u_out[...] = u
    v_out[...] = v
    h_out[...] = later[0]

    @pl.when(step == pl.num_programs(0) - 1)
    def _():
        flip = flip_matrix(lanes)
        for j in range(count):
            out[j * lanes : (j + 1) * lanes, :] = dot(
                flip, y_scr[pl.ds(j, width, stride=count), :].T.astype(LOW)
            )


def s4_backward(grads, consts, z, m, init, deps=()):
    tokens, width = grads.shape
    lanes = z.shape[-1]
    count = tokens // lanes
    whole = pl.BlockSpec((tokens, width), lambda i: (0, 0))
    by_channel = pl.BlockSpec((CHANNELS, count, lanes), lambda i: (i, 0, 0))
    per_channel = jax.ShapeDtypeStruct((width, count, lanes), FULL)
    return pl.pallas_call(
        backward_kernel,
        grid=(width // CHANNELS,),
        in_specs=[
            whole,
            pl.BlockSpec((ROWS, CHANNELS, lanes), lambda i: (0, i, 0)),
            pl.BlockSpec((CHANNELS, 2 * lanes, lanes), lambda i: (i, 0, 0)),
            pl.BlockSpec((CHANNELS, lanes, lanes), lambda i: (i, 0, 0)),
            pl.BlockSpec((CHANNELS, lanes), lambda i: (i, 0)),
        ]
        + [pl.BlockSpec(memory_space=pl.ANY)] * len(deps),
        out_specs=[whole] + [by_channel] * 4,
        out_shape=[jax.ShapeDtypeStruct((tokens, width), FULL)] + [per_channel] * 4,
        scratch_shapes=[pltpu.VMEM((width * count, lanes), FULL)] * 2,
        compiler_params=pltpu.CompilerParams(vmem_limit_bytes=VMEM),
        cost_estimate=cost(18),
        name="s4_backward",
    )(grads, consts, z, m, init, *deps)


def sums_kernel(block, x, g, p, q, s, u, v, h, z, consts, *refs):
    out = refs[-1]
    channels, count, lanes = x.shape
    states = lanes // 2
    row8 = lax.broadcasted_iota(jnp.int32, (8, lanes), 0)
    row = lax.broadcasted_iota(jnp.int32, (lanes, lanes), 0)
    lane = lax.broadcasted_iota(jnp.int32, (lanes, lanes), 1)
    place = lax.broadcasted_iota(jnp.int32, (8, lanes), 1).astype(FULL)
    live = row + lane >= lanes - 1
    first = lax.broadcasted_iota(jnp.int32, (channels, lanes), 1) < states
    w = []
    for c in range(channels):
        both = lax.dot_general(
            x[c].astype(LOW), g[c].astype(LOW), (((0,), (0,)), ((), ())), preferred_element_type=FULL
        )
        both = jnp.where(live, both, 0.0)
        tiles = [both[k : k + 8, :] for k in range(0, lanes, 8)]
        shift = 8
        while len(tiles) > 1:
            tiles = [a + pltpu.roll(b, shift, 1) for a, b in zip(tiles[::2], tiles[1::2])]
            shift *= 2
        total = pltpu.roll(tiles[0], 1, 1)
        for bit in (1, 2, 4):
            total = jnp.where(row8 & bit != 0, pltpu.roll(total, bit, 1), total)
        high, low = high_low(total)
        place_high, place_low = high_low(total * place)
        none = jnp.zeros_like(high)
        left = jnp.concatenate([high, low, place_high, place_low], axis=0)
        right = jnp.concatenate([high, none, place_high, none], axis=0)
        w.append(dot(jnp.concatenate([left, right], axis=1), z[c]))
    lag0 = jnp.sum(jnp.stack([e[:16] for e in w]), axis=1)
    lag1 = jnp.sum(jnp.stack([e[16:] for e in w]), axis=1)

    def both_halves(x):
        turned = half_turned(x)
        return jnp.where(first, x, turned), jnp.where(first, turned, x)

    def product(a, b):
        plain = jnp.sum(a * b, axis=1)
        crossed = jnp.sum(a * half_turned(b), axis=1)
        plain = jnp.where(first, plain, -plain)
        return plain + half_turned(plain), crossed + half_turned(crossed)

    states_read = product(u[...], s[...])
    slopes_read = product(u[...] + v[...], s[...])
    writes = product(h[...], p[...])
    slopes_write = product(h[...], q[...])
    carried = product(h[...], s[...])
    lag0, lag1 = both_halves(lag0), both_halves(lag1)

    def const(k):
        return consts[k]

    def const_factor(k):
        second = const(k + 1)
        return const(k), jnp.where(first, -second, second)

    bbar, read, carry = const_factor(BBAR), const_factor(READ), const_factor(CARRY)
    z_one, ratio = (const(Z), const(Z + 1)), (const(RATIO), const(RATIO + 1))
    c, b = (const(C), const(C + 1)), (const(B), const(B + 1))
    decay, freq, step = const(A_PART), const(A_PART + 1), const(STEP)
    modulus = decay * decay + freq * freq
    over_a = (-decay / modulus, -freq / modulus)
    to_c = scale(add(cmul(z_one, states_read), cmul(bbar, lag0)), 2.0)
    to_bbar = add(writes, scale(cmul(c, lag0), 2.0))
    to_log = add(
        add(cmul(read, slopes_read), cmul(bbar, slopes_write)),
        add(scale(cmul(carry, carried), float(block)), scale(cmul(cmul(c, bbar), lag1), 2.0)),
    )
    to_b = cmul(to_bbar, ratio)
    over = cmul(cmul(to_bbar, b), over_a)
    to_log = add(to_log, cmul(over, z_one))
    to_a = cmul(over, ratio)
    grad_decay = to_a[0] - step * to_log[0]
    grad_freq = to_a[1] - step * to_log[1]
    grad_step = jnp.where(first, -to_log[0] * decay, -to_log[1] * freq)
    out[0] = jnp.where(first, grad_decay, grad_freq)
    out[1] = jnp.where(first, to_b[0], -to_b[1])
    out[2] = jnp.where(first, to_c[0], -to_c[1])
    out[3] = jnp.broadcast_to(jnp.sum(grad_step, axis=1, keepdims=True), (channels, lanes))


def s4_sums(x, g, p, q, s, u, v, h, z, consts, block, deps, skip, steps):
    width, count, lanes = x.shape
    by_channel = pl.BlockSpec((CHANNELS, count, lanes), lambda i: (i + skip, 0, 0))
    return pl.pallas_call(
        lambda *refs: sums_kernel(block, *refs),
        grid=(steps,),
        in_specs=[by_channel] * 8
        + [
            pl.BlockSpec((CHANNELS, 2 * lanes, lanes), lambda i: (i + skip, 0, 0)),
            pl.BlockSpec((ROWS, CHANNELS, lanes), lambda i: (0, i + skip, 0)),
        ]
        + [pl.BlockSpec(memory_space=pl.ANY)] * len(deps),
        out_specs=pl.BlockSpec((4, CHANNELS, lanes), lambda i: (0, i, 0)),
        out_shape=jax.ShapeDtypeStruct((4, steps * CHANNELS, lanes), FULL),
        compiler_params=pltpu.CompilerParams(vmem_limit_bytes=VMEM),
        cost_estimate=cost(18 * steps * CHANNELS / width),
        name="s4_sums",
    )(x, g, p, q, s, u, v, h, z, consts, *deps)


def split(rows):
    half = rows.shape[-1] // 2
    return rows[..., :half], rows[..., half:]


def t_dot(a, b):
    return lax.dot_general(a, b, (((0,), (0,)), ((), ())), preferred_element_type=FULL)


def layer_forward(values, gain, bias, total_width, sums=None):
    if sums is None:
        sums = sum_chan(jnp.stack([jnp.sum(values, axis=-1), jnp.sum(values * values, axis=-1)]))
    center = sums[0] / total_width
    spread_var = sums[1] / total_width - center * center
    inverse = lax.rsqrt(spread_var + EPSILON)[..., None]
    normed = (values - center[..., None]) * inverse
    return normed * gain + bias, normed, inverse


def layer_backward(grad_out, normed, inverse, gain, total_width, work):
    scaled = grad_out * gain
    sums = jnp.stack([jnp.sum(scaled, axis=-1), jnp.sum(scaled * normed, axis=-1)])
    sums = after(sum_chan(sums), *work(sums))
    grad_in = inverse * (
        scaled - sums[0][..., None] / total_width - normed * sums[1][..., None] / total_width
    )
    return grad_in, jnp.sum(grad_out * normed, axis=0), jnp.sum(grad_out, axis=0)


def body(
    block_input,
    lengths,
    norm1_gain,
    norm1_bias,
    a_decay,
    a_freq,
    b_state,
    c_state,
    step_size,
    skip_gain,
    w_value,
    b_value,
    w_gate,
    b_gate,
    norm2_gain,
    norm2_bias,
    w_up,
    b_up,
    w_down,
    b_down,
    out_grad,
):
    batch, block, width = block_input.shape
    chans = lax.axis_size("chan")
    seqs = lax.axis_size("seq")
    assert seqs % batch == 0
    runs = seqs // batch
    total_width = width * chans
    assert chans == 4 and batch == 8 and block == 2 * a_decay.shape[0]
    seq_me = lax.axis_index("seq")
    chan_me = lax.axis_index("chan")
    groups = None if runs == 1 else [[r * batch + j for j in range(batch)] for r in range(runs)]
    peers = None if runs == 1 else [[r * batch + j for r in range(runs)] for j in range(batch)]

    def exchange(x):
        return lax.all_to_all(x, "seq", 0, 0, axis_index_groups=groups, tiled=True)

    def rows_of(w):
        return [
            lax.dynamic_slice_in_dim(w, (chan_me ^ d) * width, width, 0) for d in range(chans)
        ]

    moved = exchange(jnp.concatenate([block_input, out_grad], axis=-1)).reshape(batch * block, 2 * width)

    consts, base = s4_consts(a_decay, a_freq, b_state, c_state, step_size, block)
    z, m = s4_tables(base, consts, 0, 1)
    moved = after(moved, z)
    inputs = moved[:, :width].astype(FULL)
    grad_low = moved[:, width:]
    moments = sum_chan(jnp.stack([jnp.sum(inputs, axis=-1), jnp.sum(inputs * inputs, axis=-1)]))
    states = a_decay.shape[0]

    def const_factor(k):
        return consts[k, :, :states], consts[k + 1, :, states:]

    begin = (seq_me // batch) * batch * block
    places = begin + jnp.arange(batch * block, dtype=jnp.int32)
    mask = (places < lengths[seq_me % batch]).astype(FULL)[:, None]
    norm_one, normed_one, inverse_one = layer_forward(inputs, norm1_gain, norm1_bias, total_width, moments)
    signal = (mask * norm_one).astype(LOW)
    skip = skip_gain[None, :]
    init = jnp.zeros((width, 2 * states), FULL)
    if runs > 1:
        _, _, _, p, _, s = s4_forward(signal, skip, consts, z, m, init)
        carry = const_factor(CARRY)
        end = add(cmul(carry, split(s[:, -1])), cmul(const_factor(BBAR), split(p[:, -1])))
        ends = lax.all_gather(pair(*end), "seq", axis_index_groups=peers)
        hop = carry
        for _ in range(batch.bit_length() - 1):
            hop = cmul(hop, hop)
        for r in range(runs - 1):
            moved = add(cmul(hop, split(init)), split(ends[r]))
            init = jnp.where(r < seq_me // batch, pair(*moved), init)
    activ, slope, xs, ps, qs, ss = s4_forward(signal, skip, consts, z, m, init)

    wv, wg = rows_of(w_value), rows_of(w_gate)
    w_gated = [jnp.concatenate([a, b], axis=1) for a, b in zip(wv, wg)]
    w_ups = rows_of(w_up)
    w_downs = [
        lax.dynamic_slice_in_dim(w_down, (chan_me ^ d) * width, width, 1) for d in range(chans)
    ]
    grads = gather_pieces(grad_low)
    activs = gather_pieces(after(activ, grads[2]))
    both = sum(dot(a, w) for a, w in zip(activs, w_gated))
    value = both[:, :width] + b_value
    gate = both[:, width:] + b_gate
    opened = jax.nn.sigmoid(gate)
    resid = inputs + value * opened
    norm_two, normed_two, inverse_two = layer_forward(resid, norm2_gain, norm2_bias, total_width)
    norms = gather_pieces(norm_two.astype(LOW))
    hidden = sum(dot(a, w) for a, w in zip(norms, w_ups)) + b_up
    spread, gelu_pull = jax.vjp(jax.nn.gelu, hidden)
    spread = spread.astype(LOW)

    grad_out = grad_low.astype(FULL)
    grad_spread = sum(dot_t(a, w) for a, w in zip(grads, w_downs))
    grad_hidden = gelu_pull(grad_spread)[0].astype(LOW)
    grad_w_down = t_dot(after(spread, grad_hidden), jnp.concatenate(grads, axis=1)).astype(LOW)
    downs_dealt = deal(grad_w_down)
    marks = []
    hidden_late = after(grad_hidden, grad_w_down)
    grad_norm_two = reduce_pieces([dot_t(hidden_late, w) for w in w_ups], marks)
    grad_w_up = t_dot(jnp.concatenate(norms, axis=1), after(grad_hidden, *marks[:2])).astype(LOW)
    grad_norm_two = after(grad_norm_two, grad_w_up)
    chains = []

    def start_ups(dep):
        chains.append(Chain([downs_dealt, deal(after(grad_w_up, dep))], True))
        return []

    grad_resid, grad_norm2_gain, grad_norm2_bias = layer_backward(
        grad_norm_two, normed_two, inverse_two, norm2_gain, total_width, start_ups
    )
    wide_chain = chains[0]
    grad_resid = grad_out + grad_resid
    grad_value = (grad_resid * opened).astype(LOW)
    grad_gate = (grad_resid * value * opened * (1.0 - opened)).astype(LOW)
    grad_both = jnp.concatenate([grad_value, grad_gate], axis=1)
    marks = []
    grad_activ = reduce_pieces([dot_t(grad_both, w) for w in w_gated], marks)
    grad_w_gated = t_dot(jnp.concatenate(activs, axis=1), after(grad_both, *marks[:2])).astype(LOW)
    gated_chain = Chain([deal(after(grad_w_gated, grad_activ))], False)
    grad_activ = after(grad_activ, grad_w_gated)
    grad_mixed = (grad_activ * slope).astype(LOW)
    made = advance([wide_chain], grad_mixed)
    init = jnp.zeros((width, 2 * states), FULL)
    if runs > 1:
        _, _, u, _, h = s4_backward(grad_mixed, consts, z, m, init)
        end = add(cmul(carry, split(h[:, 0])), cmul(const_factor(READ), split(u[:, 0])))
        ends = lax.all_gather(pair(*end), "seq", axis_index_groups=peers)
        for r in reversed(range(1, runs)):
            moved = add(cmul(hop, split(init)), split(ends[r]))
            init = jnp.where(r > seq_me // batch, pair(*moved), init)
    grad_signal, gs, us, vs, hs = s4_backward(grad_mixed, consts, z, m, init, made)
    grad_signal = after(grad_signal, *advance([wide_chain, gated_chain], grad_signal))
    grad_signal = grad_signal + skip * grad_mixed.astype(FULL)
    s4_parts = (xs, gs, ps, qs, ss, us, vs, hs, z, consts, block)
    grad_input, grad_norm1_gain, grad_norm1_bias = layer_backward(
        grad_signal * mask, normed_one, inverse_one, norm1_gain, total_width, lambda dep: []
    )
    grad_input = (grad_resid + grad_input).astype(LOW)
    wide_own = gather(wide_chain.parts[0])
    sums = s4_sums(*s4_parts, [grad_input], 0, width // CHANNELS)
    narrow = jnp.concatenate(
        [
            grad_norm1_gain,
            grad_norm1_bias,
            jnp.sum(grad_mixed.astype(FULL) * signal.astype(FULL), axis=0),
            jnp.sum(grad_value.astype(FULL), axis=0),
            jnp.sum(grad_gate.astype(FULL), axis=0),
            grad_norm2_gain,
            grad_norm2_bias,
            jnp.sum(grad_out, axis=0),
            sums[3, :, 0],
            jnp.sum(grad_hidden.astype(FULL), axis=0),
        ]
    )
    packed = pack_small(sums, narrow)
    dealt = exchange_all(packed)
    made = join_sum(wide_chain.parts[1], *gated_chain.parts, [packed, *wide_own[1:]])
    last = gather_relayed(made)
    spread_late = after(spread, made)
    output = reduce_pieces([dot(spread_late, w) for w in w_downs])
    output = (resid + output + b_down).astype(LOW)
    parts, wide, narrow = sum_small(dealt, sums, narrow.shape[0], last[1:3])
    moved = beside(grad_input, output, [parts, *last[1:]])
    moved = exchange(moved.reshape(batch, block, 2 * width))
    grad_input, output = moved[:, :, :width].astype(FULL), moved[:, :, width:]
    vectors = [narrow[k * width : (k + 1) * width] for k in range(9)]
    vectors.insert(2, vectors.pop(8))

    zero = 0 * chan_me
    (down,) = finish([wide_own, last], 0, 2, total_width, 0, zero, chan_me >> 1, chan_me & 1)
    (up,) = finish([wide_own, last], 1, 2, grad_w_up.shape[1], 0, chan_me, zero, zero)
    grad_w_value, grad_w_gate = finish([last], 0, 1, 2 * width, total_width, chan_me, zero, zero, 2)
    return (
        output,
        grad_input,
        vectors[0],
        vectors[1],
        *wide,
        vectors[2],
        vectors[3],
        grad_w_value,
        vectors[4],
        grad_w_gate,
        vectors[5],
        vectors[6],
        vectors[7],
        up,
        narrow[9 * width :],
        down,
        vectors[8],
    )


def solution(mesh):
    in_specs = (
        P(None, "seq", "chan"),
        P(),
        P("chan"),
        P("chan"),
        P(None, "chan"),
        P(None, "chan"),
        P(None, None, "chan"),
        P(None, None, "chan"),
        P("chan"),
        P("chan"),
        P(None, "chan"),
        P("chan"),
        P(None, "chan"),
        P("chan"),
        P("chan"),
        P("chan"),
        P(None, "chan"),
        P("chan"),
        P("chan", None),
        P("chan"),
        P(None, "seq", "chan"),
    )
    out_specs = (
        P(None, "seq", "chan"),
        P(None, "seq", "chan"),
        P("chan"),
        P("chan"),
        P(None, "chan"),
        P(None, "chan"),
        P(None, None, "chan"),
        P(None, None, "chan"),
        P("chan"),
        P("chan"),
        P(None, "chan"),
        P("chan"),
        P(None, "chan"),
        P("chan"),
        P("chan"),
        P("chan"),
        P(None, "chan"),
        P("chan"),
        P("chan", None),
        P("chan"),
    )
    return jax.shard_map(body, mesh=mesh, in_specs=in_specs, out_specs=out_specs, check_vma=False)
```

```python
import jax
import jax.numpy as jnp
from jax import lax
from jax.experimental import pallas as pl
from jax.experimental.pallas import tpu as pltpu
from jax.sharding import PartitionSpec as P

EPSILON = 1e-05
LOW = jnp.bfloat16
FULL = jnp.float32
CHANNELS = 32
WIDE = 64
UNROLL = 32
SCALE = 1.0e5
VMEM = 56 * 1024 * 1024


def swap(x, axis, distance):
    return lax.ppermute(x, axis, [(i, i ^ distance) for i in range(lax.axis_size(axis))])


def axis_bits(axis):
    size = lax.axis_size(axis)
    bits = size.bit_length() - 1
    assert size == 1 << bits
    return bits


def gather_pieces(x):
    pieces = {0: x}
    for bit in reversed(range(axis_bits("chan"))):
        for d in list(pieces):
            pieces[d ^ (1 << bit)] = swap(pieces[d], "chan", 1 << bit)
    return [pieces[d] for d in range(len(pieces))]


def reduce_pieces(parts, marks=None):
    sums = dict(enumerate(parts))
    for bit in range(axis_bits("chan")):
        if marks is not None and bit == axis_bits("chan") - 1:
            marks += [sums[1 << bit], sums[0]]
        for d in sorted(sums, reverse=True):
            if d >> bit & 1:
                received = swap(sums.pop(d).astype(LOW), "chan", 1 << bit)
                if marks is not None and d == 1 << (axis_bits("chan") - 1):
                    marks.append(received)
                sums[d ^ (1 << bit)] = sums[d ^ (1 << bit)] + received.astype(FULL)
    return sums[0]


def sum_chan(x):
    return x + sum(swap(x, "chan", d) for d in range(1, lax.axis_size("chan")))


def after(x, *others):
    return lax.optimization_barrier((x, others))[0]


def exchange_all(x):
    return lax.all_to_all(x, "seq", 0, 0, tiled=True)


def small_shares(sums, size):
    seqs = lax.axis_size("seq")
    groups, width, lanes = sums.shape
    short = -(-size // (seqs * lanes))
    assert short <= 8
    share = (groups - 1) * width // seqs
    return share, short, -(-(share + 16) // 16) * 16


def pack_small(sums, narrow):
    seqs = lax.axis_size("seq")
    groups, width, lanes = sums.shape
    size = narrow.shape[0]
    share, short, rows = small_shares(sums, size)
    narrow_rows = jnp.pad(narrow, (0, seqs * short * lanes - size)).reshape(seqs, short, lanes)
    narrow_rows = jnp.pad(narrow_rows, ((0, 0), (0, 8 - short), (0, 0)))

    def pack(sums, narrow, packed):
        flat = sums[: groups - 1].reshape((groups - 1) * width, lanes)
        for k in range(seqs):
            part = narrow[k]
            high = part.astype(LOW).astype(FULL)
            pieces = [flat[k * share : (k + 1) * share], high, part - high]
            if rows > share + 16:
                pieces.append(jnp.zeros((rows - share - 16, lanes), FULL))
            packed[k] = jnp.concatenate(pieces, axis=0).astype(LOW)

    shape = jax.ShapeDtypeStruct((seqs, rows, lanes), LOW)
    return call_here(pack, [sums, narrow_rows], [], [shape], "pack_small")[0]


def sum_small(dealt, sums, size, deps):
    seqs, rows, lanes = dealt.shape
    groups, width, _ = sums.shape
    share, short, _ = small_shares(sums, size)

    def add(dealt, out):
        total = sum(dealt[k].astype(FULL) for k in range(seqs))
        narrow = total[share : share + 8] + total[share + 8 : share + 16]
        high = narrow.astype(LOW).astype(FULL)
        pieces = [total[:share], high, narrow - high] + ([total[share + 16 :]] if rows > share + 16 else [])
        total = jnp.concatenate(pieces, axis=0).astype(LOW)
        for k in range(seqs):
            out[k] = total

    parts = exchange_all(call_here(add, [dealt], deps, [jax.ShapeDtypeStruct(dealt.shape, LOW)], "sum_small")[0])
    states = lanes // 2

    def unpack(parts, decay, freq, b, c, narrow):
        flat = jnp.concatenate([parts[k, :share, :].astype(FULL) for k in range(seqs)], axis=0)
        a, b_both, c_both = (flat[g * width : (g + 1) * width].T for g in range(3))
        decay[...], freq[...] = a[:states], a[states:]
        b[0], b[1] = b_both[:states], b_both[states:]
        c[0], c[1] = c_both[:states], c_both[states:]
        for k in range(seqs):
            part = parts[k].astype(FULL)
            narrow[k] = part[share : share + 8] + part[share + 8 : share + 16]

    one, two = (states, width), (2, states, width)
    *wide, narrow = call_here(
        unpack,
        [parts],
        [],
        [jax.ShapeDtypeStruct(shape, FULL) for shape in (one, one, two, two, (seqs, 8, lanes))],
        "unpack_small",
    )
    return parts, wide, narrow[:, :short].reshape(-1)[:size]


def beside(left, right, deps):
    rows, columns = left.shape

    def kernel(left, right, out):
        out[:, :columns] = left[...]
        out[:, columns:] = right[...]

    shape = jax.ShapeDtypeStruct((rows, columns + right.shape[1]), left.dtype)
    return call_here(kernel, [left, right], deps, [shape], "beside")[0]


def call_here(kernel, ins, deps, outs, name):
    here, anywhere = pl.BlockSpec(memory_space=pltpu.VMEM), pl.BlockSpec(memory_space=pl.ANY)
    return pl.pallas_call(
        lambda *refs: kernel(*refs[: len(ins)], *refs[len(ins) + len(deps) :]),
        in_specs=[here] * len(ins) + [anywhere] * len(deps),
        out_specs=[here] * len(outs),
        out_shape=outs,
        compiler_params=pltpu.CompilerParams(vmem_limit_bytes=VMEM),
        cost_estimate=cost(2),
        name=name,
    )(*ins, *deps)


QUAD = 4


def deal(x):
    seqs = lax.axis_size("seq")
    groups = [list(range(i, i + QUAD)) for i in range(0, seqs, QUAD)]
    return lax.all_to_all(x.reshape(QUAD, -1, x.shape[1]), "seq", 0, 0, axis_index_groups=groups, tiled=True)


class Chain:
    def __init__(self, parts, halves):
        self.masks = [1 << bit for bit in range(axis_bits("seq")) if 1 << bit >= QUAD]
        self.parts = parts
        self.halves = halves
        self.tasks = ["deal" if halves else "whole", "sum"]

    def accept(self, task, outs):
        if task == "deal":
            self.parts = [outs[0], swap(outs[1], "seq", self.masks[0])]
            return
        total = outs[0]
        for mask in self.masks[1:]:
            total = (total.astype(FULL) + swap(total, "seq", mask).astype(FULL)).astype(LOW)
        self.parts = [total]
        if task == "whole" or self.halves:
            self.parts.append(swap(total, "seq", self.masks[0]))


def gather(part):
    return [part] + [swap(part, "seq", mask) for mask in range(1, QUAD)]


def gather_relayed(part):
    first, second = swap(part, "seq", 1), swap(part, "seq", 2)
    half = part.shape[0] // 2
    third = jnp.concatenate([swap(second[:half], "seq", 1), swap(first[half:], "seq", 2)])
    return [part, first, second, third]


def join_sum(left, own, received, deps):
    rows, columns = left.shape

    def kernel(left, own, received, *refs):
        out = refs[-1]
        out[:, :columns] = left[...]
        out[:, columns:] = (own[...].astype(FULL) + received[...].astype(FULL)).astype(LOW)

    here, anywhere = pl.BlockSpec(memory_space=pltpu.VMEM), pl.BlockSpec(memory_space=pl.ANY)
    return pl.pallas_call(
        kernel,
        in_specs=[here] * 3 + [anywhere] * len(deps),
        out_specs=here,
        out_shape=jax.ShapeDtypeStruct((rows, columns + own.shape[1]), LOW),
        compiler_params=pltpu.CompilerParams(vmem_limit_bytes=VMEM),
        cost_estimate=cost(2),
        name="join_sum",
    )(left, own, received, *deps)


def advance(chains, *deps):
    tasks = [chain.tasks.pop(0) for chain in chains]
    parts = [chain.parts for chain in chains]
    shapes = []
    for task, part in zip(tasks, parts):
        rows, columns = part[0].shape[-2:]
        made = {"deal": [rows // 2 * len(part)] * 2, "whole": [rows * len(part)], "sum": [rows]}[task]
        shapes.append([jax.ShapeDtypeStruct((size, columns), LOW) for size in made])
    counts = [len(part) for part in parts]
    me = lax.axis_index("seq")
    high = (me // QUAD % 2).astype(jnp.int32)[None]

    def kernel(high, *refs):
        ins = list(refs[: sum(counts)])
        outs = list(refs[len(refs) - sum(len(shape) for shape in shapes) :])
        for task, count in zip(tasks, counts):
            refs = [ins.pop(0) for _ in range(count)]
            if task == "deal":
                half = refs[0].shape[1] // 2
                for block in (high[0], 1 - high[0]):
                    place = pl.ds(pl.multiple_of(block * half, half), half)
                    out = outs.pop(0)
                    for i, ref in enumerate(refs):
                        out[i * half : (i + 1) * half, :] = sum(
                            ref[k, place, :].astype(FULL) for k in range(QUAD)
                        ).astype(LOW)
            elif task == "whole":
                out = outs.pop(0)
                rows = refs[0].shape[1]
                for i, ref in enumerate(refs):
                    out[i * rows : (i + 1) * rows, :] = sum(ref[k].astype(FULL) for k in range(QUAD)).astype(LOW)
            else:
                outs.pop(0)[...] = (refs[0][...].astype(FULL) + refs[1][...].astype(FULL)).astype(LOW)

    here, anywhere = pl.BlockSpec(memory_space=pltpu.VMEM), pl.BlockSpec(memory_space=pl.ANY)
    results = list(
        pl.pallas_call(
            kernel,
            in_specs=[pl.BlockSpec(memory_space=pltpu.SMEM)] + [here] * sum(counts) + [anywhere] * len(deps),
            out_specs=[here] * sum(len(shape) for shape in shapes),
            out_shape=[one for shape in shapes for one in shape],
            compiler_params=pltpu.CompilerParams(vmem_limit_bytes=VMEM),
            cost_estimate=cost(2),
            name="advance",
        )(high, *[array for part in parts for array in part], *deps)
    )
    rest = list(results)
    for task, chain, shape in zip(tasks, chains, shapes):
        chain.accept(task, [rest.pop(0) for _ in shape])
    return results


def finish(groups, slot, slots, columns, first, row_turn, half_turn, column_turn, outputs=1):
    rows = groups[0][0].shape[0] // slots
    width = columns // 4
    skip = first // (2 * width)
    me = lax.axis_index("seq")
    high = me // QUAD % 2
    scalars = jnp.stack([(me & (QUAD - 1)) ^ row_turn, half_turn, column_turn, high]).astype(jnp.int32)
    count = len(groups)

    def kernel(scalars, *refs):
        ins, outs = refs[: count * QUAD], refs[-outputs:]

        def put(out):
            for k in range(count):
                for q in range(QUAD):
                    block = (scalars[0] ^ q) * count
                    if count == 2:
                        block = block + (scalars[3] ^ k)
                    target = pl.ds(pl.multiple_of(block * rows, rows), rows)
                    ref = ins[k * QUAD + q]
                    for e in range(2):
                        place = pl.ds(pl.multiple_of((e ^ scalars[2]) * width, width), width)
                        out[target, place] = ref[:, e * width : (e + 1) * width].astype(FULL)

        if outputs == 1:
            put(outs[0])
        else:
            for k in range(2):
                pl.when(pl.program_id(0) == k)(lambda k=k: put(outs[k]))

    return pl.pallas_call(
        kernel,
        grid_spec=pltpu.PrefetchScalarGridSpec(
            num_scalar_prefetch=1,
            grid=(2,),
            in_specs=[pl.BlockSpec((rows, 2 * width), lambda half, n: (slot, half + skip))] * (count * QUAD),
            out_specs=[
                pl.BlockSpec(
                    (count * QUAD * rows, 2 * width),
                    (lambda half, n: (0, half ^ n[1])) if outputs == 1 else (lambda half, n: (0, 0)),
                )
            ]
            * outputs,
        ),
        out_shape=[jax.ShapeDtypeStruct((count * QUAD * rows, columns // outputs), FULL)] * outputs,
        compiler_params=pltpu.CompilerParams(vmem_limit_bytes=VMEM),
        cost_estimate=cost(3),
        name="finish",
    )(scalars, *[part for group in groups for part in group])


def cost(us):
    return pl.CostEstimate(flops=0, bytes_accessed=int(us * SCALE), transcendentals=0)


def pair(re, im):
    return jnp.concatenate([re, im], axis=-1)


def factor(re, im):
    return pair(re, re), pair(-im, im)


def times(x, first, second):
    lanes = x.shape[-1]
    return x * first + pltpu.roll(x, lanes // 2, x.ndim - 1) * second


def cmul(a, b):
    return a[0] * b[0] - a[1] * b[1], a[0] * b[1] + a[1] * b[0]


def add(a, b):
    return a[0] + b[0], a[1] + b[1]


def scale(a, k):
    return a[0] * k, a[1] * k


BBAR, READ, CARRY, STRIDE, KERNEL, Z, RATIO, C, B, A_PART, STEP = 0, 2, 4, 10, 18, 19, 21, 23, 25, 27, 29
ROWS = 30


def less_one(x):
    total = 1.0 + x / 8.0
    for k in (7.0, 6.0, 5.0, 4.0, 3.0, 2.0):
        total = 1.0 + x / k * total
    return jnp.where(x > -0.25, x * total, jnp.exp(x) - 1.0)


def consts_kernel(block, decay_ref, freq_ref, b_ref, c_ref, step_ref, consts, base):
    states, width = decay_ref.shape
    lanes = 2 * states

    def wide(x):
        return jnp.concatenate([x, x], axis=0).T

    decay, freq = wide(decay_ref[...]), wide(freq_ref[...])
    b = (wide(b_ref[0]), wide(b_ref[1]))
    c = (wide(c_ref[0]), wide(c_ref[1]))
    step = jnp.broadcast_to(step_ref[...], (lanes, width)).T
    first = lax.broadcasted_iota(jnp.int32, (width, lanes), 1) < states
    rate = step * decay
    turn = step * freq
    size = jnp.exp(-rate)
    z = (size * jnp.cos(turn), size * jnp.sin(turn))
    half_turn = jnp.sin(0.5 * turn)
    less = (less_one(-rate) * jnp.cos(turn) - 2.0 * half_turn * half_turn, z[1])
    modulus = decay * decay + freq * freq
    ratio = (
        (freq * less[1] - decay * less[0]) / modulus,
        -(decay * less[1] + freq * less[0]) / modulus,
    )
    bbar = cmul(ratio, b)
    twice_c = scale(c, 2.0)

    def put_factor(k, x):
        consts[k] = x[0]
        consts[k + 1] = jnp.where(first, -x[1], x[1])

    def put_plain(k, x):
        consts[k] = x[0]
        consts[k + 1] = x[1]

    put_factor(BBAR, bbar)
    put_factor(READ, cmul(twice_c, z))
    kernel = cmul(twice_c, bbar)
    consts[KERNEL] = jnp.where(first, kernel[0], -kernel[1])
    put_plain(Z, z)
    put_plain(RATIO, ratio)
    put_plain(C, c)
    put_plain(B, b)
    consts[A_PART] = decay
    consts[A_PART + 1] = freq
    consts[STEP] = step
    power = (jnp.ones_like(size), jnp.zeros_like(size))
    for k in range(8):
        base[k] = jnp.where(first, power[0], power[1])
        power = cmul(power, z)
    k = 8
    while k < 4 * block:
        if k <= 64:
            put_factor(STRIDE + 2 * (k.bit_length() - 4), power)
        if k >= block:
            put_factor(CARRY + 2 * ((k // block).bit_length() - 1), power)
        power = cmul(power, power)
        k *= 2
    put_factor(CARRY + 4, power)


def s4_consts(a_decay, a_freq, b_state, c_state, step_size, block):
    states, width = a_decay.shape
    return pl.pallas_call(
        lambda *refs: consts_kernel(block, *refs),
        out_shape=[
            jax.ShapeDtypeStruct((ROWS, width, 2 * states), FULL),
            jax.ShapeDtypeStruct((8, width, 2 * states), FULL),
        ],
        compiler_params=pltpu.CompilerParams(vmem_limit_bytes=VMEM),
        cost_estimate=cost(6),
        name="s4_consts",
    )(a_decay, a_freq, b_state, c_state, step_size[None, :])


def half_turned(x):
    return pltpu.roll(x, x.shape[-1] // 2, x.ndim - 1)


def high_low(x):
    high = x.astype(LOW)
    return high, (x - high.astype(FULL)).astype(LOW)


def dot(a, b):
    return lax.dot_general(a, b, (((1,), (0,)), ((), ())), preferred_element_type=FULL)


def dot_t(a, b):
    return lax.dot_general(a, b, (((1,), (1,)), ((), ())), preferred_element_type=FULL)


def tables_kernel(base, consts, *refs):
    z_out, h_out = refs[-2:]
    channels, _, lanes = z_out.shape
    row8 = lax.broadcasted_iota(jnp.int32, (8, lanes), 0)
    row = lax.broadcasted_iota(jnp.int32, (lanes, lanes), 0)
    lane = lax.broadcasted_iota(jnp.int32, (lanes, lanes), 1)
    live = row + lane >= lanes - 1

    def one(c):
        first = jnp.concatenate([base[k, pl.ds(c, 1), :] for k in range(8)], axis=0)
        tiles = [(first, half_turned(first))]
        for level in range(4):
            k = STRIDE + 2 * level
            a, b = consts[k, pl.ds(c, 1), :], consts[k + 1, pl.ds(c, 1), :]
            tiles += [(t * a + u * b, u * a - t * b) for t, u in tiles]
        z = jnp.concatenate([t for t, _ in tiles], axis=0)
        high, low = high_low(z)
        z_out[c, :lanes, :] = high
        z_out[c, lanes:, :] = low
        f_high, f_low = high_low(jnp.broadcast_to(consts[KERNEL, pl.ds(c, 1), :], (8, lanes)))
        h = dot_t(jnp.concatenate([f_high, f_low], axis=0), high)
        h = h[:8] + h[8:] + dot_t(f_high, low)
        for bit in (1, 2, 4):
            h = jnp.where((7 - row8) & bit != 0, pltpu.roll(h, bit, 1), h)
        hankel = [pltpu.roll(h, lanes - 8 - k, 1) if k < lanes - 8 else h for k in range(0, lanes, 8)]
        hankel = jnp.concatenate(hankel, axis=0)
        h_out[c] = jnp.where(live, hankel, 0.0).astype(LOW)

    @pl.loop(0, channels, step=UNROLL)
    def _(c):
        for k in range(UNROLL):
            one(c + k)


def s4_tables(base, consts, part, parts, tables=(), deps=()):
    _, width, lanes = base.shape
    steps = width // CHANNELS // parts
    skip = part * steps
    anywhere = pl.BlockSpec(memory_space=pl.ANY)
    return pl.pallas_call(
        tables_kernel,
        grid=(steps,),
        in_specs=[
            pl.BlockSpec((8, CHANNELS, lanes), lambda i: (0, i + skip, 0)),
            pl.BlockSpec((ROWS, CHANNELS, lanes), lambda i: (0, i + skip, 0)),
        ]
        + [anywhere] * (len(tables) + len(deps)),
        out_specs=[
            pl.BlockSpec((CHANNELS, 2 * lanes, lanes), lambda i: (i + skip, 0, 0)),
            pl.BlockSpec((CHANNELS, lanes, lanes), lambda i: (i + skip, 0, 0)),
        ],
        out_shape=[
            jax.ShapeDtypeStruct((width, 2 * lanes, lanes), LOW),
            jax.ShapeDtypeStruct((width, lanes, lanes), LOW),
        ],
        input_output_aliases={2: 0, 3: 1} if tables else {},
        compiler_params=pltpu.CompilerParams(vmem_limit_bytes=VMEM),
        cost_estimate=cost(24 / parts),
        name="s4_tables",
    )(base, consts, *tables, *deps)


def flip_matrix(size):
    row = lax.broadcasted_iota(jnp.int32, (size, size), 0)
    lane = lax.broadcasted_iota(jnp.int32, (size, size), 1)
    return (row + lane == size - 1).astype(FULL).astype(LOW)


def rows_of_channels(consts, k):
    return jnp.stack([consts[k, c : c + 1, :] for c in range(consts.shape[1])])


def weighted_ends(x, place, z):
    high, low = high_low(x * place)
    x = x.astype(LOW)
    none = jnp.zeros_like(x)
    left = jnp.concatenate([x, high, low, none], axis=0)
    right = jnp.concatenate([x, high, none, none], axis=0)
    ends = dot(jnp.concatenate([left, right], axis=1), z)
    count = x.shape[0]
    return ends[:count], ends[count : 2 * count] + ends[2 * count : 3 * count]


def times_both(x, consts, k):
    first, second = rows_of_channels(consts, k), rows_of_channels(consts, k + 1)
    return x[0] * first + x[1] * second, x[1] * first - x[0] * second


def scan_blocks(x, consts, row, reverse):
    count = x[0].shape[1]
    for level, d in enumerate((1, 2, 4)):
        live = row < count - d if reverse else row >= d
        moved = [jnp.where(live, pltpu.roll(e, count - d if reverse else d, 1), 0.0) for e in x]
        x = add(x, times_both(moved, consts, CARRY + 2 * level))
    return x


def forward_kernel(
    signal, skip, consts, z, m, init, activ, slope, x_out, p_out, q_out, s_out, x_scr, y_scr
):
    step = pl.program_id(0)
    channels, _, lanes = z.shape
    count = signal.shape[0] // lanes
    width = signal.shape[1]

    @pl.when(step == 0)
    def _():
        flip = flip_matrix(lanes)
        for j in range(count):
            x_scr[pl.ds(j, width, stride=count), :] = dot(flip, signal[j * lanes : (j + 1) * lanes, :]).T

    rows = pl.ds(pl.multiple_of(step * channels * count, channels * count), channels * count)
    x = x_scr[rows, :].reshape(channels, count, lanes)
    place = lax.broadcasted_iota(jnp.int32, (count, lanes), 1).astype(FULL)
    row = lax.broadcasted_iota(jnp.int32, (channels, count, lanes), 1)
    plus = lax.broadcasted_iota(jnp.int32, (channels, count, lanes), 2) < lanes // 2
    ends = [weighted_ends(x[c], place, z[c]) for c in range(channels)]
    p = jnp.stack([e[0] for e in ends])
    q = jnp.stack([e[1] for e in ends])
    start = init[...][:, None, :]
    state = times_both((p, half_turned(p)), consts, BBAR)
    state = [
        jnp.where(row == 0, e, pltpu.roll(s, 1, 1)) for e, s in zip((start, half_turned(start)), state)
    ]
    state = scan_blocks(state, consts, row, False)
    read, _ = times_both(state, consts, READ)
    read = jnp.where(plus, read, -read).astype(LOW)
    y = [dot(x[c].astype(LOW), m[c]) + dot_t(read[c], z[c, :lanes, :]) for c in range(channels)]
    y_scr[rows, :] = jnp.concatenate(y, axis=0)
    x_out[...] = x
    p_out[...] = p
    q_out[...] = q
    s_out[...] = state[0]

    @pl.when(step == pl.num_programs(0) - 1)
    def _():
        for j in range(count):
            part = slice(j * lanes, (j + 1) * lanes)
            mixed = y_scr[pl.ds(j, width, stride=count), :].T + skip[...] * signal[part, :].astype(FULL)
            inner = 0.7978845608028654 * (mixed + 0.044715 * mixed * mixed * mixed)
            bent = jnp.tanh(inner)
            activ[part, :] = (0.5 * mixed * (1.0 + bent)).astype(LOW)
            slope[part, :] = 0.5 * (1.0 + bent) + 0.5 * mixed * (1.0 - bent * bent) * (
                0.7978845608028654 * (1.0 + 3 * 0.044715 * mixed * mixed)
            )


def s4_forward(signal, skip, consts, z, m, init):
    tokens, width = signal.shape
    lanes = z.shape[-1]
    count = tokens // lanes
    whole = pl.BlockSpec((tokens, width), lambda i: (0, 0))
    by_channel = pl.BlockSpec((WIDE, count, lanes), lambda i: (i, 0, 0))
    per_channel = jax.ShapeDtypeStruct((width, count, lanes), FULL)
    return pl.pallas_call(
        forward_kernel,
        grid=(width // WIDE,),
        in_specs=[
            whole,
            pl.BlockSpec((1, width), lambda i: (0, 0)),
            pl.BlockSpec((ROWS, WIDE, lanes), lambda i: (0, i, 0)),
            pl.BlockSpec((WIDE, 2 * lanes, lanes), lambda i: (i, 0, 0)),
            pl.BlockSpec((WIDE, lanes, lanes), lambda i: (i, 0, 0)),
            pl.BlockSpec((WIDE, lanes), lambda i: (i, 0)),
        ],
        out_specs=[whole, whole] + [by_channel] * 4,
        out_shape=[
            jax.ShapeDtypeStruct((tokens, width), LOW),
            jax.ShapeDtypeStruct((tokens, width), FULL),
        ]
        + [per_channel] * 4,
        scratch_shapes=[pltpu.VMEM((width * count, lanes), FULL)] * 2,
        compiler_params=pltpu.CompilerParams(vmem_limit_bytes=VMEM),
        cost_estimate=cost(18),
        name="s4_forward",
    )(signal, skip, consts, z, m, init)


def backward_kernel(grads, consts, z, m, init, *refs):
    out, g_out, u_out, v_out, h_out, g_scr, y_scr = refs[-7:]
    step = pl.program_id(0)
    channels, _, lanes = z.shape
    count = grads.shape[0] // lanes
    width = grads.shape[1]

    @pl.when(step == 0)
    def _():
        for j in range(count):
            g_scr[pl.ds(j, width, stride=count), :] = grads[j * lanes : (j + 1) * lanes, :].astype(FULL).T

    rows = pl.ds(pl.multiple_of(step * channels * count, channels * count), channels * count)
    g = g_scr[rows, :].reshape(channels, count, lanes)
    place = lax.broadcasted_iota(jnp.int32, (count, lanes), 1).astype(FULL)
    row = lax.broadcasted_iota(jnp.int32, (channels, count, lanes), 1)
    plus = lax.broadcasted_iota(jnp.int32, (channels, count, lanes), 2) < lanes // 2
    ends = [weighted_ends(g[c], place, z[c]) for c in range(channels)]
    u = jnp.stack([e[0] for e in ends])
    v = jnp.stack([e[1] for e in ends])
    start = init[...][:, None, :]
    later = times_both((u, half_turned(u)), consts, READ)
    later = [
        jnp.where(row == count - 1, e, pltpu.roll(s, count - 1, 1))
        for e, s in zip((start, half_turned(start)), later)
    ]
    later = scan_blocks(later, consts, row, True)
    write, _ = times_both(later, consts, BBAR)
    write = jnp.where(plus, write, -write).astype(LOW)
    y = [dot(g[c].astype(LOW), m[c]) + dot_t(write[c], z[c, :lanes, :]) for c in range(channels)]
    y_scr[rows, :] = jnp.concatenate(y, axis=0)
    g_out[...] = g
    u_out[...] = u
    v_out[...] = v
    h_out[...] = later[0]

    @pl.when(step == pl.num_programs(0) - 1)
    def _():
        flip = flip_matrix(lanes)
        for j in range(count):
            out[j * lanes : (j + 1) * lanes, :] = dot(
                flip, y_scr[pl.ds(j, width, stride=count), :].T.astype(LOW)
            )


def s4_backward(grads, consts, z, m, init, deps=()):
    tokens, width = grads.shape
    lanes = z.shape[-1]
    count = tokens // lanes
    whole = pl.BlockSpec((tokens, width), lambda i: (0, 0))
    by_channel = pl.BlockSpec((WIDE, count, lanes), lambda i: (i, 0, 0))
    per_channel = jax.ShapeDtypeStruct((width, count, lanes), FULL)
    return pl.pallas_call(
        backward_kernel,
        grid=(width // WIDE,),
        in_specs=[
            whole,
            pl.BlockSpec((ROWS, WIDE, lanes), lambda i: (0, i, 0)),
            pl.BlockSpec((WIDE, 2 * lanes, lanes), lambda i: (i, 0, 0)),
            pl.BlockSpec((WIDE, lanes, lanes), lambda i: (i, 0, 0)),
            pl.BlockSpec((WIDE, lanes), lambda i: (i, 0)),
        ]
        + [pl.BlockSpec(memory_space=pl.ANY)] * len(deps),
        out_specs=[whole] + [by_channel] * 4,
        out_shape=[jax.ShapeDtypeStruct((tokens, width), FULL)] + [per_channel] * 4,
        scratch_shapes=[pltpu.VMEM((width * count, lanes), FULL)] * 2,
        compiler_params=pltpu.CompilerParams(vmem_limit_bytes=VMEM),
        cost_estimate=cost(18),
        name="s4_backward",
    )(grads, consts, z, m, init, *deps)


def sums_kernel(block, x, g, p, q, s, u, v, h, z, consts, *refs):
    out = refs[-1]
    channels, count, lanes = x.shape
    states = lanes // 2
    row8 = lax.broadcasted_iota(jnp.int32, (8, lanes), 0)
    row = lax.broadcasted_iota(jnp.int32, (lanes, lanes), 0)
    lane = lax.broadcasted_iota(jnp.int32, (lanes, lanes), 1)
    place = lax.broadcasted_iota(jnp.int32, (8, lanes), 1).astype(FULL)
    live = row + lane >= lanes - 1
    first = lax.broadcasted_iota(jnp.int32, (channels, lanes), 1) < states
    w = []
    for c in range(channels):
        both = lax.dot_general(
            x[c].astype(LOW), g[c].astype(LOW), (((0,), (0,)), ((), ())), preferred_element_type=FULL
        )
        both = jnp.where(live, both, 0.0)
        tiles = [both[k : k + 8, :] for k in range(0, lanes, 8)]
        shift = 8
        while len(tiles) > 1:
            tiles = [a + pltpu.roll(b, shift, 1) for a, b in zip(tiles[::2], tiles[1::2])]
            shift *= 2
        total = pltpu.roll(tiles[0], 1, 1)
        for bit in (1, 2, 4):
            total = jnp.where(row8 & bit != 0, pltpu.roll(total, bit, 1), total)
        high, low = high_low(total)
        place_high, place_low = high_low(total * place)
        none = jnp.zeros_like(high)
        left = jnp.concatenate([high, low, place_high, place_low], axis=0)
        right = jnp.concatenate([high, none, place_high, none], axis=0)
        w.append(dot(jnp.concatenate([left, right], axis=1), z[c]))
    lag0 = jnp.sum(jnp.stack([e[:16] for e in w]), axis=1)
    lag1 = jnp.sum(jnp.stack([e[16:] for e in w]), axis=1)

    def both_halves(x):
        turned = half_turned(x)
        return jnp.where(first, x, turned), jnp.where(first, turned, x)

    def product(a, b):
        plain = jnp.sum(a * b, axis=1)
        crossed = jnp.sum(a * half_turned(b), axis=1)
        plain = jnp.where(first, plain, -plain)
        return plain + half_turned(plain), crossed + half_turned(crossed)

    states_read = product(u[...], s[...])
    slopes_read = product(u[...] + v[...], s[...])
    writes = product(h[...], p[...])
    slopes_write = product(h[...], q[...])
    carried = product(h[...], s[...])
    lag0, lag1 = both_halves(lag0), both_halves(lag1)

    def const(k):
        return consts[k]

    def const_factor(k):
        second = const(k + 1)
        return const(k), jnp.where(first, -second, second)

    bbar, read, carry = const_factor(BBAR), const_factor(READ), const_factor(CARRY)
    z_one, ratio = (const(Z), const(Z + 1)), (const(RATIO), const(RATIO + 1))
    c, b = (const(C), const(C + 1)), (const(B), const(B + 1))
    decay, freq, step = const(A_PART), const(A_PART + 1), const(STEP)
    modulus = decay * decay + freq * freq
    over_a = (-decay / modulus, -freq / modulus)
    to_c = scale(add(cmul(z_one, states_read), cmul(bbar, lag0)), 2.0)
    to_bbar = add(writes, scale(cmul(c, lag0), 2.0))
    to_log = add(
        add(cmul(read, slopes_read), cmul(bbar, slopes_write)),
        add(scale(cmul(carry, carried), float(block)), scale(cmul(cmul(c, bbar), lag1), 2.0)),
    )
    to_b = cmul(to_bbar, ratio)
    over = cmul(cmul(to_bbar, b), over_a)
    to_log = add(to_log, cmul(over, z_one))
    to_a = cmul(over, ratio)
    grad_decay = to_a[0] - step * to_log[0]
    grad_freq = to_a[1] - step * to_log[1]
    grad_step = jnp.where(first, -to_log[0] * decay, -to_log[1] * freq)
    out[0] = jnp.where(first, grad_decay, grad_freq)
    out[1] = jnp.where(first, to_b[0], -to_b[1])
    out[2] = jnp.where(first, to_c[0], -to_c[1])
    out[3] = jnp.broadcast_to(jnp.sum(grad_step, axis=1, keepdims=True), (channels, lanes))


def s4_sums(x, g, p, q, s, u, v, h, z, consts, block, deps, skip, steps):
    width, count, lanes = x.shape
    by_channel = pl.BlockSpec((CHANNELS, count, lanes), lambda i: (i + skip, 0, 0))
    return pl.pallas_call(
        lambda *refs: sums_kernel(block, *refs),
        grid=(steps,),
        in_specs=[by_channel] * 8
        + [
            pl.BlockSpec((CHANNELS, 2 * lanes, lanes), lambda i: (i + skip, 0, 0)),
            pl.BlockSpec((ROWS, CHANNELS, lanes), lambda i: (0, i + skip, 0)),
        ]
        + [pl.BlockSpec(memory_space=pl.ANY)] * len(deps),
        out_specs=pl.BlockSpec((4, CHANNELS, lanes), lambda i: (0, i, 0)),
        out_shape=jax.ShapeDtypeStruct((4, steps * CHANNELS, lanes), FULL),
        compiler_params=pltpu.CompilerParams(vmem_limit_bytes=VMEM),
        cost_estimate=cost(18 * steps * CHANNELS / width),
        name="s4_sums",
    )(x, g, p, q, s, u, v, h, z, consts, *deps)


def split(rows):
    half = rows.shape[-1] // 2
    return rows[..., :half], rows[..., half:]


def t_dot(a, b):
    return lax.dot_general(a, b, (((0,), (0,)), ((), ())), preferred_element_type=FULL)


def layer_forward(values, gain, bias, total_width, sums=None):
    if sums is None:
        sums = sum_chan(jnp.stack([jnp.sum(values, axis=-1), jnp.sum(values * values, axis=-1)]))
    center = sums[0] / total_width
    spread_var = sums[1] / total_width - center * center
    inverse = lax.rsqrt(spread_var + EPSILON)[..., None]
    normed = (values - center[..., None]) * inverse
    return normed * gain + bias, normed, inverse


def layer_backward(grad_out, normed, inverse, gain, total_width, work):
    scaled = grad_out * gain
    sums = jnp.stack([jnp.sum(scaled, axis=-1), jnp.sum(scaled * normed, axis=-1)])
    sums = after(sum_chan(sums), *work(sums))
    grad_in = inverse * (
        scaled - sums[0][..., None] / total_width - normed * sums[1][..., None] / total_width
    )
    return grad_in, jnp.sum(grad_out * normed, axis=0), jnp.sum(grad_out, axis=0)


def body(
    block_input,
    lengths,
    norm1_gain,
    norm1_bias,
    a_decay,
    a_freq,
    b_state,
    c_state,
    step_size,
    skip_gain,
    w_value,
    b_value,
    w_gate,
    b_gate,
    norm2_gain,
    norm2_bias,
    w_up,
    b_up,
    w_down,
    b_down,
    out_grad,
):
    batch, block, width = block_input.shape
    chans = lax.axis_size("chan")
    seqs = lax.axis_size("seq")
    assert seqs % batch == 0
    runs = seqs // batch
    total_width = width * chans
    assert chans == 4 and batch == 8 and block == 2 * a_decay.shape[0]
    seq_me = lax.axis_index("seq")
    chan_me = lax.axis_index("chan")
    groups = None if runs == 1 else [[r * batch + j for j in range(batch)] for r in range(runs)]
    peers = None if runs == 1 else [[r * batch + j for r in range(runs)] for j in range(batch)]

    def exchange(x):
        return lax.all_to_all(x, "seq", 0, 0, axis_index_groups=groups, tiled=True)

    def rows_of(w):
        return [
            lax.dynamic_slice_in_dim(w, (chan_me ^ d) * width, width, 0) for d in range(chans)
        ]

    moved = exchange(jnp.concatenate([block_input, out_grad], axis=-1)).reshape(batch * block, 2 * width)

    consts, base = s4_consts(a_decay, a_freq, b_state, c_state, step_size, block)
    z, m = s4_tables(base, consts, 0, 1)
    moved = after(moved, z)
    inputs = moved[:, :width].astype(FULL)
    grad_low = moved[:, width:]
    moments = sum_chan(jnp.stack([jnp.sum(inputs, axis=-1), jnp.sum(inputs * inputs, axis=-1)]))
    states = a_decay.shape[0]

    def const_factor(k):
        return consts[k, :, :states], consts[k + 1, :, states:]

    begin = (seq_me // batch) * batch * block
    places = begin + jnp.arange(batch * block, dtype=jnp.int32)
    mask = (places < lengths[seq_me % batch]).astype(FULL)[:, None]
    norm_one, normed_one, inverse_one = layer_forward(inputs, norm1_gain, norm1_bias, total_width, moments)
    signal = (mask * norm_one).astype(LOW)
    skip = skip_gain[None, :]
    init = jnp.zeros((width, 2 * states), FULL)
    if runs > 1:
        _, _, _, p, _, s = s4_forward(signal, skip, consts, z, m, init)
        carry = const_factor(CARRY)
        end = add(cmul(carry, split(s[:, -1])), cmul(const_factor(BBAR), split(p[:, -1])))
        ends = lax.all_gather(pair(*end), "seq", axis_index_groups=peers)
        hop = carry
        for _ in range(batch.bit_length() - 1):
            hop = cmul(hop, hop)
        for r in range(runs - 1):
            moved = add(cmul(hop, split(init)), split(ends[r]))
            init = jnp.where(r < seq_me // batch, pair(*moved), init)
    activ, slope, xs, ps, qs, ss = s4_forward(signal, skip, consts, z, m, init)

    wv, wg = rows_of(w_value), rows_of(w_gate)
    w_gated = [jnp.concatenate([a, b], axis=1) for a, b in zip(wv, wg)]
    w_ups = rows_of(w_up)
    w_downs = [
        lax.dynamic_slice_in_dim(w_down, (chan_me ^ d) * width, width, 1) for d in range(chans)
    ]
    grads = gather_pieces(grad_low)
    activs = gather_pieces(after(activ, grads[2]))
    both = sum(dot(a, w) for a, w in zip(activs, w_gated))
    value = both[:, :width] + b_value
    gate = both[:, width:] + b_gate
    opened = jax.nn.sigmoid(gate)
    resid = inputs + value * opened
    norm_two, normed_two, inverse_two = layer_forward(resid, norm2_gain, norm2_bias, total_width)
    norms = gather_pieces(norm_two.astype(LOW))
    hidden = sum(dot(a, w) for a, w in zip(norms, w_ups)) + b_up
    spread, gelu_pull = jax.vjp(jax.nn.gelu, hidden)
    spread = spread.astype(LOW)

    grad_out = grad_low.astype(FULL)
    grad_spread = sum(dot_t(a, w) for a, w in zip(grads, w_downs))
    grad_hidden = gelu_pull(grad_spread)[0].astype(LOW)
    grad_w_down = t_dot(after(spread, grad_hidden), jnp.concatenate(grads, axis=1)).astype(LOW)
    downs_dealt = deal(grad_w_down)
    marks = []
    hidden_late = after(grad_hidden, grad_w_down)
    grad_norm_two = reduce_pieces([dot_t(hidden_late, w) for w in w_ups], marks)
    grad_w_up = t_dot(jnp.concatenate(norms, axis=1), after(grad_hidden, *marks[:2])).astype(LOW)
    grad_norm_two = after(grad_norm_two, grad_w_up)
    chains = []

    def start_ups(dep):
        chains.append(Chain([downs_dealt, deal(after(grad_w_up, dep))], True))
        return []

    grad_resid, grad_norm2_gain, grad_norm2_bias = layer_backward(
        grad_norm_two, normed_two, inverse_two, norm2_gain, total_width, start_ups
    )
    wide_chain = chains[0]
    grad_resid = grad_out + grad_resid
    grad_value = (grad_resid * opened).astype(LOW)
    grad_gate = (grad_resid * value * opened * (1.0 - opened)).astype(LOW)
    grad_both = jnp.concatenate([grad_value, grad_gate], axis=1)
    marks = []
    grad_activ = reduce_pieces([dot_t(grad_both, w) for w in w_gated], marks)
    grad_w_gated = t_dot(jnp.concatenate(activs, axis=1), after(grad_both, *marks[:2])).astype(LOW)
    gated_chain = Chain([deal(after(grad_w_gated, grad_activ))], False)
    grad_activ = after(grad_activ, grad_w_gated)
    grad_mixed = (grad_activ * slope).astype(LOW)
    made = advance([wide_chain], grad_mixed)
    init = jnp.zeros((width, 2 * states), FULL)
    if runs > 1:
        _, _, u, _, h = s4_backward(grad_mixed, consts, z, m, init)
        end = add(cmul(carry, split(h[:, 0])), cmul(const_factor(READ), split(u[:, 0])))
        ends = lax.all_gather(pair(*end), "seq", axis_index_groups=peers)
        for r in reversed(range(1, runs)):
            moved = add(cmul(hop, split(init)), split(ends[r]))
            init = jnp.where(r > seq_me // batch, pair(*moved), init)
    grad_signal, gs, us, vs, hs = s4_backward(grad_mixed, consts, z, m, init, made)
    grad_signal = after(grad_signal, *advance([wide_chain, gated_chain], grad_signal))
    grad_signal = grad_signal + skip * grad_mixed.astype(FULL)
    s4_parts = (xs, gs, ps, qs, ss, us, vs, hs, z, consts, block)
    grad_input, grad_norm1_gain, grad_norm1_bias = layer_backward(
        grad_signal * mask, normed_one, inverse_one, norm1_gain, total_width, lambda dep: []
    )
    grad_input = (grad_resid + grad_input).astype(LOW)
    wide_own = gather(wide_chain.parts[0])
    sums = s4_sums(*s4_parts, [grad_input], 0, width // CHANNELS)
    narrow = jnp.concatenate(
        [
            grad_norm1_gain,
            grad_norm1_bias,
            jnp.sum(grad_mixed.astype(FULL) * signal.astype(FULL), axis=0),
            jnp.sum(grad_value.astype(FULL), axis=0),
            jnp.sum(grad_gate.astype(FULL), axis=0),
            grad_norm2_gain,
            grad_norm2_bias,
            jnp.sum(grad_out, axis=0),
            sums[3, :, 0],
            jnp.sum(grad_hidden.astype(FULL), axis=0),
        ]
    )
    packed = pack_small(sums, narrow)
    dealt = exchange_all(packed)
    made = join_sum(wide_chain.parts[1], *gated_chain.parts, [packed, *wide_own[1:]])
    last = gather_relayed(made)
    spread_late = after(spread, made)
    output = reduce_pieces([dot(spread_late, w) for w in w_downs])
    output = (resid + output + b_down).astype(LOW)
    parts, wide, narrow = sum_small(dealt, sums, narrow.shape[0], last[1:3])
    moved = beside(grad_input, output, [parts, *last[1:]])
    moved = exchange(moved.reshape(batch, block, 2 * width))
    grad_input, output = moved[:, :, :width].astype(FULL), moved[:, :, width:]
    vectors = [narrow[k * width : (k + 1) * width] for k in range(9)]
    vectors.insert(2, vectors.pop(8))

    zero = 0 * chan_me
    (down,) = finish([wide_own, last], 0, 2, total_width, 0, zero, chan_me >> 1, chan_me & 1)
    (up,) = finish([wide_own, last], 1, 2, grad_w_up.shape[1], 0, chan_me, zero, zero)
    grad_w_value, grad_w_gate = finish([last], 0, 1, 2 * width, total_width, chan_me, zero, zero, 2)
    return (
        output,
        grad_input,
        vectors[0],
        vectors[1],
        *wide,
        vectors[2],
        vectors[3],
        grad_w_value,
        vectors[4],
        grad_w_gate,
        vectors[5],
        vectors[6],
        vectors[7],
        up,
        narrow[9 * width :],
        down,
        vectors[8],
    )


def solution(mesh):
    in_specs = (
        P(None, "seq", "chan"),
        P(),
        P("chan"),
        P("chan"),
        P(None, "chan"),
        P(None, "chan"),
        P(None, None, "chan"),
        P(None, None, "chan"),
        P("chan"),
        P("chan"),
        P(None, "chan"),
        P("chan"),
        P(None, "chan"),
        P("chan"),
        P("chan"),
        P("chan"),
        P(None, "chan"),
        P("chan"),
        P("chan", None),
        P("chan"),
        P(None, "seq", "chan"),
    )
    out_specs = (
        P(None, "seq", "chan"),
        P(None, "seq", "chan"),
        P("chan"),
        P("chan"),
        P(None, "chan"),
        P(None, "chan"),
        P(None, None, "chan"),
        P(None, None, "chan"),
        P("chan"),
        P("chan"),
        P(None, "chan"),
        P("chan"),
        P(None, "chan"),
        P("chan"),
        P("chan"),
        P("chan"),
        P(None, "chan"),
        P("chan"),
        P("chan", None),
        P("chan"),
    )
    return jax.shard_map(body, mesh=mesh, in_specs=in_specs, out_specs=out_specs, check_vma=False)
```

```python
import jax
import jax.numpy as jnp
from jax import lax
from jax.experimental import pallas as pl
from jax.experimental.pallas import tpu as pltpu
from jax.sharding import PartitionSpec as P

EPSILON = 1e-05
LOW = jnp.bfloat16
FULL = jnp.float32
CHANNELS = 32
WIDE = 64
UNROLL = 32
SCALE = 1.0e5
VMEM = 56 * 1024 * 1024


def swap(x, axis, distance):
    return lax.ppermute(x, axis, [(i, i ^ distance) for i in range(lax.axis_size(axis))])


def axis_bits(axis):
    size = lax.axis_size(axis)
    bits = size.bit_length() - 1
    assert size == 1 << bits
    return bits


def gather_pieces(x):
    pieces = {0: x}
    for bit in reversed(range(axis_bits("chan"))):
        for d in list(pieces):
            pieces[d ^ (1 << bit)] = swap(pieces[d], "chan", 1 << bit)
    return [pieces[d] for d in range(len(pieces))]


def reduce_pieces(parts, marks=None):
    sums = dict(enumerate(parts))
    for bit in range(axis_bits("chan")):
        if marks is not None and bit == axis_bits("chan") - 1:
            marks += [sums[1 << bit], sums[0]]
        for d in sorted(sums, reverse=True):
            if d >> bit & 1:
                received = swap(sums.pop(d).astype(LOW), "chan", 1 << bit)
                if marks is not None and d == 1 << (axis_bits("chan") - 1):
                    marks.append(received)
                sums[d ^ (1 << bit)] = sums[d ^ (1 << bit)] + received.astype(FULL)
    return sums[0]


def sum_chan(x):
    return x + sum(swap(x, "chan", d) for d in range(1, lax.axis_size("chan")))


def after(x, *others):
    return lax.optimization_barrier((x, others))[0]


def exchange_all(x):
    return lax.all_to_all(x, "seq", 0, 0, tiled=True)


def small_shares(sums, size):
    seqs = lax.axis_size("seq")
    groups, width, lanes = sums.shape
    short = -(-size // (seqs * lanes))
    assert short <= 8
    share = (groups - 1) * width // seqs
    return share, short, -(-(share + 16) // 16) * 16


def pack_small(sums, narrow):
    seqs = lax.axis_size("seq")
    groups, width, lanes = sums.shape
    size = narrow.shape[0]
    share, short, rows = small_shares(sums, size)
    narrow_rows = jnp.pad(narrow, (0, seqs * short * lanes - size)).reshape(seqs, short, lanes)
    narrow_rows = jnp.pad(narrow_rows, ((0, 0), (0, 8 - short), (0, 0)))

    def pack(sums, narrow, packed):
        flat = sums[: groups - 1].reshape((groups - 1) * width, lanes)
        for k in range(seqs):
            part = narrow[k]
            high = part.astype(LOW).astype(FULL)
            pieces = [flat[k * share : (k + 1) * share], high, part - high]
            if rows > share + 16:
                pieces.append(jnp.zeros((rows - share - 16, lanes), FULL))
            packed[k] = jnp.concatenate(pieces, axis=0).astype(LOW)

    shape = jax.ShapeDtypeStruct((seqs, rows, lanes), LOW)
    return call_here(pack, [sums, narrow_rows], [], [shape], "pack_small")[0]


def sum_small(dealt, sums, size, deps):
    seqs, rows, lanes = dealt.shape
    groups, width, _ = sums.shape
    share, short, _ = small_shares(sums, size)

    def add(dealt, out):
        total = sum(dealt[k].astype(FULL) for k in range(seqs))
        narrow = total[share : share + 8] + total[share + 8 : share + 16]
        high = narrow.astype(LOW).astype(FULL)
        pieces = [total[:share], high, narrow - high] + ([total[share + 16 :]] if rows > share + 16 else [])
        total = jnp.concatenate(pieces, axis=0).astype(LOW)
        for k in range(seqs):
            out[k] = total

    parts = exchange_all(call_here(add, [dealt], deps, [jax.ShapeDtypeStruct(dealt.shape, LOW)], "sum_small")[0])
    states = lanes // 2

    def unpack(parts, decay, freq, b, c, narrow):
        flat = jnp.concatenate([parts[k, :share, :].astype(FULL) for k in range(seqs)], axis=0)
        a, b_both, c_both = (flat[g * width : (g + 1) * width].T for g in range(3))
        decay[...], freq[...] = a[:states], a[states:]
        b[0], b[1] = b_both[:states], b_both[states:]
        c[0], c[1] = c_both[:states], c_both[states:]
        for k in range(seqs):
            part = parts[k].astype(FULL)
            narrow[k] = part[share : share + 8] + part[share + 8 : share + 16]

    one, two = (states, width), (2, states, width)
    *wide, narrow = call_here(
        unpack,
        [parts],
        [],
        [jax.ShapeDtypeStruct(shape, FULL) for shape in (one, one, two, two, (seqs, 8, lanes))],
        "unpack_small",
    )
    return parts, wide, narrow[:, :short].reshape(-1)[:size]


def beside(left, right, deps):
    rows, columns = left.shape

    def kernel(left, right, out):
        out[:, :columns] = left[...]
        out[:, columns:] = right[...]

    shape = jax.ShapeDtypeStruct((rows, columns + right.shape[1]), left.dtype)
    return call_here(kernel, [left, right], deps, [shape], "beside")[0]


def call_here(kernel, ins, deps, outs, name):
    here, anywhere = pl.BlockSpec(memory_space=pltpu.VMEM), pl.BlockSpec(memory_space=pl.ANY)
    return pl.pallas_call(
        lambda *refs: kernel(*refs[: len(ins)], *refs[len(ins) + len(deps) :]),
        in_specs=[here] * len(ins) + [anywhere] * len(deps),
        out_specs=[here] * len(outs),
        out_shape=outs,
        compiler_params=pltpu.CompilerParams(vmem_limit_bytes=VMEM),
        cost_estimate=cost(2),
        name=name,
    )(*ins, *deps)


QUAD = 4


def deal(x):
    seqs = lax.axis_size("seq")
    groups = [list(range(i, i + QUAD)) for i in range(0, seqs, QUAD)]
    return lax.all_to_all(x.reshape(QUAD, -1, x.shape[1]), "seq", 0, 0, axis_index_groups=groups, tiled=True)


class Chain:
    def __init__(self, parts, halves):
        self.masks = [1 << bit for bit in range(axis_bits("seq")) if 1 << bit >= QUAD]
        self.parts = parts
        self.halves = halves
        self.tasks = ["deal" if halves else "whole", "sum"]

    def accept(self, task, outs):
        if task == "deal":
            self.parts = [outs[0], swap(outs[1], "seq", self.masks[0])]
            return
        total = outs[0]
        for mask in self.masks[1:]:
            total = (total.astype(FULL) + swap(total, "seq", mask).astype(FULL)).astype(LOW)
        self.parts = [total]
        if task == "whole" or self.halves:
            self.parts.append(swap(total, "seq", self.masks[0]))


def gather(part):
    return [part] + [swap(part, "seq", mask) for mask in range(1, QUAD)]


def gather_relayed(part):
    first, second = swap(part, "seq", 1), swap(part, "seq", 2)
    half = part.shape[0] // 2
    third = jnp.concatenate([swap(second[:half], "seq", 1), swap(first[half:], "seq", 2)])
    return [part, first, second, third]


def join_sum(left, own, received, deps):
    rows, columns = left.shape

    def kernel(left, own, received, *refs):
        out = refs[-1]
        out[:, :columns] = left[...]
        out[:, columns:] = (own[...].astype(FULL) + received[...].astype(FULL)).astype(LOW)

    here, anywhere = pl.BlockSpec(memory_space=pltpu.VMEM), pl.BlockSpec(memory_space=pl.ANY)
    return pl.pallas_call(
        kernel,
        in_specs=[here] * 3 + [anywhere] * len(deps),
        out_specs=here,
        out_shape=jax.ShapeDtypeStruct((rows, columns + own.shape[1]), LOW),
        compiler_params=pltpu.CompilerParams(vmem_limit_bytes=VMEM),
        cost_estimate=cost(2),
        name="join_sum",
    )(left, own, received, *deps)


def advance(chains, *deps):
    tasks = [chain.tasks.pop(0) for chain in chains]
    parts = [chain.parts for chain in chains]
    shapes = []
    for task, part in zip(tasks, parts):
        rows, columns = part[0].shape[-2:]
        made = {"deal": [rows // 2 * len(part)] * 2, "whole": [rows * len(part)], "sum": [rows]}[task]
        shapes.append([jax.ShapeDtypeStruct((size, columns), LOW) for size in made])
    counts = [len(part) for part in parts]
    me = lax.axis_index("seq")
    high = (me // QUAD % 2).astype(jnp.int32)[None]

    def kernel(high, *refs):
        ins = list(refs[: sum(counts)])
        outs = list(refs[len(refs) - sum(len(shape) for shape in shapes) :])
        for task, count in zip(tasks, counts):
            refs = [ins.pop(0) for _ in range(count)]
            if task == "deal":
                half = refs[0].shape[1] // 2
                for block in (high[0], 1 - high[0]):
                    place = pl.ds(pl.multiple_of(block * half, half), half)
                    out = outs.pop(0)
                    for i, ref in enumerate(refs):
                        out[i * half : (i + 1) * half, :] = sum(
                            ref[k, place, :].astype(FULL) for k in range(QUAD)
                        ).astype(LOW)
            elif task == "whole":
                out = outs.pop(0)
                rows = refs[0].shape[1]
                for i, ref in enumerate(refs):
                    out[i * rows : (i + 1) * rows, :] = sum(ref[k].astype(FULL) for k in range(QUAD)).astype(LOW)
            else:
                outs.pop(0)[...] = (refs[0][...].astype(FULL) + refs[1][...].astype(FULL)).astype(LOW)

    here, anywhere = pl.BlockSpec(memory_space=pltpu.VMEM), pl.BlockSpec(memory_space=pl.ANY)
    results = list(
        pl.pallas_call(
            kernel,
            in_specs=[pl.BlockSpec(memory_space=pltpu.SMEM)] + [here] * sum(counts) + [anywhere] * len(deps),
            out_specs=[here] * sum(len(shape) for shape in shapes),
            out_shape=[one for shape in shapes for one in shape],
            compiler_params=pltpu.CompilerParams(vmem_limit_bytes=VMEM),
            cost_estimate=cost(2),
            name="advance",
        )(high, *[array for part in parts for array in part], *deps)
    )
    rest = list(results)
    for task, chain, shape in zip(tasks, chains, shapes):
        chain.accept(task, [rest.pop(0) for _ in shape])
    return results


def finish(groups, slot, slots, columns, first, row_turn, half_turn, column_turn, outputs=1):
    rows = groups[0][0].shape[0] // slots
    width = columns // 4
    skip = first // (2 * width)
    me = lax.axis_index("seq")
    high = me // QUAD % 2
    scalars = jnp.stack([(me & (QUAD - 1)) ^ row_turn, half_turn, column_turn, high]).astype(jnp.int32)
    count = len(groups)

    def kernel(scalars, *refs):
        ins, outs = refs[: count * QUAD], refs[-outputs:]

        def put(out):
            for k in range(count):
                for q in range(QUAD):
                    block = (scalars[0] ^ q) * count
                    if count == 2:
                        block = block + (scalars[3] ^ k)
                    target = pl.ds(pl.multiple_of(block * rows, rows), rows)
                    ref = ins[k * QUAD + q]
                    for e in range(2):
                        place = pl.ds(pl.multiple_of((e ^ scalars[2]) * width, width), width)
                        out[target, place] = ref[:, e * width : (e + 1) * width].astype(FULL)

        if outputs == 1:
            put(outs[0])
        else:
            for k in range(2):
                pl.when(pl.program_id(0) == k)(lambda k=k: put(outs[k]))

    return pl.pallas_call(
        kernel,
        grid_spec=pltpu.PrefetchScalarGridSpec(
            num_scalar_prefetch=1,
            grid=(2,),
            in_specs=[pl.BlockSpec((rows, 2 * width), lambda half, n: (slot, half + skip))] * (count * QUAD),
            out_specs=[
                pl.BlockSpec(
                    (count * QUAD * rows, 2 * width),
                    (lambda half, n: (0, half ^ n[1])) if outputs == 1 else (lambda half, n: (0, 0)),
                )
            ]
            * outputs,
        ),
        out_shape=[jax.ShapeDtypeStruct((count * QUAD * rows, columns // outputs), FULL)] * outputs,
        compiler_params=pltpu.CompilerParams(vmem_limit_bytes=VMEM),
        cost_estimate=cost(3),
        name="finish",
    )(scalars, *[part for group in groups for part in group])


def cost(us):
    return pl.CostEstimate(flops=0, bytes_accessed=int(us * SCALE), transcendentals=0)


def pair(re, im):
    return jnp.concatenate([re, im], axis=-1)


def factor(re, im):
    return pair(re, re), pair(-im, im)


def times(x, first, second):
    lanes = x.shape[-1]
    return x * first + pltpu.roll(x, lanes // 2, x.ndim - 1) * second


def cmul(a, b):
    return a[0] * b[0] - a[1] * b[1], a[0] * b[1] + a[1] * b[0]


def add(a, b):
    return a[0] + b[0], a[1] + b[1]


def scale(a, k):
    return a[0] * k, a[1] * k


BBAR, READ, CARRY, STRIDE, KERNEL, Z, RATIO, C, B, A_PART, STEP = 0, 2, 4, 10, 18, 19, 21, 23, 25, 27, 29
ROWS = 30


def less_one(x):
    total = 1.0 + x / 8.0
    for k in (7.0, 6.0, 5.0, 4.0, 3.0, 2.0):
        total = 1.0 + x / k * total
    return jnp.where(x > -0.25, x * total, jnp.exp(x) - 1.0)


def consts_kernel(block, decay_ref, freq_ref, b_ref, c_ref, step_ref, consts, base):
    states, width = decay_ref.shape
    lanes = 2 * states

    def wide(x):
        return jnp.concatenate([x, x], axis=0).T

    decay, freq = wide(decay_ref[...]), wide(freq_ref[...])
    b = (wide(b_ref[0]), wide(b_ref[1]))
    c = (wide(c_ref[0]), wide(c_ref[1]))
    step = jnp.broadcast_to(step_ref[...], (lanes, width)).T
    first = lax.broadcasted_iota(jnp.int32, (width, lanes), 1) < states
    rate = step * decay
    turn = step * freq
    size = jnp.exp(-rate)
    z = (size * jnp.cos(turn), size * jnp.sin(turn))
    half_turn = jnp.sin(0.5 * turn)
    less = (less_one(-rate) * jnp.cos(turn) - 2.0 * half_turn * half_turn, z[1])
    modulus = decay * decay + freq * freq
    ratio = (
        (freq * less[1] - decay * less[0]) / modulus,
        -(decay * less[1] + freq * less[0]) / modulus,
    )
    bbar = cmul(ratio, b)
    twice_c = scale(c, 2.0)

    def put_factor(k, x):
        consts[k] = x[0]
        consts[k + 1] = jnp.where(first, -x[1], x[1])

    def put_plain(k, x):
        consts[k] = x[0]
        consts[k + 1] = x[1]

    put_factor(BBAR, bbar)
    put_factor(READ, cmul(twice_c, z))
    kernel = cmul(twice_c, bbar)
    consts[KERNEL] = jnp.where(first, kernel[0], -kernel[1])
    put_plain(Z, z)
    put_plain(RATIO, ratio)
    put_plain(C, c)
    put_plain(B, b)
    consts[A_PART] = decay
    consts[A_PART + 1] = freq
    consts[STEP] = step
    power = (jnp.ones_like(size), jnp.zeros_like(size))
    for k in range(8):
        base[k] = jnp.where(first, power[0], power[1])
        power = cmul(power, z)
    k = 8
    while k < 4 * block:
        if k <= 64:
            put_factor(STRIDE + 2 * (k.bit_length() - 4), power)
        if k >= block:
            put_factor(CARRY + 2 * ((k // block).bit_length() - 1), power)
        power = cmul(power, power)
        k *= 2
    put_factor(CARRY + 4, power)


def s4_consts(a_decay, a_freq, b_state, c_state, step_size, block):
    states, width = a_decay.shape
    return pl.pallas_call(
        lambda *refs: consts_kernel(block, *refs),
        out_shape=[
            jax.ShapeDtypeStruct((ROWS, width, 2 * states), FULL),
            jax.ShapeDtypeStruct((8, width, 2 * states), FULL),
        ],
        compiler_params=pltpu.CompilerParams(vmem_limit_bytes=VMEM),
        cost_estimate=cost(6),
        name="s4_consts",
    )(a_decay, a_freq, b_state, c_state, step_size[None, :])


def half_turned(x):
    return pltpu.roll(x, x.shape[-1] // 2, x.ndim - 1)


def high_low(x):
    high = x.astype(LOW)
    return high, (x - high.astype(FULL)).astype(LOW)


def dot(a, b):
    return lax.dot_general(a, b, (((1,), (0,)), ((), ())), preferred_element_type=FULL)


def dot_t(a, b):
    return lax.dot_general(a, b, (((1,), (1,)), ((), ())), preferred_element_type=FULL)


def tables_kernel(base, consts, *refs):
    z_out, h_out = refs[-2:]
    channels, _, lanes = z_out.shape
    row8 = lax.broadcasted_iota(jnp.int32, (8, lanes), 0)
    row = lax.broadcasted_iota(jnp.int32, (lanes, lanes), 0)
    lane = lax.broadcasted_iota(jnp.int32, (lanes, lanes), 1)
    live = row + lane >= lanes - 1

    def one(c):
        first = jnp.concatenate([base[k, pl.ds(c, 1), :] for k in range(8)], axis=0)
        tiles = [(first, half_turned(first))]
        for level in range(4):
            k = STRIDE + 2 * level
            a, b = consts[k, pl.ds(c, 1), :], consts[k + 1, pl.ds(c, 1), :]
            tiles += [(t * a + u * b, u * a - t * b) for t, u in tiles]
        z = jnp.concatenate([t for t, _ in tiles], axis=0)
        high, low = high_low(z)
        z_out[c, :lanes, :] = high
        z_out[c, lanes:, :] = low
        f_high, f_low = high_low(jnp.broadcast_to(consts[KERNEL, pl.ds(c, 1), :], (8, lanes)))
        h = dot_t(jnp.concatenate([f_high, f_low], axis=0), high)
        h = h[:8] + h[8:] + dot_t(f_high, low)
        for bit in (1, 2, 4):
            h = jnp.where((7 - row8) & bit != 0, pltpu.roll(h, bit, 1), h)
        hankel = [pltpu.roll(h, lanes - 8 - k, 1) if k < lanes - 8 else h for k in range(0, lanes, 8)]
        hankel = jnp.concatenate(hankel, axis=0)
        h_out[c] = jnp.where(live, hankel, 0.0).astype(LOW)

    @pl.loop(0, channels, step=UNROLL)
    def _(c):
        for k in range(UNROLL):
            one(c + k)


def s4_tables(base, consts, part, parts, tables=(), deps=()):
    _, width, lanes = base.shape
    steps = width // CHANNELS // parts
    skip = part * steps
    anywhere = pl.BlockSpec(memory_space=pl.ANY)
    return pl.pallas_call(
        tables_kernel,
        grid=(steps,),
        in_specs=[
            pl.BlockSpec((8, CHANNELS, lanes), lambda i: (0, i + skip, 0)),
            pl.BlockSpec((ROWS, CHANNELS, lanes), lambda i: (0, i + skip, 0)),
        ]
        + [anywhere] * (len(tables) + len(deps)),
        out_specs=[
            pl.BlockSpec((CHANNELS, 2 * lanes, lanes), lambda i: (i + skip, 0, 0)),
            pl.BlockSpec((CHANNELS, lanes, lanes), lambda i: (i + skip, 0, 0)),
        ],
        out_shape=[
            jax.ShapeDtypeStruct((width, 2 * lanes, lanes), LOW),
            jax.ShapeDtypeStruct((width, lanes, lanes), LOW),
        ],
        input_output_aliases={2: 0, 3: 1} if tables else {},
        compiler_params=pltpu.CompilerParams(vmem_limit_bytes=VMEM),
        cost_estimate=cost(24 / parts),
        name="s4_tables",
    )(base, consts, *tables, *deps)


def flip_matrix(size):
    row = lax.broadcasted_iota(jnp.int32, (size, size), 0)
    lane = lax.broadcasted_iota(jnp.int32, (size, size), 1)
    return (row + lane == size - 1).astype(FULL).astype(LOW)


def rows_of_channels(consts, k):
    return jnp.stack([consts[k, c : c + 1, :] for c in range(consts.shape[1])])


def weighted_ends(x, place, z):
    high, low = high_low(x * place)
    x = x.astype(LOW)
    none = jnp.zeros_like(x)
    left = jnp.concatenate([x, high, low, none], axis=0)
    right = jnp.concatenate([x, high, none, none], axis=0)
    ends = dot(jnp.concatenate([left, right], axis=1), z)
    count = x.shape[0]
    return ends[:count], ends[count : 2 * count] + ends[2 * count : 3 * count]


def times_both(x, consts, k):
    first, second = rows_of_channels(consts, k), rows_of_channels(consts, k + 1)
    return x[0] * first + x[1] * second, x[1] * first - x[0] * second


def scan_blocks(x, consts, row, reverse):
    count = x[0].shape[1]
    for level, d in enumerate((1, 2, 4)):
        live = row < count - d if reverse else row >= d
        moved = [jnp.where(live, pltpu.roll(e, count - d if reverse else d, 1), 0.0) for e in x]
        x = add(x, times_both(moved, consts, CARRY + 2 * level))
    return x


def forward_kernel(
    signal, skip, consts, z, m, init, activ, slope, x_out, p_out, q_out, s_out, x_scr, y_scr
):
    step = pl.program_id(0)
    channels, _, lanes = z.shape
    count = signal.shape[0] // lanes
    width = signal.shape[1]

    @pl.when(step == 0)
    def _():
        flip = flip_matrix(lanes)
        for j in range(count):
            x_scr[pl.ds(j, width, stride=count), :] = dot(flip, signal[j * lanes : (j + 1) * lanes, :]).T

    rows = pl.ds(pl.multiple_of(step * channels * count, channels * count), channels * count)
    x = x_scr[rows, :].reshape(channels, count, lanes)
    place = lax.broadcasted_iota(jnp.int32, (count, lanes), 1).astype(FULL)
    row = lax.broadcasted_iota(jnp.int32, (channels, count, lanes), 1)
    plus = lax.broadcasted_iota(jnp.int32, (channels, count, lanes), 2) < lanes // 2
    ends = [weighted_ends(x[c], place, z[c]) for c in range(channels)]
    p = jnp.stack([e[0] for e in ends])
    q = jnp.stack([e[1] for e in ends])
    start = init[...][:, None, :]
    state = times_both((p, half_turned(p)), consts, BBAR)
    state = [
        jnp.where(row == 0, e, pltpu.roll(s, 1, 1)) for e, s in zip((start, half_turned(start)), state)
    ]
    state = scan_blocks(state, consts, row, False)
    read, _ = times_both(state, consts, READ)
    read = jnp.where(plus, read, -read).astype(LOW)
    y = [dot(x[c].astype(LOW), m[c]) + dot_t(read[c], z[c, :lanes, :]) for c in range(channels)]
    y_scr[rows, :] = jnp.concatenate(y, axis=0)
    x_out[...] = x
    p_out[...] = p
    q_out[...] = q
    s_out[...] = state[0]

    @pl.when(step == pl.num_programs(0) - 1)
    def _():
        for j in range(count):
            part = slice(j * lanes, (j + 1) * lanes)
            mixed = y_scr[pl.ds(j, width, stride=count), :].T + skip[...] * signal[part, :].astype(FULL)
            inner = 0.7978845608028654 * (mixed + 0.044715 * mixed * mixed * mixed)
            bent = jnp.tanh(inner)
            activ[part, :] = (0.5 * mixed * (1.0 + bent)).astype(LOW)
            slope[part, :] = 0.5 * (1.0 + bent) + 0.5 * mixed * (1.0 - bent * bent) * (
                0.7978845608028654 * (1.0 + 3 * 0.044715 * mixed * mixed)
            )


def s4_forward(signal, skip, consts, z, m, init):
    tokens, width = signal.shape
    lanes = z.shape[-1]
    count = tokens // lanes
    whole = pl.BlockSpec((tokens, width), lambda i: (0, 0))
    by_channel = pl.BlockSpec((WIDE, count, lanes), lambda i: (i, 0, 0))
    per_channel = jax.ShapeDtypeStruct((width, count, lanes), FULL)
    return pl.pallas_call(
        forward_kernel,
        grid=(width // WIDE,),
        in_specs=[
            whole,
            pl.BlockSpec((1, width), lambda i: (0, 0)),
            pl.BlockSpec((ROWS, WIDE, lanes), lambda i: (0, i, 0)),
            pl.BlockSpec((WIDE, 2 * lanes, lanes), lambda i: (i, 0, 0)),
            pl.BlockSpec((WIDE, lanes, lanes), lambda i: (i, 0, 0)),
            pl.BlockSpec((WIDE, lanes), lambda i: (i, 0)),
        ],
        out_specs=[whole, whole] + [by_channel] * 4,
        out_shape=[
            jax.ShapeDtypeStruct((tokens, width), LOW),
            jax.ShapeDtypeStruct((tokens, width), FULL),
        ]
        + [per_channel] * 4,
        scratch_shapes=[pltpu.VMEM((width * count, lanes), FULL)] * 2,
        compiler_params=pltpu.CompilerParams(vmem_limit_bytes=VMEM),
        cost_estimate=cost(18),
        name="s4_forward",
    )(signal, skip, consts, z, m, init)


def backward_kernel(grads, consts, z, m, init, *refs):
    out, g_out, u_out, v_out, h_out, g_scr, y_scr = refs[-7:]
    step = pl.program_id(0)
    channels, _, lanes = z.shape
    count = grads.shape[0] // lanes
    width = grads.shape[1]

    @pl.when(step == 0)
    def _():
        for j in range(count):
            g_scr[pl.ds(j, width, stride=count), :] = grads[j * lanes : (j + 1) * lanes, :].astype(FULL).T

    rows = pl.ds(pl.multiple_of(step * channels * count, channels * count), channels * count)
    g = g_scr[rows, :].reshape(channels, count, lanes)
    place = lax.broadcasted_iota(jnp.int32, (count, lanes), 1).astype(FULL)
    row = lax.broadcasted_iota(jnp.int32, (channels, count, lanes), 1)
    plus = lax.broadcasted_iota(jnp.int32, (channels, count, lanes), 2) < lanes // 2
    ends = [weighted_ends(g[c], place, z[c]) for c in range(channels)]
    u = jnp.stack([e[0] for e in ends])
    v = jnp.stack([e[1] for e in ends])
    start = init[...][:, None, :]
    later = times_both((u, half_turned(u)), consts, READ)
    later = [
        jnp.where(row == count - 1, e, pltpu.roll(s, count - 1, 1))
        for e, s in zip((start, half_turned(start)), later)
    ]
    later = scan_blocks(later, consts, row, True)
    write, _ = times_both(later, consts, BBAR)
    write = jnp.where(plus, write, -write).astype(LOW)
    y = [dot(g[c].astype(LOW), m[c]) + dot_t(write[c], z[c, :lanes, :]) for c in range(channels)]
    y_scr[rows, :] = jnp.concatenate(y, axis=0)
    g_out[...] = g
    u_out[...] = u
    v_out[...] = v
    h_out[...] = later[0]

    @pl.when(step == pl.num_programs(0) - 1)
    def _():
        flip = flip_matrix(lanes)
        for j in range(count):
            out[j * lanes : (j + 1) * lanes, :] = dot(
                flip, y_scr[pl.ds(j, width, stride=count), :].T.astype(LOW)
            )


def s4_backward(grads, consts, z, m, init, deps=()):
    tokens, width = grads.shape
    lanes = z.shape[-1]
    count = tokens // lanes
    whole = pl.BlockSpec((tokens, width), lambda i: (0, 0))
    by_channel = pl.BlockSpec((WIDE, count, lanes), lambda i: (i, 0, 0))
    per_channel = jax.ShapeDtypeStruct((width, count, lanes), FULL)
    return pl.pallas_call(
        backward_kernel,
        grid=(width // WIDE,),
        in_specs=[
            whole,
            pl.BlockSpec((ROWS, WIDE, lanes), lambda i: (0, i, 0)),
            pl.BlockSpec((WIDE, 2 * lanes, lanes), lambda i: (i, 0, 0)),
            pl.BlockSpec((WIDE, lanes, lanes), lambda i: (i, 0, 0)),
            pl.BlockSpec((WIDE, lanes), lambda i: (i, 0)),
        ]
        + [pl.BlockSpec(memory_space=pl.ANY)] * len(deps),
        out_specs=[whole] + [by_channel] * 4,
        out_shape=[jax.ShapeDtypeStruct((tokens, width), FULL)] + [per_channel] * 4,
        scratch_shapes=[pltpu.VMEM((width * count, lanes), FULL)] * 2,
        compiler_params=pltpu.CompilerParams(vmem_limit_bytes=VMEM),
        cost_estimate=cost(18),
        name="s4_backward",
    )(grads, consts, z, m, init, *deps)


def sums_kernel(block, x, g, p, q, s, u, v, h, z, consts, *refs):
    out = refs[-1]
    channels, count, lanes = x.shape
    states = lanes // 2
    row8 = lax.broadcasted_iota(jnp.int32, (8, lanes), 0)
    row = lax.broadcasted_iota(jnp.int32, (lanes, lanes), 0)
    lane = lax.broadcasted_iota(jnp.int32, (lanes, lanes), 1)
    place = lax.broadcasted_iota(jnp.int32, (8, lanes), 1).astype(FULL)
    live = row + lane >= lanes - 1
    first = lax.broadcasted_iota(jnp.int32, (channels, lanes), 1) < states
    w = []
    for c in range(channels):
        both = lax.dot_general(
            x[c].astype(LOW), g[c].astype(LOW), (((0,), (0,)), ((), ())), preferred_element_type=FULL
        )
        both = jnp.where(live, both, 0.0)
        tiles = [both[k : k + 8, :] for k in range(0, lanes, 8)]
        shift = 8
        while len(tiles) > 1:
            tiles = [a + pltpu.roll(b, shift, 1) for a, b in zip(tiles[::2], tiles[1::2])]
            shift *= 2
        total = pltpu.roll(tiles[0], 1, 1)
        for bit in (1, 2, 4):
            total = jnp.where(row8 & bit != 0, pltpu.roll(total, bit, 1), total)
        high, low = high_low(total)
        place_high, place_low = high_low(total * place)
        none = jnp.zeros_like(high)
        left = jnp.concatenate([high, low, place_high, place_low], axis=0)
        right = jnp.concatenate([high, none, place_high, none], axis=0)
        w.append(dot(jnp.concatenate([left, right], axis=1), z[c]))
    lag0 = jnp.sum(jnp.stack([e[:16] for e in w]), axis=1)
    lag1 = jnp.sum(jnp.stack([e[16:] for e in w]), axis=1)

    def both_halves(x):
        turned = half_turned(x)
        return jnp.where(first, x, turned), jnp.where(first, turned, x)

    def product(a, b):
        plain = jnp.sum(a * b, axis=1)
        crossed = jnp.sum(a * half_turned(b), axis=1)
        plain = jnp.where(first, plain, -plain)
        return plain + half_turned(plain), crossed + half_turned(crossed)

    states_read = product(u[...], s[...])
    slopes_read = product(u[...] + v[...], s[...])
    writes = product(h[...], p[...])
    slopes_write = product(h[...], q[...])
    carried = product(h[...], s[...])
    lag0, lag1 = both_halves(lag0), both_halves(lag1)

    def const(k):
        return consts[k]

    def const_factor(k):
        second = const(k + 1)
        return const(k), jnp.where(first, -second, second)

    bbar, read, carry = const_factor(BBAR), const_factor(READ), const_factor(CARRY)
    z_one, ratio = (const(Z), const(Z + 1)), (const(RATIO), const(RATIO + 1))
    c, b = (const(C), const(C + 1)), (const(B), const(B + 1))
    decay, freq, step = const(A_PART), const(A_PART + 1), const(STEP)
    modulus = decay * decay + freq * freq
    over_a = (-decay / modulus, -freq / modulus)
    to_c = scale(add(cmul(z_one, states_read), cmul(bbar, lag0)), 2.0)
    to_bbar = add(writes, scale(cmul(c, lag0), 2.0))
    to_log = add(
        add(cmul(read, slopes_read), cmul(bbar, slopes_write)),
        add(scale(cmul(carry, carried), float(block)), scale(cmul(cmul(c, bbar), lag1), 2.0)),
    )
    to_b = cmul(to_bbar, ratio)
    over = cmul(cmul(to_bbar, b), over_a)
    to_log = add(to_log, cmul(over, z_one))
    to_a = cmul(over, ratio)
    grad_decay = to_a[0] - step * to_log[0]
    grad_freq = to_a[1] - step * to_log[1]
    grad_step = jnp.where(first, -to_log[0] * decay, -to_log[1] * freq)
    out[0] = jnp.where(first, grad_decay, grad_freq)
    out[1] = jnp.where(first, to_b[0], -to_b[1])
    out[2] = jnp.where(first, to_c[0], -to_c[1])
    out[3] = jnp.broadcast_to(jnp.sum(grad_step, axis=1, keepdims=True), (channels, lanes))


def s4_sums(x, g, p, q, s, u, v, h, z, consts, block, deps, skip, steps):
    width, count, lanes = x.shape
    by_channel = pl.BlockSpec((CHANNELS, count, lanes), lambda i: (i + skip, 0, 0))
    return pl.pallas_call(
        lambda *refs: sums_kernel(block, *refs),
        grid=(steps,),
        in_specs=[by_channel] * 8
        + [
            pl.BlockSpec((CHANNELS, 2 * lanes, lanes), lambda i: (i + skip, 0, 0)),
            pl.BlockSpec((ROWS, CHANNELS, lanes), lambda i: (0, i + skip, 0)),
        ]
        + [pl.BlockSpec(memory_space=pl.ANY)] * len(deps),
        out_specs=pl.BlockSpec((4, CHANNELS, lanes), lambda i: (0, i, 0)),
        out_shape=jax.ShapeDtypeStruct((4, steps * CHANNELS, lanes), FULL),
        compiler_params=pltpu.CompilerParams(vmem_limit_bytes=VMEM),
        cost_estimate=cost(18 * steps * CHANNELS / width),
        name="s4_sums",
    )(x, g, p, q, s, u, v, h, z, consts, *deps)


def split(rows):
    half = rows.shape[-1] // 2
    return rows[..., :half], rows[..., half:]


def t_dot(a, b):
    return lax.dot_general(a, b, (((0,), (0,)), ((), ())), preferred_element_type=FULL)


def layer_forward(values, gain, bias, total_width, sums=None):
    if sums is None:
        sums = sum_chan(jnp.stack([jnp.sum(values, axis=-1), jnp.sum(values * values, axis=-1)]))
    center = sums[0] / total_width
    spread_var = sums[1] / total_width - center * center
    inverse = lax.rsqrt(spread_var + EPSILON)[..., None]
    normed = (values - center[..., None]) * inverse
    return normed * gain + bias, normed, inverse


def layer_backward(grad_out, normed, inverse, gain, total_width, work):
    scaled = grad_out * gain
    sums = jnp.stack([jnp.sum(scaled, axis=-1), jnp.sum(scaled * normed, axis=-1)])
    sums = after(sum_chan(sums), *work(sums))
    grad_in = inverse * (
        scaled - sums[0][..., None] / total_width - normed * sums[1][..., None] / total_width
    )
    return grad_in, jnp.sum(grad_out * normed, axis=0), jnp.sum(grad_out, axis=0)


def body(
    block_input,
    lengths,
    norm1_gain,
    norm1_bias,
    a_decay,
    a_freq,
    b_state,
    c_state,
    step_size,
    skip_gain,
    w_value,
    b_value,
    w_gate,
    b_gate,
    norm2_gain,
    norm2_bias,
    w_up,
    b_up,
    w_down,
    b_down,
    out_grad,
):
    batch, block, width = block_input.shape
    chans = lax.axis_size("chan")
    seqs = lax.axis_size("seq")
    assert seqs % batch == 0
    runs = seqs // batch
    total_width = width * chans
    assert chans == 4 and batch == 8 and block == 2 * a_decay.shape[0]
    seq_me = lax.axis_index("seq")
    chan_me = lax.axis_index("chan")
    groups = None if runs == 1 else [[r * batch + j for j in range(batch)] for r in range(runs)]
    peers = None if runs == 1 else [[r * batch + j for r in range(runs)] for j in range(batch)]

    def exchange(x):
        return lax.all_to_all(x, "seq", 0, 0, axis_index_groups=groups, tiled=True)

    def rows_of(w):
        return [
            lax.dynamic_slice_in_dim(w, (chan_me ^ d) * width, width, 0) for d in range(chans)
        ]

    moved = exchange(jnp.concatenate([block_input, out_grad], axis=-1)).reshape(batch * block, 2 * width)

    consts, base = s4_consts(a_decay, a_freq, b_state, c_state, step_size, block)
    z, m = s4_tables(base, consts, 0, 1)
    moved = after(moved, z)
    inputs = moved[:, :width].astype(FULL)
    grad_low = moved[:, width:]
    moments = sum_chan(jnp.stack([jnp.sum(inputs, axis=-1), jnp.sum(inputs * inputs, axis=-1)]))
    states = a_decay.shape[0]

    def const_factor(k):
        return consts[k, :, :states], consts[k + 1, :, states:]

    begin = (seq_me // batch) * batch * block
    places = begin + jnp.arange(batch * block, dtype=jnp.int32)
    mask = (places < lengths[seq_me % batch]).astype(FULL)[:, None]
    norm_one, normed_one, inverse_one = layer_forward(inputs, norm1_gain, norm1_bias, total_width, moments)
    signal = (mask * norm_one).astype(LOW)
    skip = skip_gain[None, :]
    init = jnp.zeros((width, 2 * states), FULL)
    if runs > 1:
        _, _, _, p, _, s = s4_forward(signal, skip, consts, z, m, init)
        carry = const_factor(CARRY)
        end = add(cmul(carry, split(s[:, -1])), cmul(const_factor(BBAR), split(p[:, -1])))
        ends = lax.all_gather(pair(*end), "seq", axis_index_groups=peers)
        hop = carry
        for _ in range(batch.bit_length() - 1):
            hop = cmul(hop, hop)
        for r in range(runs - 1):
            moved = add(cmul(hop, split(init)), split(ends[r]))
            init = jnp.where(r < seq_me // batch, pair(*moved), init)
    activ, slope, xs, ps, qs, ss = s4_forward(signal, skip, consts, z, m, init)

    wv, wg = rows_of(w_value), rows_of(w_gate)
    w_gated = [jnp.concatenate([a, b], axis=1) for a, b in zip(wv, wg)]
    w_ups = rows_of(w_up)
    w_downs = [
        lax.dynamic_slice_in_dim(w_down, (chan_me ^ d) * width, width, 1) for d in range(chans)
    ]
    grads = gather_pieces(grad_low)
    activs = gather_pieces(after(activ, grads[2]))
    both = sum(dot(a, w) for a, w in zip(activs, w_gated))
    value = both[:, :width] + b_value
    gate = both[:, width:] + b_gate
    opened = jax.nn.sigmoid(gate)
    resid = inputs + value * opened
    norm_two, normed_two, inverse_two = layer_forward(resid, norm2_gain, norm2_bias, total_width)
    norms = gather_pieces(norm_two.astype(LOW))
    hidden = sum(dot(a, w) for a, w in zip(norms, w_ups)) + b_up
    spread, gelu_pull = jax.vjp(jax.nn.gelu, hidden)
    spread = spread.astype(LOW)

    grad_out = grad_low.astype(FULL)
    grad_spread = sum(dot_t(a, w) for a, w in zip(grads, w_downs))
    grad_hidden = gelu_pull(grad_spread)[0].astype(LOW)
    grad_w_down = t_dot(after(spread, grad_hidden), jnp.concatenate(grads, axis=1)).astype(LOW)
    downs_dealt = deal(grad_w_down)
    marks = []
    hidden_late = after(grad_hidden, grad_w_down)
    grad_norm_two = reduce_pieces([dot_t(hidden_late, w) for w in w_ups], marks)
    grad_w_up = t_dot(jnp.concatenate(norms, axis=1), after(grad_hidden, *marks[:2])).astype(LOW)
    grad_norm_two = after(grad_norm_two, grad_w_up)
    chains = []

    def start_ups(dep):
        chains.append(Chain([downs_dealt, deal(after(grad_w_up, dep))], True))
        return []

    grad_resid, grad_norm2_gain, grad_norm2_bias = layer_backward(
        grad_norm_two, normed_two, inverse_two, norm2_gain, total_width, start_ups
    )
    wide_chain = chains[0]
    grad_resid = grad_out + grad_resid
    grad_value = (grad_resid * opened).astype(LOW)
    grad_gate = (grad_resid * value * opened * (1.0 - opened)).astype(LOW)
    grad_both = jnp.concatenate([grad_value, grad_gate], axis=1)
    marks = []
    grad_activ = reduce_pieces([dot_t(grad_both, w) for w in w_gated], marks)
    grad_w_gated = t_dot(jnp.concatenate(activs, axis=1), after(grad_both, *marks[:2])).astype(LOW)
    gated_chain = Chain([deal(after(grad_w_gated, grad_activ))], False)
    grad_activ = after(grad_activ, grad_w_gated)
    grad_mixed = (grad_activ * slope).astype(LOW)
    made = advance([wide_chain], grad_mixed)
    init = jnp.zeros((width, 2 * states), FULL)
    if runs > 1:
        _, _, u, _, h = s4_backward(grad_mixed, consts, z, m, init)
        end = add(cmul(carry, split(h[:, 0])), cmul(const_factor(READ), split(u[:, 0])))
        ends = lax.all_gather(pair(*end), "seq", axis_index_groups=peers)
        for r in reversed(range(1, runs)):
            moved = add(cmul(hop, split(init)), split(ends[r]))
            init = jnp.where(r > seq_me // batch, pair(*moved), init)
    grad_signal, gs, us, vs, hs = s4_backward(grad_mixed, consts, z, m, init, made)
    grad_signal = after(grad_signal, *advance([wide_chain, gated_chain], grad_signal))
    grad_signal = grad_signal + skip * grad_mixed.astype(FULL)
    s4_parts = (xs, gs, ps, qs, ss, us, vs, hs, z, consts, block)
    grad_input, grad_norm1_gain, grad_norm1_bias = layer_backward(
        grad_signal * mask, normed_one, inverse_one, norm1_gain, total_width, lambda dep: []
    )
    grad_input = (grad_resid + grad_input).astype(LOW)
    wide_own = gather(wide_chain.parts[0])
    sums = s4_sums(*s4_parts, [grad_input], 0, width // CHANNELS)
    narrow = jnp.concatenate(
        [
            grad_norm1_gain,
            grad_norm1_bias,
            jnp.sum(grad_mixed.astype(FULL) * signal.astype(FULL), axis=0),
            jnp.sum(grad_value.astype(FULL), axis=0),
            jnp.sum(grad_gate.astype(FULL), axis=0),
            grad_norm2_gain,
            grad_norm2_bias,
            jnp.sum(grad_out, axis=0),
            sums[3, :, 0],
            jnp.sum(grad_hidden.astype(FULL), axis=0),
        ]
    )
    packed = pack_small(sums, narrow)
    dealt = exchange_all(packed)
    made = join_sum(wide_chain.parts[1], *gated_chain.parts, [packed, *wide_own[1:]])
    last = gather_relayed(made)
    spread_late = after(spread, made)
    output = reduce_pieces([dot(spread_late, w) for w in w_downs])
    output = (resid + output + b_down).astype(LOW)
    parts, wide, narrow = sum_small(dealt, sums, narrow.shape[0], last[2:3])
    moved = beside(grad_input, output, [parts, *last[1:]])
    moved = exchange(moved.reshape(batch, block, 2 * width))
    grad_input, output = moved[:, :, :width].astype(FULL), moved[:, :, width:]
    vectors = [narrow[k * width : (k + 1) * width] for k in range(9)]
    vectors.insert(2, vectors.pop(8))

    zero = 0 * chan_me
    (down,) = finish([wide_own, last], 0, 2, total_width, 0, zero, chan_me >> 1, chan_me & 1)
    (up,) = finish([wide_own, last], 1, 2, grad_w_up.shape[1], 0, chan_me, zero, zero)
    grad_w_value, grad_w_gate = finish([last], 0, 1, 2 * width, total_width, chan_me, zero, zero, 2)
    return (
        output,
        grad_input,
        vectors[0],
        vectors[1],
        *wide,
        vectors[2],
        vectors[3],
        grad_w_value,
        vectors[4],
        grad_w_gate,
        vectors[5],
        vectors[6],
        vectors[7],
        up,
        narrow[9 * width :],
        down,
        vectors[8],
    )


def solution(mesh):
    in_specs = (
        P(None, "seq", "chan"),
        P(),
        P("chan"),
        P("chan"),
        P(None, "chan"),
        P(None, "chan"),
        P(None, None, "chan"),
        P(None, None, "chan"),
        P("chan"),
        P("chan"),
        P(None, "chan"),
        P("chan"),
        P(None, "chan"),
        P("chan"),
        P("chan"),
        P("chan"),
        P(None, "chan"),
        P("chan"),
        P("chan", None),
        P("chan"),
        P(None, "seq", "chan"),
    )
    out_specs = (
        P(None, "seq", "chan"),
        P(None, "seq", "chan"),
        P("chan"),
        P("chan"),
        P(None, "chan"),
        P(None, "chan"),
        P(None, None, "chan"),
        P(None, None, "chan"),
        P("chan"),
        P("chan"),
        P(None, "chan"),
        P("chan"),
        P(None, "chan"),
        P("chan"),
        P("chan"),
        P("chan"),
        P(None, "chan"),
        P("chan"),
        P("chan", None),
        P("chan"),
    )
    return jax.shard_map(body, mesh=mesh, in_specs=in_specs, out_specs=out_specs, check_vma=False)
```
